32 devices in a mesh: clip: 8 (over z, y), unit: 4 (over x, core).
Axes of the slice: x: 2, y: 2, z: 4, core: 2. Of those that a mesh axis runs over, the one named last changes fastest.
Arguments:
- tokens: bfloat16 [16, 392, 16, 192], P('clip', 'unit'), may hold values from -6 to 6
- first_gain: bfloat16 [192], replicated, may hold values from 0.5 to 1.5
- first_shift: bfloat16 [192], replicated, may hold values from -1 to 1
- proj_weight: bfloat16 [192, 384], replicated, may hold values from -0.875 to 0.875
- proj_bias: bfloat16 [384], replicated, may hold values from -1 to 1
- qkv_weight: bfloat16 [192, 1152], replicated, may hold values from -0.625 to 0.625
- query_bias: bfloat16 [384], replicated, may hold values from -1.5 to 1.5
- value_bias: bfloat16 [384], replicated, may hold values from -1.5 to 1.5
- output_weight: bfloat16 [384, 384], replicated, may hold values from -3.5 to 3.5
- output_bias: bfloat16 [384], replicated, may hold values from -1 to 1
- second_gain: bfloat16 [384], replicated, may hold values from 0.5 to 1.5
- second_shift: bfloat16 [384], replicated, may hold values from -1 to 1
- expand_weight: bfloat16 [384, 1536], replicated, may hold values from -0.3125 to 0.3125
- expand_bias: bfloat16 [1536], replicated, may hold values from -1.5 to 1.5
- shrink_weight: bfloat16 [1536, 384], replicated, may hold values from -0.21875 to 0.21875
- shrink_bias: bfloat16 [384], replicated, may hold values from -1 to 1
- frame_counts: int32 [16], P('clip'), may hold values from 1 to 8, as said below
- unit_frames: int32 [16, 392], P('clip', 'unit'), may hold values from 0 to 7, as said below
- cotangent: bfloat16 [16, 392, 4, 384], P('clip', 'unit'), may hold values from -6 to 6
Outputs:
- layer_out: float32 [16, 392, 4, 384], P('clip', 'unit')
- input_grad: float32 [16, 392, 16, 192], P('clip', 'unit')
- first_gain_grad: float32 [192], P('unit')
- first_shift_grad: float32 [192], P('unit')
- proj_weight_grad: float32 [192, 384], P(None, 'unit')
- proj_bias_grad: float32 [384], P('unit')
- qkv_weight_grad: float32 [192, 1152], P(None, 'unit')
- query_bias_grad: float32 [384], P('unit')
- value_bias_grad: float32 [384], P('unit')
- output_weight_grad: float32 [384, 384], P(None, 'unit')
- output_bias_grad: float32 [384], P('unit')
- second_gain_grad: float32 [384], P('unit')
- second_shift_grad: float32 [384], P('unit')
- expand_weight_grad: float32 [384, 1536], P(None, 'unit')
- expand_bias_grad: float32 [1536], P('unit')
- shrink_weight_grad: float32 [1536, 384], P('unit')
- shrink_bias_grad: float32 [384], P('unit')
The draws below stay inside these ranges and needn't reach their ends.
Inputs may be any that keep to these rules, and one draw needn't show every extreme that they name: `frame_counts`: each clip's count of valid frames; some clip has all 8. `unit_frames`: each frame of a clip has exactly 49 units, and every device along unit holds at least one unit of every frame of each of its clips.
All inputs are finite; a program needn't handle non-finite values.
Results may differ from the reference program's by a relative error of at most 0.012.
Values may be sent and summed in bfloat16 or wider, within the bound.
No kernel may reach another device: no remote copies, remote signals or barrier semaphores. Data moves between devices by JAX's collectives and lax.ppermute only.
A program may use at most 384 MiB of HBM per device.

```python
import jax
import jax.numpy as jnp
from jax import lax

D_IN = 192
D_OUT = 384
HEADS = 4
FF = 1536
HEAD_DIM = 96
FRAMES = 8
FRAME_UNITS = 49
UNITS = 392
UNIT_DEV = 98
CLIPS = 16


def draw_frame_counts(key, part):
    key = jax.random.fold_in(key, 11)
    count_key, pick_key = jax.random.split(key)
    counts = jax.random.randint(count_key, (CLIPS,), 1, FRAMES + 1)
    chosen = jax.random.randint(pick_key, (), 0, CLIPS)
    return jnp.where(jnp.arange(CLIPS) == chosen, FRAMES, counts).astype(jnp.int32)


def draw_unit_frames(key, part):
    key = jax.random.fold_in(key, 23)
    groups = UNITS // UNIT_DEV
    scores = jax.random.randint(key, (CLIPS, groups, UNIT_DEV), 0, 1 << 20)
    slot_index = jnp.arange(UNIT_DEV, dtype=jnp.int32)
    distinct = scores * UNIT_DEV + slot_index[None, None, :]
    ranking = jnp.argsort(distinct, axis=-1, stable=True).astype(jnp.int32)
    device = jnp.arange(groups, dtype=jnp.int32)[None, :, None]
    global_unit = ranking * groups + device
    return (global_unit // FRAME_UNITS).reshape(CLIPS, UNITS).astype(jnp.int32)


def with_spikes(values, stream_key, source, target, shards_of, factor):
    def block_of(axis_at):
        return (jnp.arange(values.shape[axis_at]) // (values.shape[axis_at] // shards_of)).reshape((-1,) + (1,) * (values.ndim - 1 - axis_at))

    first = jax.random.permutation(stream_key, shards_of)[block_of(target)]
    far = (block_of(target) + shards_of // 2) % shards_of
    return jnp.where((block_of(source) == first) | (block_of(source) == far), factor * values, values)


def levels(own_key, dims, cuts, low, top_value):
    def one(position, blocks):
        draws = jax.random.uniform(jax.random.fold_in(jax.random.fold_in(own_key, 6), position), (blocks,), jnp.float32, low / len(cuts), top_value / len(cuts))
        return jnp.repeat(jnp.exp(draws), dims[position] // blocks).reshape((-1,) + (1,) * (len(dims) - position - 1))

    gain = one(*cuts[0])
    for cut in cuts[1:]:
        gain = gain * one(*cut)
    return gain


def noise(rng, shape, deviation, bound, cuts=(), held_as=jnp.bfloat16):
    entries = jax.random.normal(rng, shape, jnp.float32) * deviation
    if len(cuts) > 0:
        entries = levels(rng, shape, cuts, -0.22, 0.18) * entries
    return jnp.clip(entries, min=-bound, max=bound).astype(held_as)


def noise_with(own_key, dims, scale, bound, cuts, heavy, kind=jnp.bfloat16):
    entries = scale * jax.random.normal(own_key, dims, jnp.float32)
    if cuts:
        entries = entries * levels(own_key, dims, cuts, -0.22, 0.18)
    return jnp.clip(with_spikes(entries, jax.random.fold_in(own_key, 3), *heavy), -bound, bound).astype(kind)


def setup_inputs(seed: int = 0) -> dict:
    seeds = jax.random.split(jax.random.key(seed), 20)
    return {
        "tokens": noise(seeds[0], (CLIPS, UNITS, 16, D_IN), 1.0, 6.0, ((0, 8), (1, 4))),
        "first_gain": jnp.clip(1.0 + 0.1 * jax.random.normal(seeds[1], (D_IN,), jnp.float32), 0.5, 1.5).astype(jnp.bfloat16),
        "first_shift": noise(seeds[2], (D_IN,), 0.2, 1.0),
        "proj_weight": noise(seeds[3], (D_IN, D_OUT), (D_IN // 4) ** -0.5, 0.875),
        "proj_bias": noise(seeds[4], (D_OUT,), 0.2, 1.0),
        "qkv_weight": noise(seeds[5], (D_IN, 3 * D_OUT), (D_IN // 2) ** -0.5, 0.625),
        "query_bias": noise(seeds[6], (D_OUT,), 0.3, 1.5),
        "value_bias": noise(seeds[7], (D_OUT,), 0.3, 1.5),
        "output_weight": noise(seeds[8], (D_OUT, D_OUT), 3 ** -0.5, 3.5),
        "output_bias": noise(seeds[9], (D_OUT,), 0.2, 1.0),
        "second_gain": jnp.clip(1.0 + 0.1 * jax.random.normal(seeds[10], (D_OUT,), jnp.float32), 0.5, 1.5).astype(jnp.bfloat16),
        "second_shift": noise(seeds[11], (D_OUT,), 0.2, 1.0),
        "expand_weight": noise(seeds[12], (D_OUT, FF), D_OUT ** -0.5, 0.3125),
        "expand_bias": noise(seeds[13], (FF,), 0.3, 1.5),
        "shrink_weight": noise(seeds[14], (FF, D_OUT), (FF // 2) ** -0.5, 0.21875),
        "shrink_bias": noise(seeds[15], (D_OUT,), 0.2, 1.0),
        "frame_counts": draw_frame_counts(jax.random.fold_in(seeds[19], 71), 0),
        "unit_frames": draw_unit_frames(jax.random.fold_in(seeds[19], 71), 0),
        "cotangent": noise_with(seeds[18], (CLIPS, UNITS, 4, D_OUT), 1.0, 6.0, ((0, 8), (1, 4)), (1, 3, 4, 2.0)),
    }


@jax.custom_vjp
def low(v):
    return lax.optimization_barrier(v.astype(jnp.bfloat16)).astype(jnp.float32)

@jax.custom_vjp
def low_back(v):
    return v

def low_keep(v):
    return (low(v), None)

def low_pass(kept, grad):
    return (grad,)

def back_keep(v):
    return (v, None)

def back_low(kept, grad):
    return (low(grad),)
low.defvjp(low_keep, low_pass)
low_back.defvjp(back_keep, back_low)

def layer_norm(values, gain_vector, shift_vector):
    center = values - lax.optimization_barrier(jnp.mean(values, axis=-1, keepdims=True))
    spread = lax.optimization_barrier(jnp.mean(center * center, axis=-1, keepdims=True))
    return center * lax.rsqrt(spread + 1e-06) * gain_vector + shift_vector

def pool_units(tensor):
    leading = tensor.shape[:-2]
    channels = tensor.shape[-1]
    blocks = tensor.reshape(leading + (2, 2, 2, 2, channels))
    return lax.optimization_barrier(jnp.mean(blocks, axis=(-4, -2))).reshape(leading + (4, channels))

def matmul(operand, weight_matrix):
    return jnp.dot(operand, weight_matrix, precision=lax.Precision.HIGHEST, preferred_element_type=jnp.float32)

def clip_forward(params, clip_tokens, frame_count, frames):
    first_gain, first_shift, proj_weight, proj_bias, qkv_weight, query_bias, value_bias, output_weight, output_bias, second_gain, second_shift, expand_weight, expand_bias, shrink_weight, shrink_bias = params
    unit_count = clip_tokens.shape[0]
    normed = low(layer_norm(clip_tokens, first_gain, first_shift)).reshape(unit_count * 16, D_IN)
    projection = (matmul(normed, proj_weight) + proj_bias).reshape(unit_count, 16, D_OUT)
    residual = pool_units(projection).reshape(unit_count * 4, D_OUT)
    projected = low_back(matmul(normed, qkv_weight)).reshape(unit_count, 16, 3 * D_OUT)
    queries = low(pool_units(projected[:, :, :D_OUT]).reshape(unit_count * 4, D_OUT) + query_bias)
    key_rows = low(projected[:, :, D_OUT:2 * D_OUT].reshape(unit_count * 16, D_OUT))
    value_rows = low(projected[:, :, 2 * D_OUT:].reshape(unit_count * 16, D_OUT) + value_bias)
    key_valid = jnp.repeat(frames < frame_count, 16)
    query_heads = queries.reshape(-1, HEADS, HEAD_DIM)
    key_heads = key_rows.reshape(-1, HEADS, HEAD_DIM)
    value_heads = value_rows.reshape(-1, HEADS, HEAD_DIM)
    scores = low_back(jnp.einsum('qhd,khd->hqk', query_heads, key_heads, precision=lax.Precision.HIGHEST) * HEAD_DIM ** (-0.5))
    scores = jnp.where(key_valid[None, None, :], scores, -1e+30)
    highest = lax.optimization_barrier(jnp.max(scores, axis=-1, keepdims=True))
    weights = jnp.exp(scores - highest)
    probability = weights / lax.optimization_barrier(jnp.sum(weights, axis=-1, keepdims=True))
    attended = jnp.einsum('hqk,khd->qhd', low(probability), value_heads, precision=lax.Precision.HIGHEST)
    attended = low(low_back(attended.reshape(unit_count * 4, D_OUT)))
    hidden = low_back(residual + matmul(attended, output_weight) + output_bias)
    second = low(layer_norm(hidden, second_gain, second_shift))
    before = low_back(matmul(second, expand_weight) + expand_bias)
    active = low(jax.nn.gelu(before, approximate=False))
    return hidden + matmul(active, shrink_weight) + shrink_bias

def reference(tokens, first_gain, first_shift, proj_weight, proj_bias, qkv_weight, query_bias, value_bias, output_weight, output_bias, second_gain, second_shift, expand_weight, expand_bias, shrink_weight, shrink_bias, frame_counts, unit_frames, cotangent):
    params = tuple((weight_array.astype(jnp.float32) for weight_array in (first_gain, first_shift, proj_weight, proj_bias, qkv_weight, query_bias, value_bias, output_weight, output_bias, second_gain, second_shift, expand_weight, expand_bias, shrink_weight, shrink_bias)))
    inputs = tokens.astype(jnp.float32)

    def forward(params, inputs):

        def one_clip(operands):
            clip_tokens, frame_count, frames = operands
            return clip_forward(params, clip_tokens, frame_count, frames)
        return lax.map(jax.checkpoint(one_clip), (inputs, frame_counts, unit_frames))
    layer_out, pullback = jax.vjp(forward, params, inputs)
    param_grads, input_grad = pullback(cotangent.astype(jnp.float32).reshape(layer_out.shape))
    return (layer_out.reshape(CLIPS, UNITS, 4, D_OUT), input_grad, param_grads[0], param_grads[1], param_grads[2], param_grads[3], param_grads[4], param_grads[5], param_grads[6], param_grads[7], param_grads[8], param_grads[9], param_grads[10], param_grads[11], param_grads[12], param_grads[13], param_grads[14])
```

```python
import functools

import jax
import jax.numpy as jnp
from jax import lax
from jax.experimental import pallas as pl
from jax.experimental.pallas import tpu as pltpu
from jax.sharding import PartitionSpec as P

D_IN = 192
D_OUT = 384
HEADS = 4
HEAD_DIM = 96
FF = 1536
LANES = 128
EXT = 208
SCALE = HEAD_DIM**-0.5
LOG2E = 1.4426950408889634
BF = jnp.bfloat16
F32 = jnp.float32
VMEM_BYTES = 60 * 2**20


def mm(a, b, ca, cb):
    return lax.dot_general(a, b, (((ca,), (cb,)), ((), ())), preferred_element_type=F32)


def iota(shape, dim):
    return lax.broadcasted_iota(jnp.int32, shape, dim)


def call(body, grid, ins, outs, scratch=(), name=None, cost=None, after=()):
    count = len(ins)

    def run(*refs):
        body(*refs[:count], *refs[count + len(after) :])

    ins = [*ins, *((pl.BlockSpec(memory_space=pl.ANY), value) for value in after)]
    return pl.pallas_call(
        run,
        grid=grid,
        in_specs=[spec for spec, _ in ins],
        out_specs=[spec for spec, _, _ in outs],
        out_shape=[jax.ShapeDtypeStruct(shape, dtype) for _, shape, dtype in outs],
        scratch_shapes=list(scratch),
        compiler_params=pltpu.CompilerParams(
            dimension_semantics=("arbitrary",) * len(grid), vmem_limit_bytes=VMEM_BYTES
        ),
        name=name,
        cost_estimate=pl.CostEstimate(
            flops=int(cost * 1.1e9), bytes_accessed=int(cost * 1e6), transcendentals=0
        ),
    )(*[value for _, value in ins])


def whole(value):
    rank = len(value.shape)
    return (pl.BlockSpec(value.shape, lambda *_: (0,) * rank), value)


def part(value):
    rank = len(value.shape)
    return (pl.BlockSpec((1,) + value.shape[1:], lambda i: (i,) + (0,) * (rank - 1)), value)


def at_clip(value, clip):
    rank = len(value.shape)
    return (pl.BlockSpec((1,) + value.shape[1:], lambda *_: (clip,) + (0,) * (rank - 1)), value)


def at_head(value, clip):
    rank = len(value.shape)
    return (
        pl.BlockSpec((None, 1) + value.shape[2:], lambda i: (clip, i) + (0,) * (rank - 2)),
        value,
    )


def out_part(shape, dtype):
    rank = len(shape)
    return (pl.BlockSpec((1,) + shape[1:], lambda i: (i,) + (0,) * (rank - 1)), shape, dtype)


def out_whole(shape, dtype):
    rank = len(shape)
    return (pl.BlockSpec(shape, lambda *_: (0,) * rank), shape, dtype)


V_GAIN1, V_SHIFT1, V_PROJ, V_OUT, V_GAIN2, V_SHIFT2, V_SHRINK, V_EXPAND, V_QKV = range(9)


def vec(table, row, width):
    return table[row : row + 1, :width]


def normed_body(tok_ref, inv_ref, cols_ref, nt_ref, pooled_ref):
    slots, _, units = tok_ref.shape[1:]
    gain, shift = cols_ref[:, 0:1], cols_ref[:, 1:2]
    pieces = []
    for s in range(slots):
        x = tok_ref[0, s].astype(F32)
        center = x - jnp.mean(x, axis=0, keepdims=True)
        var = jnp.mean(center * center, axis=0, keepdims=True)
        pieces.append((center * lax.rsqrt(var + 1e-06) * gain + shift).astype(BF).astype(F32))
    nt_ref[:D_IN, :] = jnp.concatenate(pieces, axis=1).astype(BF)
    extra = iota((EXT - D_IN, units), 0)
    extra = jnp.where(extra == 0, 1.0, jnp.where(extra == 1, inv_ref[0], 0.0))
    nt_ref[D_IN:, :] = jnp.concatenate([extra] * slots, axis=1).astype(BF)
    means = []
    for p in range(4):
        first = 8 * (p >> 1) + 2 * (p & 1)
        means.append(
            (pieces[first] + pieces[first + 1] + pieces[first + 4] + pieces[first + 5]) * 0.25
        )
    pooled = jnp.concatenate(means, axis=1)
    row = iota((2 * LANES - D_IN, 4 * units), 0)
    pooled = jnp.concatenate([pooled, jnp.where(row == 0, 1.0, 0.0)], axis=0)
    pooled_ref[...] = pooled.T.astype(BF)


def normed_tokens(clip, tokens, invalid, cols):
    _, slots, _, units = tokens.shape
    return call(
        normed_body,
        (1,),
        [at_clip(tokens, clip), at_clip(invalid, clip), whole(cols)],
        [out_whole((EXT, slots * units), BF), out_whole((4 * units, 2 * LANES), BF)],
        name="normed",
        cost=3,
    )


def query_body(clips, qkv_ref, wp_ref, table_ref, *refs):
    pooled_refs, wt_ref, q_refs = refs[:clips], refs[clips], refs[clips + 1 :]
    bias = jnp.where(
        iota((EXT - D_IN, 3 * D_OUT), 0) == 0, vec(table_ref, V_QKV, 3 * D_OUT), 0.0
    ).astype(BF)
    extended = jnp.concatenate([qkv_ref[...], bias], axis=0)
    eye = jnp.where(iota((LANES, HEAD_DIM), 0) == iota((LANES, HEAD_DIM), 1), 1.0, 0.0).astype(BF)
    row, lane = iota((LANES, EXT), 0), iota((LANES, EXT), 1)
    ones = (lane == D_IN) & (row >= HEAD_DIM)
    extras = (
        jnp.where(ones & (row == HEAD_DIM), 8.0, 0.0),
        jnp.where((lane == D_IN + 1) & (row == HEAD_DIM), -1e30, 0.0),
        jnp.where(ones & (row <= HEAD_DIM + 1), 1.0, 0.0),
    )
    for block in range(3 * HEADS):
        columns = extended[:, HEAD_DIM * block : HEAD_DIM * (block + 1)]
        wt_ref[block, :, :EXT] = (mm(eye, columns, 1, 1) + extras[block // HEADS]).astype(BF)
        wt_ref[block, :, EXT:] = jnp.zeros((LANES, 2 * LANES - EXT), BF)
    eye = jnp.where(iota((LANES, LANES), 0) == iota((LANES, LANES), 1), 1.0, 0.0).astype(BF)
    for block in range(D_OUT // LANES):
        columns = wp_ref[:, LANES * block : LANES * (block + 1)]
        wt_ref[3 * HEADS + block, :, :D_IN] = mm(eye, columns, 1, 1).astype(BF)
        wt_ref[3 * HEADS + block, :, D_IN:] = jnp.zeros((LANES, 2 * LANES - D_IN), BF)
    for c in range(clips):
        pooled = pooled_refs[c][...]
        for h in range(HEADS):
            q_refs[2 * c][h] = (mm(pooled, wt_ref[h], 1, 1) * (SCALE * LOG2E)).astype(BF)
            q_refs[2 * c + 1][h] = (mm(wt_ref[h, :HEAD_DIM], pooled, 1, 1) * SCALE).astype(BF)


def queries_of(qkv, wp, table, pooled):
    clips, count = len(pooled), pooled[0].shape[0]
    wt, *rest = call(
        functools.partial(query_body, clips),
        (1,),
        [whole(qkv), whole(wp), whole(table), *(whole(value) for value in pooled)],
        [
            out_whole((3 * HEADS + D_OUT // LANES, LANES, 2 * LANES), BF),
            *[
                out_whole((HEADS, count, LANES), BF),
                out_whole((HEADS, HEAD_DIM, count), BF),
            ]
            * clips,
        ],
        name="queries",
        cost=5,
    )
    return wt, [(rest[2 * c], rest[2 * c + 1]) for c in range(clips)]


def forward_body(na_ref, nb_ref, wt_ref, qs_ref, p_ref, kt_ref, vt_ref, o_ref, n_ref):
    rows = na_ref.shape[1]

    @pl.when(pl.program_id(0) == 0)
    def _():
        n_ref[:, :rows] = na_ref[...]
        n_ref[:, rows:] = nb_ref[...]

    n = n_ref[...]
    h = pl.program_id(0)
    kt = mm(wt_ref[HEADS + h][:, :EXT], n, 1, 0).astype(BF)
    vt = mm(wt_ref[2 * HEADS + h][:, :EXT], n, 1, 0).astype(BF)
    kt_ref[0] = kt
    vt_ref[0] = vt
    s = mm(qs_ref[0], kt, 1, 0)
    m = jnp.max(s, axis=1, keepdims=True)
    p = jnp.exp2(s - m).astype(BF)
    p_ref[0] = p
    o = mm(p, vt, 1, 1)
    o_ref[0] = jnp.where(iota(o.shape, 1) == HEAD_DIM + 1, m, o)


def forward(na, nb, wt, qs, after=()):
    rows = na.shape[1]
    queries = qs.shape[1]
    return call(
        forward_body,
        (HEADS,),
        [whole(na), whole(nb), whole(wt), part(qs)],
        [
            out_part((HEADS, queries, 2 * rows), BF),
            out_part((HEADS, LANES, 2 * rows), BF),
            out_part((HEADS, LANES, 2 * rows), BF),
            out_part((HEADS, queries, LANES), F32),
        ],
        [pltpu.VMEM((EXT, 2 * rows), BF)],
        name="attend",
        after=after,
        cost=16,
    )


def middle_body(clips, me_ref, *refs):
    o1_refs, o2_refs, pooled_refs = refs[:clips], refs[clips : 2 * clips], refs[2 * clips : 3 * clips]
    for c in range(clips):

        @pl.when(pl.program_id(0) == c)
        def _():
            middle_clip(
                clips, c, me_ref, o1_refs[c], o2_refs[c], pooled_refs[c], *refs[3 * clips :]
            )


def middle_clip(
    clips,
    step,
    me_ref,
    o1_ref,
    o2_ref,
    pooled_ref,
    up_ref,
    table_ref,
    wp_ref,
    wo_ref,
    we_ref,
    ws_ref,
    out_ref,
    hg_ref,
    do1_ref,
    do2_ref,
    do1t_ref,
    do2t_ref,
    keep_ref,
    send_ref,
    wpt_ref,
    we_acc,
    ws_acc,
    wo_acc,
    wp_acc,
    misc_acc,
):
    queries = pooled_ref.shape[0]
    pooled = pooled_ref[...]
    up_low = up_ref[0]
    up = up_low.astype(F32)

    if step == 0:
        we_acc[...] = jnp.zeros_like(we_acc)
        ws_acc[...] = jnp.zeros_like(ws_acc)
        wo_acc[...] = jnp.zeros_like(wo_acc)
        wp_acc[...] = jnp.zeros_like(wp_acc)
        misc_acc[...] = jnp.zeros_like(misc_acc)

    heads = []
    factors = []
    for h in range(HEADS):
        o1, o2 = o1_ref[h], o2_ref[h]
        l1, l2 = o1[:, HEAD_DIM : HEAD_DIM + 1], o2[:, HEAD_DIM : HEAD_DIM + 1]
        m1, m2 = o1[:, HEAD_DIM + 1 : HEAD_DIM + 2], o2[:, HEAD_DIM + 1 : HEAD_DIM + 2]
        m = jnp.maximum(m1, m2)
        a1, a2 = jnp.exp2(m1 - m), jnp.exp2(m2 - m)
        inverse = 1.0 / (a1 * l1 + a2 * l2)
        c1, c2 = a1 * inverse, a2 * inverse
        heads.append(o1[:, :HEAD_DIM] * c1 + o2[:, :HEAD_DIM] * c2)
        factors.append((c1, c2))
    attended = jnp.concatenate(heads, axis=1)
    attended_low = attended.astype(BF)
    hidden = mm(pooled[:, :D_IN], wp_ref[...], 1, 0) + vec(table_ref, V_PROJ, D_OUT)
    hidden = hidden + mm(attended_low, wo_ref[...], 1, 0) + vec(table_ref, V_OUT, D_OUT)
    center = hidden - jnp.mean(hidden, axis=1, keepdims=True)
    inv_std = lax.rsqrt(jnp.mean(center * center, axis=1, keepdims=True) + 1e-06)
    n = center * inv_std
    gain2 = vec(table_ref, V_GAIN2, D_OUT)
    second = (n * gain2 + vec(table_ref, V_SHIFT2, D_OUT)).astype(BF)
    before = mm(second, we_ref[...], 1, 0) + vec(table_ref, V_EXPAND, FF)
    cdf = 0.5 + 0.5 * lax.erf(before * (0.5**0.5))
    active = (before * cdf).astype(BF)
    out_ref[0] = hidden + mm(active, ws_ref[...], 1, 0) + vec(table_ref, V_SHRINK, D_OUT)
    slope = cdf + before * (jnp.exp(before * before * -0.5) * (0.5 / jnp.pi) ** 0.5)
    before_grad = (mm(up_low, ws_ref[...], 1, 1) * slope).astype(BF)
    ws_acc[...] += mm(up_low, active, 0, 0)
    we_acc[...] += mm(second, before_grad, 0, 0)
    second_grad = mm(before_grad, we_ref[...], 1, 1)
    e = gain2 * second_grad
    back = (
        e - jnp.mean(e, axis=1, keepdims=True) - n * jnp.mean(e * n, axis=1, keepdims=True)
    ) * inv_std
    hidden_grad = (up + back).astype(BF)
    hg_ref[0] = hidden_grad
    wo_acc[...] += mm(hidden_grad, attended_low, 0, 0)
    wp_acc[...] += mm(hidden_grad, pooled, 0, 0)
    misc_acc[0:1, :] += jnp.sum(before_grad.astype(F32), axis=0, keepdims=True)
    misc_acc[1:2, :D_OUT] += jnp.sum(second_grad * n, axis=0, keepdims=True)
    misc_acc[2:3, :D_OUT] += jnp.sum(second_grad, axis=0, keepdims=True)
    misc_acc[3:4, :D_OUT] += jnp.sum(up, axis=0, keepdims=True)
    misc_acc[4:5, :D_OUT] += jnp.sum(hidden_grad.astype(F32), axis=0, keepdims=True)
    attended_grad = mm(hidden_grad, wo_ref[...], 1, 1).astype(BF).astype(F32)
    lane = iota((queries, LANES), 1)
    eye = jnp.where(iota((HEAD_DIM, LANES), 0) == iota((HEAD_DIM, LANES), 1), 1.0, 0.0).astype(BF)
    fill = jnp.zeros((queries, LANES - HEAD_DIM), F32)
    for h in range(HEADS):
        own = attended_grad[:, HEAD_DIM * h : HEAD_DIM * (h + 1)]
        for factor, do_ref, dot_ref in zip(
            factors[h], (do1_ref, do2_ref), (do1t_ref, do2t_ref), strict=True
        ):
            scaled = (own * factor).astype(BF).astype(F32)
            inner = jnp.sum(scaled * heads[h], axis=1, keepdims=True)
            high = inner.astype(BF).astype(F32)
            grad = jnp.concatenate([scaled, fill], axis=1)
            grad = jnp.where(lane == HEAD_DIM, -high, grad)
            grad = jnp.where(lane == HEAD_DIM + 1, high - inner, grad).astype(BF)
            do_ref[0, h] = grad
            dot_ref[0, h] = mm(eye, grad, 1, 1).astype(BF)

    if step == clips - 1:
        me = me_ref[0]
        wpt_ref[...] = wp_acc[...]
        for u in range(4):
            for k in range(4):
                misc_acc[8 + u : 9 + u, HEAD_DIM * k : HEAD_DIM * (k + 1)] = misc_acc[
                    1 + k : 2 + k, HEAD_DIM * u : HEAD_DIM * (u + 1)
                ]
        for r in range(4):
            u = me ^ r
            ref, at = (send_ref if r & 1 else keep_ref), r >> 1
            wide = pl.ds(pl.multiple_of(u * 384, LANES), 384)
            tall = pl.ds(pl.multiple_of(u * 96, 8), 96)
            ref[at, 0:384, :] = we_acc[:, wide].astype(BF)
            ref[at, 384:768, :] = ws_acc[:, wide].astype(BF)
            ref[at, 768:864, :] = wo_acc[tall, :].astype(BF)
            wp = wp_acc[tall, :]
            ref[at, 864:912, :] = jnp.concatenate([wp[:48, :D_IN], wp[48:, :D_IN]], axis=1).astype(BF)
            bias = misc_acc[0:1, wide]
            others = misc_acc[pl.ds(8 + u, 1), :384]
            row = iota((48, 384), 0)
            ref[at, 912:960, :] = jnp.where(row == 0, bias, jnp.where(row == 1, others, 0.0)).astype(BF)


def middle(me, o1, o2, pooled, up, table, wp, wo, we, ws):
    clips = len(pooled)
    queries = pooled[0].shape[0]
    grad = (clips, HEADS, queries, LANES)
    grad_t = (clips, HEADS, HEAD_DIM, queries)
    return call(
        functools.partial(middle_body, clips),
        (clips,),
        [
            (pl.BlockSpec(memory_space=pltpu.SMEM), me),
            *(whole(value) for value in o1 + o2 + pooled),
            part(up),
            whole(table),
            whole(wp),
            whole(wo),
            whole(we),
            whole(ws),
        ],
        [
            out_part((clips, queries, D_OUT), F32),
            out_part((clips, queries, D_OUT), BF),
            out_part(grad, BF),
            out_part(grad, BF),
            out_part(grad_t, BF),
            out_part(grad_t, BF),
            out_whole((2, 960, 384), BF),
            out_whole((2, 960, 384), BF),
            out_whole((D_OUT, 2 * LANES), F32),
        ],
        [
            pltpu.VMEM((D_OUT, FF), F32),
            pltpu.VMEM((D_OUT, FF), F32),
            pltpu.VMEM((D_OUT, D_OUT), F32),
            pltpu.VMEM((D_OUT, 2 * LANES), F32),
            pltpu.VMEM((16, FF), F32),
        ],
        name="middle",
        cost=24,
    )


def backward_body(
    na_ref,
    nb_ref,
    wt_ref,
    p_ref,
    kt_ref,
    vt_ref,
    do_ref,
    dot_ref,
    qt_ref,
    dq_ref,
    dw_ref,
    ga_ref,
    gb_ref,
    n_ref,
    g_ref,
):
    rows = na_ref.shape[1]
    h = pl.program_id(0)

    @pl.when(h == 0)
    def _():
        n_ref[:, :rows] = na_ref[...]
        n_ref[:, rows:] = nb_ref[...]

    p = p_ref[0]
    kt = kt_ref[0]
    dp = mm(do_ref[0], vt_ref[0], 1, 0)
    ds = p * dp.astype(BF)
    dq_ref[0] = mm(ds, kt, 1, 1)
    both = jnp.concatenate([mm(qt_ref[0], ds, 1, 0), mm(dot_ref[0], p, 1, 0)], axis=0).astype(BF)
    dw_ref[0] = jnp.concatenate(
        [mm(both, n_ref[...], 1, 1), jnp.zeros((2 * HEAD_DIM, 2 * LANES - EXT), F32)], axis=1
    )
    w = jnp.concatenate(
        [wt_ref[HEADS + h][:HEAD_DIM, :D_IN], wt_ref[2 * HEADS + h][:HEAD_DIM, :D_IN]], axis=0
    )
    g = mm(w, both, 0, 0)

    @pl.when(h == 0)
    def _():
        g_ref[...] = g

    @pl.when((h > 0) & (h < HEADS - 1))
    def _():
        g_ref[...] += g

    @pl.when(h == HEADS - 1)
    def _():
        total = (g_ref[...] + g).astype(BF)
        ga_ref[...] = total[:, :rows]
        gb_ref[...] = total[:, rows:]


def backward(clip, na, nb, wt, p, kt, vt, do, dot, qt, after=()):
    rows = na.shape[1]
    queries = qt.shape[2]
    return call(
        backward_body,
        (HEADS,),
        [
            whole(na),
            whole(nb),
            whole(wt),
            part(p),
            part(kt),
            part(vt),
            at_head(do, clip),
            at_head(dot, clip),
            part(qt),
        ],
        [
            out_part((HEADS, queries, LANES), F32),
            out_part((HEADS, 2 * HEAD_DIM, 2 * LANES), F32),
            out_whole((D_IN, rows), BF),
            out_whole((D_IN, rows), BF),
        ],
        [pltpu.VMEM((EXT, 2 * rows), BF), pltpu.VMEM((D_IN, 2 * rows), F32)],
        name="attend_back",
        after=after,
        cost=18,
    )


def gather_body(clips, me_ref, *refs):
    dq_refs, dw_refs, pooled_refs = (
        refs[: 2 * clips],
        refs[2 * clips : 4 * clips],
        refs[4 * clips : 5 * clips],
    )
    hg_ref, wt_ref, wpt_ref, table_ref = refs[5 * clips : 5 * clips + 4]
    g_ref, keep_ref, send_ref, dw_acc, line_ref, shard_ref = refs[5 * clips + 4 :]
    gain_sum = jnp.zeros((1, D_IN), F32)
    shift_sum = jnp.zeros((1, D_IN), F32)
    low = [[None] * HEADS for _ in range(clips)]
    for h in range(HEADS):
        columns = slice(HEAD_DIM * h, HEAD_DIM * (h + 1))
        dw = jnp.zeros((LANES, 2 * LANES), F32)
        bias = jnp.zeros((1, LANES), F32)
        for c in range(clips):
            dq = (dq_refs[2 * c][h] + dq_refs[2 * c + 1][h]) * SCALE
            bias = bias + jnp.sum(dq, axis=0, keepdims=True)
            low[c][h] = dq.astype(BF)
            dw = dw + mm(low[c][h], pooled_refs[c][...], 0, 0)
        dw_acc[h] = dw[:HEAD_DIM]
        line_ref[0:1, columns] = bias[:, :HEAD_DIM]
        total = dw_refs[0][h]
        for ref in dw_refs[1:]:
            total = total + ref[h]
        dw_acc[HEADS + h] = total[:HEAD_DIM]
        dw_acc[2 * HEADS + h] = total[HEAD_DIM:]
        sums = jnp.concatenate(
            [total[HEAD_DIM:, LANES:], jnp.zeros((LANES - HEAD_DIM, LANES), F32)], axis=0
        ).T
        line_ref[1:2, columns] = sums[D_IN - LANES : D_IN - LANES + 1, :HEAD_DIM]
    wp = wt_ref[3 * HEADS :].reshape(D_OUT, 2 * LANES)[:, :D_IN]
    for c in range(clips):
        g = mm(hg_ref[c], wp, 1, 0)
        for h in range(HEADS):
            g = g + mm(low[c][h], wt_ref[h][:, :D_IN], 1, 0)
        g_ref[c] = g
    terms = [(wt_ref[b][:HEAD_DIM, :D_IN], dw_acc[b]) for b in range(3 * HEADS)]
    for w, dw in [*terms, (wp, wpt_ref[...])]:
        w = w.astype(F32)
        gain_sum = gain_sum + jnp.sum(w * dw[:, :D_IN], axis=0, keepdims=True)
        shift_sum = shift_sum + jnp.sum(w * dw[:, D_IN : D_IN + 1], axis=0, keepdims=True)
    gain_sum = (gain_sum - vec(table_ref, V_SHIFT1, D_IN) * shift_sum) / vec(
        table_ref, V_GAIN1, D_IN
    )
    line_ref[2:3, :D_IN] = gain_sum
    line_ref[3:4, :D_IN] = shift_sum
    for u in range(4):
        at = 0
        for source, size in ((0, 96), (1, 96), (2, 48), (3, 48)):
            shard_ref[u : u + 1, at : at + size] = line_ref[
                source : source + 1, size * u : size * (u + 1)
            ]
            at += size
        shard_ref[u : u + 1, at:] = jnp.zeros((1, D_OUT - at), F32)
    for r in range(4):
        u = me_ref[0] ^ r
        ref, at = (send_ref if r & 1 else keep_ref), r >> 1
        rows = jnp.concatenate([dw_acc[3 * u + i][:, :D_IN] for i in range(3)], axis=0)
        ref[at, :144, :] = jnp.concatenate([rows[:144], rows[144:]], axis=1).astype(BF)
        ref[at, 144:, :] = jnp.where(
            iota((16, D_OUT), 0) == 0, shard_ref[pl.ds(u, 1), :], 0.0
        ).astype(BF)


def gather(me, dq, dw, pooled, hg, wt, wpt, table, after=()):
    clips, queries, _ = hg.shape
    return call(
        functools.partial(gather_body, clips),
        (1,),
        [
            (pl.BlockSpec(memory_space=pltpu.SMEM), me),
            *(whole(value) for value in (*dq, *dw, *pooled, hg, wt, wpt, table)),
        ],
        [
            out_whole((clips, queries, D_IN), F32),
            out_whole((2, 160, D_OUT), BF),
            out_whole((2, 160, D_OUT), BF),
        ],
        [
            pltpu.VMEM((3 * HEADS, HEAD_DIM, 2 * LANES), F32),
            pltpu.VMEM((8, D_OUT), F32),
            pltpu.VMEM((8, D_OUT), F32),
        ],
        name="gather",
        after=after,
        cost=6,
    )


def final_body(clips, terms, tok_ref, *refs):
    part_refs = refs[: clips * terms]
    g_ref, cols_ref, out_ref, total_ref = refs[clips * terms :]
    slots, _, units = tok_ref.shape[1:]
    for c in range(clips):

        @pl.when(pl.program_id(0) == c)
        def _():
            total = part_refs[terms * c][...].astype(F32)
            for ref in part_refs[terms * c + 1 : terms * (c + 1)]:
                total = total + ref[...].astype(F32)
            total_ref[...] = total

    gain = cols_ref[:, 0:1]
    spread = g_ref[0].T * 0.25
    for s in range(slots):
        p = 2 * (s >> 3) + ((s >> 1) & 1)
        grad = total_ref[:, units * s : units * (s + 1)] + spread[:, units * p : units * (p + 1)]
        x = tok_ref[0, s].astype(F32)
        center = x - jnp.mean(x, axis=0, keepdims=True)
        inv_std = lax.rsqrt(jnp.mean(center * center, axis=0, keepdims=True) + 1e-06)
        n = center * inv_std
        e = grad * gain
        out_ref[0, s] = (
            e - jnp.mean(e, axis=0, keepdims=True) - n * jnp.mean(e * n, axis=0, keepdims=True)
        ) * inv_std


def final(tokens, parts, g, cols):
    clips, slots, _, units = tokens.shape
    terms = len(parts[0])
    return call(
        functools.partial(final_body, clips, terms),
        (clips,),
        [
            part(tokens),
            *(whole(value) for values in parts for value in values),
            part(g),
            whole(cols),
        ],
        [out_part(tokens.shape, F32)],
        [pltpu.VMEM((D_IN, slots * units), F32)],
        name="final",
        cost=7,
    )[0]


def swap_unit(value, bit):
    return lax.ppermute(value, "unit", [(i, i ^ bit) for i in range(4)])


def swap_clip(value, bit):
    size = lax.axis_size("clip")
    return lax.ppermute(value, "clip", [(i, i ^ bit) for i in range(size)])


def add(a, b):
    return (a.astype(F32) + b.astype(F32)).astype(BF)


def halve(value, bit):
    upper = (lax.axis_index("clip") & bit) != 0
    half = value.shape[0] // 2
    mine = jnp.where(upper, value[half:], value[:half])
    other = jnp.where(upper, value[:half], value[half:])
    return add(mine, swap_clip(other, bit))


def double(value, bit):
    upper = (lax.axis_index("clip") & bit) != 0
    other = swap_clip(value, bit)
    return jnp.where(upper, jnp.concatenate([other, value]), jnp.concatenate([value, other]))


def clip_bits(rows):
    size, bit, cut, rest = lax.axis_size("clip"), 1, [], []
    while bit < size:
        if not rest and rows % 16 == 0:
            cut.append(bit)
            rows //= 2
        else:
            rest.append(bit)
        bit *= 2
    return cut, rest


def reduce_clips(value):
    cut, rest = clip_bits(value.shape[0])
    for bit in cut:
        value = halve(value, bit)
    for bit in rest:
        value = add(value, swap_clip(value, bit))
    for bit in reversed(cut):
        value = double(value, bit)
    return value


def shards(
    tokens,
    first_gain,
    first_shift,
    proj_weight,
    proj_bias,
    qkv_weight,
    query_bias,
    value_bias,
    output_weight,
    output_bias,
    second_gain,
    second_shift,
    expand_weight,
    expand_bias,
    shrink_weight,
    shrink_bias,
    frame_counts,
    unit_frames,
    cotangent,
):
    clips, units = tokens.shape[:2]
    me = lax.axis_index("unit").astype(jnp.int32).reshape(1)
    lines = [
        [first_gain],
        [first_shift],
        [proj_bias],
        [output_bias],
        [second_gain],
        [second_shift],
        [shrink_bias],
        [expand_bias],
        [query_bias, jnp.zeros_like(query_bias), value_bias],
    ]
    pieces = []
    for line in lines:
        pieces += line
        pieces.append(jnp.zeros((FF - sum(v.shape[0] for v in line),), BF))
    table = jnp.concatenate(pieces).astype(F32).reshape(len(lines), FF)
    cols = jnp.stack([first_gain, first_shift], axis=1).astype(F32)
    invalid = (unit_frames >= frame_counts[:, None]).astype(F32).reshape(clips, 1, units)
    flat = tokens.transpose(0, 2, 3, 1)
    upstream = cotangent.transpose(0, 2, 1, 3).reshape(clips, 4 * units, D_OUT)
    near, across, pooled = [], [], []
    for c in range(clips):
        n, pool = normed_tokens(c, flat, invalid, cols)
        near.append((n, swap_unit(n, 1)))
        across.append(swap_unit(n, 2))
        pooled.append(pool)
    wt, query = queries_of(qkv_weight, proj_weight, table, pooled)
    own, rest, far = [], [], []
    for c in range(clips):
        own.append(forward(*near[c], wt, query[c][0], after=[v[3] for v in own[-1:]]))
    for c in range(clips):
        held, _ = lax.optimization_barrier((across[c], own[0][3]))
        far.append((held, swap_unit(held, 1)))
        rest.append(
            forward(*far[c], wt, query[c][0], after=[v[3] for v in (own + rest)[-1:]])
        )
    out, hg, do1, do2, do1t, do2t, keep, send, wpt = middle(
        me,
        [value[3] for value in own],
        [value[3] for value in rest],
        pooled,
        upstream,
        table,
        proj_weight,
        output_weight,
        expand_weight,
        shrink_weight,
    )
    dq, dw = [[None, None] for _ in range(clips)], [[None, None] for _ in range(clips)]
    parts = [[] for _ in range(clips)]
    first = add(keep, swap_unit(send, 1))
    after = []
    for c in range(clips):
        dq[c][1], dw[c][1], ga, gb = backward(
            c, *far[c], wt, *rest[c][:3], do2, do2t, query[c][1], after=after
        )
        parts[c].append(add(ga, swap_unit(gb, 1)))
        after = [dq[c][1], first]
        if c == 0:
            first = add(first[0], swap_unit(first[1], 2))
    cut, left = clip_bits(first.shape[0])
    for c in range(clips):
        after += [parts[c][0]]
        dq[c][0], dw[c][0], ga, gb = backward(
            c, *near[c], wt, *own[c][:3], do1, do1t, query[c][1], after=after
        )
        parts[c][0] = swap_unit(parts[c][0], 2)
        parts[c] += [ga, swap_unit(gb, 1)]
        if cut:
            first = halve(first, cut[0])
            cut = cut[1:]
        after = [dq[c][0], first, parts[c][0]]
    done = clip_bits(960)[0]
    for bit in cut:
        first = halve(first, bit)
    for bit in left:
        first = add(first, swap_clip(first, bit))
    for bit in reversed(done):
        first = double(first, bit)
    g, keep, send = gather(
        me, [v for pair in dq for v in pair], [v for pair in dw for v in pair], pooled, hg, wt, wpt, table,
        after=after,
    )
    second = add(keep, swap_unit(send, 1))
    second = add(second[0], swap_unit(second[1], 2))
    second = reduce_clips(second).astype(F32)
    first = first.astype(F32)
    input_grad = final(flat, parts, g, cols)

    def lanes(value, row, start, size):
        return value[row, start : start + size]

    proj = jnp.concatenate([first[864:912, :D_IN], first[864:912, D_IN:]], axis=0)
    qkv = jnp.concatenate([second[:144, :D_IN], second[:144, D_IN:]], axis=0)
    return (
        out.reshape(clips, 4, units, D_OUT).transpose(0, 2, 1, 3),
        input_grad.transpose(0, 3, 1, 2),
        lanes(second, 144, 192, 48),
        lanes(second, 144, 240, 48),
        proj.T,
        lanes(first, 913, 288, 96),
        qkv.T,
        lanes(second, 144, 0, 96),
        lanes(second, 144, 96, 96),
        first[768:864].T,
        lanes(first, 913, 288, 96),
        lanes(first, 913, 0, 96),
        lanes(first, 913, 96, 96),
        first[:384],
        lanes(first, 912, 0, 384),
        first[384:768].T,
        lanes(first, 913, 192, 96),
    )


def solution(mesh):
    every = P()
    split = P("clip", "unit", None, None)
    return jax.shard_map(
        shards,
        mesh=mesh,
        in_specs=(split,) + (every,) * 15 + (P("clip"), P("clip", "unit"), split),
        out_specs=(
            split,
            split,
            P("unit"),
            P("unit"),
            P(None, "unit"),
            P("unit"),
            P(None, "unit"),
            P("unit"),
            P("unit"),
            P(None, "unit"),
            P("unit"),
            P("unit"),
            P("unit"),
            P(None, "unit"),
            P("unit"),
            P("unit", None),
            P("unit"),
        ),
        check_vma=False,
    )
```

```python
import functools

import jax
import jax.numpy as jnp
from jax import lax
from jax.experimental import pallas as pl
from jax.experimental.pallas import tpu as pltpu
from jax.sharding import PartitionSpec as P

D_IN = 192
D_OUT = 384
HEADS = 4
HEAD_DIM = 96
FF = 1536
LANES = 128
EXT = 208
SCALE = HEAD_DIM**-0.5
LOG2E = 1.4426950408889634
BF = jnp.bfloat16
F32 = jnp.float32
VMEM_BYTES = 64 * 2**20
FF_BLOCK = 768


def mm(a, b, ca, cb):
    return lax.dot_general(a, b, (((ca,), (cb,)), ((), ())), preferred_element_type=F32)


def iota(shape, dim):
    return lax.broadcasted_iota(jnp.int32, shape, dim)


def call(body, grid, ins, outs, scratch=(), name=None, cost=None, after=(), aliases=None):
    count = len(ins)

    def run(*refs):
        body(*refs[:count], *refs[count + len(after) :])

    ins = [*ins, *((pl.BlockSpec(memory_space=pl.ANY), value) for value in after)]
    return pl.pallas_call(
        run,
        grid=grid,
        in_specs=[spec for spec, _ in ins],
        out_specs=[spec for spec, _, _ in outs],
        out_shape=[jax.ShapeDtypeStruct(shape, dtype) for _, shape, dtype in outs],
        scratch_shapes=list(scratch),
        compiler_params=pltpu.CompilerParams(
            dimension_semantics=("arbitrary",) * len(grid), vmem_limit_bytes=VMEM_BYTES
        ),
        name=name,
        cost_estimate=pl.CostEstimate(
            flops=int(cost * 1.1e9), bytes_accessed=int(cost * 1e6), transcendentals=0
        ),
        input_output_aliases=aliases or {},
    )(*[value for _, value in ins])


def whole(value):
    rank = len(value.shape)
    return (pl.BlockSpec(value.shape, lambda *_: (0,) * rank), value)


def part(value):
    rank = len(value.shape)
    return (pl.BlockSpec((1,) + value.shape[1:], lambda i: (i,) + (0,) * (rank - 1)), value)


def at_clip(value, clip):
    rank = len(value.shape)
    return (pl.BlockSpec((1,) + value.shape[1:], lambda *_: (clip,) + (0,) * (rank - 1)), value)


def at_head(value, clip):
    rank = len(value.shape)
    return (
        pl.BlockSpec((None, 1) + value.shape[2:], lambda i: (clip, i) + (0,) * (rank - 2)),
        value,
    )


def out_part(shape, dtype):
    rank = len(shape)
    return (pl.BlockSpec((1,) + shape[1:], lambda i: (i,) + (0,) * (rank - 1)), shape, dtype)


def out_whole(shape, dtype):
    rank = len(shape)
    return (pl.BlockSpec(shape, lambda *_: (0,) * rank), shape, dtype)


def line(ref):
    return ref[...].astype(F32).reshape(1, -1)


def eye(size):
    return jnp.where(iota((size, size), 0) == iota((size, size), 1), 1.0, 0.0).astype(BF)


def column(ref):
    size = ref.shape[0]
    values = jnp.broadcast_to(line(ref), (16, size)).astype(BF)
    return mm(eye(size), values, 1, 1)[:, 0:1]


def normed_body(clip, tok_ref, frames_ref, counts_ref, gain_ref, shift_ref, nt_ref, pooled_ref):
    slots, _, units = tok_ref.shape[1:]
    gain, shift = column(gain_ref), column(shift_ref)
    x = jnp.concatenate([tok_ref[0, s].astype(F32) for s in range(slots)], axis=1)
    center = x - jnp.mean(x, axis=0, keepdims=True)
    var = jnp.mean(center * center, axis=0, keepdims=True)
    normed = (center * lax.rsqrt(var + 1e-06) * gain + shift).astype(BF)
    nt_ref[:D_IN, :] = normed
    normed = normed.astype(F32)
    pieces = [normed[:, units * s : units * (s + 1)] for s in range(slots)]
    extra = iota((EXT - D_IN, units), 0)
    invalid = jnp.where(frames_ref[clip : clip + 1, :] >= counts_ref[clip], 1.0, 0.0)
    extra = jnp.where(extra == 0, 1.0, jnp.where(extra == 1, invalid, 0.0))
    nt_ref[D_IN:, :] = jnp.concatenate([extra] * slots, axis=1).astype(BF)
    means = []
    for p in range(4):
        first = 8 * (p >> 1) + 2 * (p & 1)
        means.append(
            (pieces[first] + pieces[first + 1] + pieces[first + 4] + pieces[first + 5]) * 0.25
        )
    pooled = jnp.concatenate(means, axis=1)
    row = iota((2 * LANES - D_IN, 4 * units), 0)
    pooled = jnp.concatenate([pooled, jnp.where(row == 0, 1.0, 0.0)], axis=0)
    pooled_ref[...] = pooled.T.astype(BF)


def normed_tokens(clip, tokens, frames, counts, gain, shift):
    _, slots, _, units = tokens.shape
    return call(
        functools.partial(normed_body, clip),
        (1,),
        [
            at_clip(tokens, clip),
            whole(frames),
            (pl.BlockSpec(memory_space=pltpu.SMEM), counts),
            whole(gain),
            whole(shift),
        ],
        [out_whole((EXT, slots * units), BF), out_whole((4 * units, 2 * LANES), BF)],
        name="normed",
        cost=3,
    )


def query_body(clips, qkv_ref, wp_ref, qbias_ref, vbias_ref, *refs):
    pooled_refs, wt_ref, wg_ref, q_refs = refs[:clips], refs[clips], refs[clips + 1], refs[clips + 2 :]
    bias = jnp.concatenate(
        [line(qbias_ref), jnp.zeros((1, D_OUT), F32), line(vbias_ref)], axis=1
    )
    bias = jnp.where(iota((EXT - D_IN, 3 * D_OUT), 0) == 0, bias, 0.0).astype(BF)
    extended = jnp.concatenate([qkv_ref[...], bias], axis=0)
    tall = jnp.where(iota((LANES, HEAD_DIM), 0) == iota((LANES, HEAD_DIM), 1), 1.0, 0.0).astype(BF)
    row, lane = iota((LANES, EXT), 0), iota((LANES, EXT), 1)
    ones = (lane == D_IN) & (row >= HEAD_DIM)
    extras = (
        jnp.where(ones & (row == HEAD_DIM), 8.0, 0.0),
        jnp.where(
            (lane == D_IN + 1) & (row == HEAD_DIM),
            -1e30,
            jnp.where(ones & (row == HEAD_DIM + 1), 1.0, 0.0),
        ),
        jnp.where(ones & (row <= HEAD_DIM + 1), 1.0, 0.0),
    )
    for block in range(3 * HEADS):
        columns = extended[:, HEAD_DIM * block : HEAD_DIM * (block + 1)]
        wt_ref[block, :, :EXT] = (mm(tall, columns, 1, 1) + extras[block // HEADS]).astype(BF)
        wt_ref[block, :, EXT:] = jnp.zeros((LANES, 2 * LANES - EXT), BF)
    wg_ref[...] = jnp.concatenate(
        [
            qkv_ref[:, start : start + HEAD_DIM]
            for h in range(HEADS)
            for start in (D_OUT + HEAD_DIM * h, 2 * D_OUT + HEAD_DIM * h)
        ],
        axis=1,
    )
    for block in range(D_OUT // LANES):
        columns = wp_ref[:, LANES * block : LANES * (block + 1)]
        wt_ref[3 * HEADS + block, :, :D_IN] = mm(eye(LANES), columns, 1, 1).astype(BF)
        wt_ref[3 * HEADS + block, :, D_IN:] = jnp.zeros((LANES, 2 * LANES - D_IN), BF)
    for c in range(clips):
        pooled = pooled_refs[c][...]
        for h in range(HEADS):
            q_refs[2 * c][h] = (mm(pooled, wt_ref[h], 1, 1) * (SCALE * LOG2E)).astype(BF)
            q_refs[2 * c + 1][h] = (mm(wt_ref[h, :HEAD_DIM], pooled, 1, 1) * SCALE).astype(BF)


def queries_of(qkv, wp, qbias, vbias, pooled):
    clips, count = len(pooled), pooled[0].shape[0]
    wt, wg, *rest = call(
        functools.partial(query_body, clips),
        (1,),
        [whole(v) for v in (qkv, wp, qbias, vbias, *pooled)],
        [
            out_whole((3 * HEADS + D_OUT // LANES, LANES, 2 * LANES), BF),
            out_whole((D_IN, 2 * D_OUT), BF),
            *[
                out_whole((HEADS, count, LANES), BF),
                out_whole((HEADS, HEAD_DIM, count), BF),
            ]
            * clips,
        ],
        name="queries",
        cost=5,
    )
    return wt, wg, [(rest[2 * c], rest[2 * c + 1]) for c in range(clips)]


def forward_body(na_ref, nb_ref, wt_ref, qs_ref, p_ref, kt_ref, vt_ref, o_ref, n_ref):
    rows = na_ref.shape[1]
    queries = qs_ref.shape[1]

    @pl.when(pl.program_id(0) == 0)
    def _():
        n_ref[:, :rows] = na_ref[...]
        n_ref[:, rows:] = nb_ref[...]

    h = pl.program_id(0)
    lane = iota((queries, LANES), 1)
    bound_lane = lane == HEAD_DIM + 1
    pick = (iota((16, LANES), 0) == 0) & (iota((16, LANES), 1) == HEAD_DIM + 1)
    pick = jnp.where(pick, 1.0, 0.0).astype(BF)
    tall = HEAD_DIM + 16
    kt = mm(wt_ref[HEADS + h][:, :EXT], n_ref[...], 1, 0)
    vt = mm(wt_ref[2 * HEADS + h][:, :EXT], n_ref[...], 1, 0).astype(BF)
    plain = kt[:HEAD_DIM]
    longest = jnp.max(jnp.sum(plain * plain, axis=0, keepdims=True), axis=1, keepdims=True)
    kt = kt.astype(BF)
    kt_ref[0] = kt
    vt_ref[0] = vt
    q = qs_ref[0].astype(F32)
    norm = jnp.sum(jnp.where(lane < HEAD_DIM, q * q, 0.0), axis=1, keepdims=True)
    q = jnp.where(bound_lane, -jnp.sqrt(norm * longest), q).astype(BF)
    p = jnp.exp2(mm(q, kt, 1, 0)).astype(BF)
    p_ref[0] = p
    o = mm(vt[:tall], p, 1, 1)
    o_ref[0, :tall] = o
    o_ref[0, tall:] = mm(pick, q, 1, 1)

    @pl.when(jnp.min(o[HEAD_DIM : HEAD_DIM + 1]) < 1e-27)
    def _():
        s = mm(qs_ref[0], kt_ref[0], 1, 0)
        m = jnp.max(s, axis=1, keepdims=True).astype(BF).astype(F32)
        again = jnp.exp2(s - m).astype(BF)
        p_ref[0] = again
        o_ref[0, :tall] = mm(vt_ref[0, :tall], again, 1, 1)
        o_ref[0, tall:] = mm(
            pick, jnp.where(bound_lane, -m, qs_ref[0].astype(F32)).astype(BF), 1, 1
        )


def forward(na, nb, wt, qs, after=()):
    rows = na.shape[1]
    queries = qs.shape[1]
    return call(
        forward_body,
        (HEADS,),
        [whole(na), whole(nb), whole(wt), part(qs)],
        [
            out_part((HEADS, queries, 2 * rows), BF),
            out_part((HEADS, LANES, 2 * rows), BF),
            out_part((HEADS, LANES, 2 * rows), BF),
            out_part((HEADS, LANES, queries), F32),
        ],
        [pltpu.VMEM((EXT, 2 * rows), BF)],
        name="attend",
        after=after,
        cost=12,
    )


def middle_body(clips, me_ref, *refs):
    o1_refs, o2_refs, pooled_refs = refs[:clips], refs[clips : 2 * clips], refs[2 * clips : 3 * clips]
    up_ref, bproj_ref, bout_ref, gain_ref, shift_ref, bshrink_ref, bexpand_ref = refs[
        3 * clips : 3 * clips + 7
    ]
    wp_ref, wo_ref, we_ref, ws_ref = refs[3 * clips + 7 : 3 * clips + 11]
    out_ref, hg_ref, attended_ref, factor_ref = refs[3 * clips + 11 : 3 * clips + 15]
    shard_refs, wpt_ref = refs[3 * clips + 15 : 3 * clips + 19], refs[3 * clips + 19]
    we_acc, ws_acc, wo_acc, wp_acc, misc_acc = refs[3 * clips + 20 :]
    queries = pooled_refs[0].shape[0]
    rows = [slice(queries * c, queries * (c + 1)) for c in range(clips)]
    heads = [[] for _ in range(clips)]
    for c in range(clips):
        for h in range(HEADS):
            o1, o2 = o1_refs[c][h], o2_refs[c][h]
            l1, l2 = o1[HEAD_DIM : HEAD_DIM + 1], o2[HEAD_DIM : HEAD_DIM + 1]
            m1, m2 = -o1[HEAD_DIM + 16 : HEAD_DIM + 17], -o2[HEAD_DIM + 16 : HEAD_DIM + 17]
            m = jnp.maximum(m1, m2)
            a1, a2 = jnp.exp2(m1 - m), jnp.exp2(m2 - m)
            inverse = 1.0 / (a1 * l1 + a2 * l2)
            c1, c2 = a1 * inverse, a2 * inverse
            heads[c].append(o1[:HEAD_DIM] * c1 + o2[:HEAD_DIM] * c2)
            attended_ref[c, h] = heads[c][h]
            factor_ref[c, h] = jnp.concatenate([c1, c2, jnp.zeros((6, queries), F32)], axis=0)
    attended = jnp.concatenate([jnp.concatenate(parts, axis=0).T for parts in heads], axis=0)
    attended = attended.astype(BF)
    pooled = jnp.concatenate([ref[...].astype(F32) for ref in pooled_refs], axis=0).astype(BF)
    up = jnp.concatenate([up_ref[c].astype(F32) for c in range(clips)], axis=0)
    up_low = up.astype(BF)
    hidden = mm(pooled[:, :D_IN], wp_ref[...], 1, 0) + line(bproj_ref)
    hidden = hidden + mm(attended, wo_ref[...], 1, 0) + line(bout_ref)
    center = hidden - jnp.mean(hidden, axis=1, keepdims=True)
    inv_std = lax.rsqrt(jnp.mean(center * center, axis=1, keepdims=True) + 1e-06)
    n = center * inv_std
    gain2 = line(gain_ref)
    second = (n * gain2 + line(shift_ref)).astype(BF)
    out = hidden + line(bshrink_ref)
    second_grad = jnp.zeros(out.shape, F32)
    bexpand = line(bexpand_ref)
    for start in range(0, FF, FF_BLOCK):
        block = slice(start, start + FF_BLOCK)
        before = mm(second, we_ref[:, block], 1, 0) + bexpand[:, block]
        cdf = 0.5 + 0.5 * lax.erf(before * (0.5**0.5))
        active = (before * cdf).astype(BF)
        out = out + mm(active, ws_ref[block, :], 1, 0)
        slope = cdf + before * (jnp.exp(before * before * -0.5) * (0.5 / jnp.pi) ** 0.5)
        before_grad = (mm(up_low, ws_ref[block, :], 1, 1) * slope).astype(BF)
        ws_acc[:, block] = mm(up_low, active, 0, 0)
        we_acc[:, block] = mm(second, before_grad, 0, 0)
        second_grad = second_grad + mm(before_grad, we_ref[:, block], 1, 1)
        misc_acc[0:1, block] = jnp.sum(before_grad.astype(F32), axis=0, keepdims=True)
    for c in range(clips):
        out_ref[c] = out[rows[c]]
    e = gain2 * second_grad
    back = (
        e - jnp.mean(e, axis=1, keepdims=True) - n * jnp.mean(e * n, axis=1, keepdims=True)
    ) * inv_std
    hidden_full = (up + back).astype(BF).astype(F32)
    hidden_grad = hidden_full.astype(BF)
    wo_acc[...] = mm(hidden_grad, attended, 0, 0)
    wp_acc[...] = mm(hidden_grad, pooled, 0, 0)
    misc_acc[1:2, :D_OUT] = jnp.sum(second_grad * n, axis=0, keepdims=True)
    misc_acc[2:3, :D_OUT] = jnp.sum(second_grad, axis=0, keepdims=True)
    misc_acc[3:4, :D_OUT] = jnp.sum(up, axis=0, keepdims=True)
    misc_acc[4:5, :D_OUT] = jnp.sum(hidden_full, axis=0, keepdims=True)
    for c in range(clips):
        hg_ref[c] = hidden_full[rows[c]].astype(BF)
    me = me_ref[0]
    wpt_ref[...] = wp_acc[...]
    for u in range(4):
        for k in range(4):
            misc_acc[8 + u : 9 + u, HEAD_DIM * k : HEAD_DIM * (k + 1)] = misc_acc[
                1 + k : 2 + k, HEAD_DIM * u : HEAD_DIM * (u + 1)
            ]
    for r in range(4):
        u = me ^ r
        ref = shard_refs[r]
        wide = pl.ds(pl.multiple_of(u * 384, LANES), 384)
        tall = pl.ds(pl.multiple_of(u * 96, 8), 96)
        ref[0:384, :] = we_acc[:, wide].astype(BF)
        ref[384:768, :] = ws_acc[:, wide].astype(BF)
        ref[768:864, :] = wo_acc[tall, :].astype(BF)
        wp = wp_acc[tall, :]
        ref[864:912, :] = jnp.concatenate([wp[:48, :D_IN], wp[48:, :D_IN]], axis=1).astype(BF)
        bias = misc_acc[0:1, wide]
        others = misc_acc[pl.ds(8 + u, 1), :384]
        row = iota((48, 384), 0)
        ref[912:960, :] = jnp.where(row == 0, bias, jnp.where(row == 1, others, 0.0)).astype(BF)


def middle(me, o1, o2, pooled, up, vectors, weights):
    clips = len(pooled)
    queries = pooled[0].shape[0]
    return call(
        functools.partial(middle_body, clips),
        (1,),
        [
            (pl.BlockSpec(memory_space=pltpu.SMEM), me),
            *(whole(value) for value in (*o1, *o2, *pooled, up, *vectors, *weights)),
        ],
        [
            out_whole((clips, queries, D_OUT), F32),
            out_whole((clips, queries, D_OUT), BF),
            out_whole((clips, HEADS, HEAD_DIM, queries), F32),
            out_whole((clips, HEADS, 8, queries), F32),
            *([out_whole((960, 384), BF)] * 4),
            out_whole((D_OUT, 2 * LANES), F32),
        ],
        [
            pltpu.VMEM((D_OUT, FF), F32),
            pltpu.VMEM((D_OUT, FF), F32),
            pltpu.VMEM((D_OUT, D_OUT), F32),
            pltpu.VMEM((D_OUT, 2 * LANES), F32),
            pltpu.VMEM((16, FF), F32),
        ],
        name="middle",
        cost=16,
    )


def attended_grad_body(hg_ref, attended_ref, factor_ref, wo_ref, do1_ref, do2_ref, do1t_ref, do2t_ref):
    queries = hg_ref.shape[1]
    row = iota((LANES - HEAD_DIM, queries), 0)
    grad = mm(wo_ref[...], hg_ref[0], 1, 1).astype(BF).astype(F32)
    for h in range(HEADS):
        own = grad[HEAD_DIM * h : HEAD_DIM * (h + 1)]
        for k, do_ref, dot_ref in ((0, do1_ref, do1t_ref), (1, do2_ref, do2t_ref)):
            scaled = (own * factor_ref[0, h, k : k + 1]).astype(BF)
            dot_ref[0, h] = scaled
            scaled = scaled.astype(F32)
            inner = jnp.sum(scaled * attended_ref[0, h], axis=0, keepdims=True)
            high = inner.astype(BF).astype(F32)
            extra = jnp.where(row == 0, -high, jnp.where(row == 1, high - inner, 0.0))
            do_ref[0, h] = jnp.concatenate([scaled, extra], axis=0).T.astype(BF)


def attended_grads(hg, attended, factors, wo):
    clips, queries, _ = hg.shape
    grad = (clips, HEADS, queries, LANES)
    grad_t = (clips, HEADS, HEAD_DIM, queries)
    return call(
        attended_grad_body,
        (clips,),
        [part(hg), part(attended), part(factors), whole(wo)],
        [out_part(grad, BF), out_part(grad, BF), out_part(grad_t, BF), out_part(grad_t, BF)],
        name="attended_grads",
        cost=5,
    )


def backward_body(
    na_ref,
    nb_ref,
    wg_ref,
    p_ref,
    kt_ref,
    vt_ref,
    do_ref,
    dot_ref,
    qt_ref,
    dq_ref,
    dw_ref,
    ga_ref,
    gb_ref,
    n_ref,
    both_ref,
):
    rows = na_ref.shape[1]
    h = pl.program_id(0)
    p = p_ref[0]
    ds = p * mm(do_ref[0], vt_ref[0], 1, 0).astype(BF)
    dq_ref[0] = mm(kt_ref[0, :HEAD_DIM], ds, 1, 1)
    both_ref[h, :HEAD_DIM] = mm(qt_ref[0], ds, 1, 0).astype(BF)
    both_ref[h, HEAD_DIM:] = mm(dot_ref[0], p, 1, 0).astype(BF)

    @pl.when(h == HEADS - 1)
    def _():
        n_ref[:, :rows] = na_ref[...]
        n_ref[:, rows:] = nb_ref[...]
        both = both_ref[...].reshape(2 * D_OUT, 2 * rows)
        dw_ref[...] = mm(both, n_ref[...], 1, 1)
        g = mm(wg_ref[...], both, 1, 0).astype(BF)
        ga_ref[...] = g[:, :rows]
        gb_ref[...] = g[:, rows:]


def backward(clip, na, nb, wg, p, kt, vt, do, dot, qt, after=()):
    rows = na.shape[1]
    queries = qt.shape[2]
    return call(
        backward_body,
        (HEADS,),
        [
            whole(na),
            whole(nb),
            whole(wg),
            part(p),
            part(kt),
            part(vt),
            at_head(do, clip),
            at_head(dot, clip),
            part(qt),
        ],
        [
            out_part((HEADS, HEAD_DIM, queries), F32),
            out_whole((2 * D_OUT, EXT), F32),
            out_whole((D_IN, rows), BF),
            out_whole((D_IN, rows), BF),
        ],
        [pltpu.VMEM((EXT, 2 * rows), BF), pltpu.VMEM((HEADS, 2 * HEAD_DIM, 2 * rows), BF)],
        name="attend_back",
        after=after,
        cost=17,
    )


def gather_body(clips, me_ref, *refs):
    dq_refs, dw_refs, pooled_refs = (
        refs[: 2 * clips],
        refs[2 * clips : 4 * clips],
        refs[4 * clips : 5 * clips],
    )
    wt_ref, wpt_ref, gain_ref, shift_ref = refs[5 * clips : 5 * clips + 4]
    shard_refs, (dw_acc, line_ref, shard_ref) = refs[5 * clips + 4 : 5 * clips + 8], refs[5 * clips + 8 :]
    total = dw_refs[0][...]
    for ref in dw_refs[1:]:
        total = total + ref[...]
    for h in range(HEADS):
        at = 2 * HEAD_DIM * h
        dw_acc[HEADS + h] = total[at : at + HEAD_DIM]
        dw_acc[2 * HEADS + h] = total[at + HEAD_DIM : at + 2 * HEAD_DIM]
    dw = None
    for c in range(clips):
        dq = (dq_refs[2 * c][...] + dq_refs[2 * c + 1][...]) * SCALE
        dq = dq.reshape(D_OUT, dq.shape[2]).astype(BF)
        term = mm(dq, pooled_refs[c][...], 1, 0)
        dw = term if dw is None else dw + term
    for h in range(HEADS):
        dw_acc[h] = dw[HEAD_DIM * h : HEAD_DIM * (h + 1), :EXT]
    gain_sum = jnp.zeros((1, D_IN), F32)
    shift_sum = jnp.zeros((1, D_IN), F32)
    wp = wt_ref[3 * HEADS :].reshape(D_OUT, 2 * LANES)[:, :D_IN]
    terms = [(wt_ref[b][:HEAD_DIM, :D_IN], dw_acc[b]) for b in range(3 * HEADS)]
    for w, dw in [*terms, (wp, wpt_ref[...])]:
        w = w.astype(F32)
        gain_sum = gain_sum + jnp.sum(w * dw[:, :D_IN], axis=0, keepdims=True)
        shift_sum = shift_sum + jnp.sum(w * dw[:, D_IN : D_IN + 1], axis=0, keepdims=True)
    gain_sum = (gain_sum - line(shift_ref) * shift_sum) / line(gain_ref)
    for at, first in ((0, 0), (1, 2 * HEADS)):
        for h in range(HEADS):
            sums = dw_acc[first + h][:, LANES:]
            sums = jnp.concatenate(
                [sums, jnp.zeros((HEAD_DIM, 2 * LANES - EXT), F32)], axis=1
            )
            sums = jnp.concatenate([sums, jnp.zeros((LANES - HEAD_DIM, LANES), F32)], axis=0).T
            line_ref[at : at + 1, HEAD_DIM * h : HEAD_DIM * (h + 1)] = sums[
                D_IN - LANES : D_IN - LANES + 1, :HEAD_DIM
            ]
    line_ref[2:3, :D_IN] = gain_sum
    line_ref[3:4, :D_IN] = shift_sum
    for u in range(4):
        at = 0
        for source, size in ((0, 96), (1, 96), (2, 48), (3, 48)):
            shard_ref[u : u + 1, at : at + size] = line_ref[
                source : source + 1, size * u : size * (u + 1)
            ]
            at += size
        shard_ref[u : u + 1, at:] = jnp.zeros((1, D_OUT - at), F32)
    for r in range(4):
        u = me_ref[0] ^ r
        ref = shard_refs[r]
        rows = jnp.concatenate([dw_acc[3 * u + i][:, :D_IN] for i in range(3)], axis=0)
        ref[:144, :] = jnp.concatenate([rows[:144], rows[144:]], axis=1).astype(BF)
        ref[144:, :] = jnp.where(
            iota((16, D_OUT), 0) == 0, shard_ref[pl.ds(u, 1), :], 0.0
        ).astype(BF)


def gather(me, dq, dw, pooled, wt, wpt, gain, shift, after=()):
    clips = len(pooled)
    return call(
        functools.partial(gather_body, clips),
        (1,),
        [
            (pl.BlockSpec(memory_space=pltpu.SMEM), me),
            *(whole(v) for v in (*dq, *dw, *pooled, wt, wpt, gain, shift)),
        ],
        [out_whole((160, D_OUT), BF)] * 4,
        [
            pltpu.VMEM((3 * HEADS, HEAD_DIM, EXT), F32),
            pltpu.VMEM((8, D_OUT), F32),
            pltpu.VMEM((8, D_OUT), F32),
        ],
        name="gather",
        after=after,
        cost=6,
    )


def final_body(terms, tok_ref, hg_ref, wp_ref, qkv_ref, gain_ref, dq1_ref, dq2_ref, *refs):
    part_refs, out_ref = refs[:terms], refs[-1]
    slots, _, units = tok_ref.shape[1:]
    gain = column(gain_ref)
    dq = ((dq1_ref[...] + dq2_ref[...]) * SCALE).reshape(D_OUT, 4 * units).astype(BF)
    spread = mm(wp_ref[...], hg_ref[0], 1, 1) + mm(qkv_ref[:, :D_OUT], dq, 1, 0)
    spread = spread * 0.25
    places = [slice(units * s, units * (s + 1)) for s in range(slots)]
    spread = [spread[:, places[2 * (s >> 3) + ((s >> 1) & 1)]] for s in range(slots)]
    grad = total_of(part_refs) + jnp.concatenate(spread, axis=1)
    x = jnp.concatenate([tok_ref[0, s].astype(F32) for s in range(slots)], axis=1)
    center = x - jnp.mean(x, axis=0, keepdims=True)
    inv_std = lax.rsqrt(jnp.mean(center * center, axis=0, keepdims=True) + 1e-06)
    n = center * inv_std
    e = grad * gain
    back = e - jnp.mean(e, axis=0, keepdims=True) - n * jnp.mean(e * n, axis=0, keepdims=True)
    back = back * inv_std
    for s in range(slots):
        out_ref[0, s] = back[:, places[s]]


def final(clip, tokens, hg, dq, wp, qkv, gain, parts, filled, after=()):
    terms = len(parts)
    return call(
        functools.partial(final_body, terms),
        (1,),
        [
            at_clip(tokens, clip),
            at_clip(hg, clip),
            *(whole(v) for v in (wp, qkv, gain, *dq, *parts)),
            *([] if filled is None else [(pl.BlockSpec(memory_space=pl.ANY), filled)]),
        ],
        [(at_clip(tokens, clip)[0], tokens.shape, F32)],
        name="final",
        cost=6,
        after=after,
        aliases=None if filled is None else {7 + terms: 0},
    )[0]


def unpack_first_body(
    place_ref,
    value_ref,
    other_ref,
    proj_ref,
    bproj_ref,
    wo_ref,
    bout_ref,
    gain_ref,
    shift_ref,
    we_ref,
    be_ref,
    ws_ref,
    bs_ref,
    rows_ref,
):
    half = value_ref.shape[0]
    at = pl.multiple_of(place_ref[0] * half, 8)
    rows_ref[pl.ds(at, half), :] = value_ref[...].astype(F32)
    rows_ref[pl.ds(pl.multiple_of(half - at, 8), half), :] = other_ref[...].astype(F32)
    we_ref[...] = rows_ref[:384]
    ws_ref[...] = rows_ref[384:768].T
    wo_ref[...] = rows_ref[768:864].T
    proj = jnp.concatenate([rows_ref[864:912, :D_IN], rows_ref[864:912, D_IN:]], axis=0)
    proj_ref[...] = proj.T
    lines = rows_ref[912:920]
    be_ref[...] = lines[0:1].reshape(384)
    for ref, k in ((gain_ref, 0), (shift_ref, 1), (bs_ref, 2), (bout_ref, 3), (bproj_ref, 3)):
        ref[...] = lines[1:2, 96 * k : 96 * (k + 1)].reshape(96)


def unpack_first(place, value, other, after=()):
    shapes = [(192, 96), (96,), (384, 96), (96,), (96,), (96,), (384, 384), (384,), (384, 384), (96,)]
    return call(
        unpack_first_body,
        (1,),
        [(pl.BlockSpec(memory_space=pltpu.SMEM), place), whole(value), whole(other)],
        [out_whole(shape, F32) for shape in shapes],
        [pltpu.VMEM((2 * value.shape[0], D_OUT), F32)],
        name="unpack_first",
        after=after,
        cost=2,
    )


def unpack_second_body(a_ref, b_ref, qkv_ref, bq_ref, bv_ref, gain_ref, shift_ref):
    total = a_ref[...].astype(F32) + b_ref[...].astype(F32)
    qkv_ref[...] = jnp.concatenate([total[:144, :D_IN], total[:144, D_IN:]], axis=0).T
    at = 0
    for ref in (bq_ref, bv_ref, gain_ref, shift_ref):
        size = ref.shape[0]
        ref[...] = total[144:145, at : at + size].reshape(size)
        at += size


def unpack_second(a, b):
    shapes = [(192, 288), (96,), (96,), (48,), (48,)]
    return call(
        unpack_second_body,
        (1,),
        [whole(a), whole(b)],
        [out_whole(shape, F32) for shape in shapes],
        name="unpack_second",
        cost=1,
    )


def swap_unit(value, bit):
    return lax.ppermute(value, "unit", [(i, i ^ bit) for i in range(4)])


def swap_clip(value, bit):
    size = lax.axis_size("clip")
    return lax.ppermute(value, "clip", [(i, i ^ bit) for i in range(size)])


def add(*values):
    return functools.reduce(lambda a, b: a + b, [v.astype(F32) for v in values]).astype(BF)


def member():
    at = lax.axis_index("clip").astype(jnp.int32)
    return jnp.stack([at & 1, (at >> 1) & 3])


def total_of(refs):
    return functools.reduce(lambda a, b: a + b, [ref[...].astype(F32) for ref in refs])


def between(kind, sums, place, grads=None):
    rows, width = sums[0].shape
    count, more = len(sums), grads or []
    pieces = {"plain": 1, "halves": 2, "quarters": 4, "join": 1}[kind]
    tall = rows * 4 if kind == "join" else rows // pieces

    def body(place_ref, *refs):
        terms, refs = refs[:count], refs[count:]
        others, refs = refs[: len(more)], refs[len(more) :]
        outs, scratch = refs[:-1], refs[-1]
        if more:
            outs[-1][...] = total_of(others).astype(BF)
        if kind == "plain":
            outs[0][...] = total_of(terms).astype(BF)
        elif kind == "join":
            for d in range(4):
                at = pl.multiple_of((place_ref[1] ^ d) * rows, 8)
                scratch[pl.ds(at, rows), :] = terms[d][...].astype(F32)
            outs[0][...] = scratch[...].astype(BF)
        else:
            scratch[...] = total_of(terms)
            own = place_ref[0] if kind == "halves" else place_ref[1]
            for d in range(pieces):
                at = pl.multiple_of((own ^ d) * tall, 8)
                outs[d][...] = scratch[pl.ds(at, tall), :].astype(BF)

    return call(
        body,
        (1,),
        [(pl.BlockSpec(memory_space=pltpu.SMEM), place), *(whole(v) for v in (*sums, *more))],
        [
            *([out_whole((tall, width), BF)] * pieces),
            *([out_whole(more[0].shape, BF)] if more else []),
        ],
        [pltpu.VMEM((max(rows, tall), width), F32)],
        name="between",
        cost=2,
    )


def together(*values):
    return lax.optimization_barrier(values)


def shards(
    tokens,
    first_gain,
    first_shift,
    proj_weight,
    proj_bias,
    qkv_weight,
    query_bias,
    value_bias,
    output_weight,
    output_bias,
    second_gain,
    second_shift,
    expand_weight,
    expand_bias,
    shrink_weight,
    shrink_bias,
    frame_counts,
    unit_frames,
    cotangent,
):
    clips, units = tokens.shape[:2]
    me = lax.axis_index("unit").astype(jnp.int32).reshape(1)
    vectors = [proj_bias, output_bias, second_gain, second_shift, shrink_bias, expand_bias]
    flat = tokens.transpose(0, 2, 3, 1)
    upstream = cotangent.transpose(0, 2, 1, 3).reshape(clips, 4 * units, D_OUT)
    near, across, pooled = [], [], []
    for c in range(clips):
        n, pool = normed_tokens(
            c, flat, unit_frames, frame_counts, first_gain, first_shift
        )
        near.append((n, swap_unit(n, 1)))
        pooled.append(pool)
    wt, wg, query = queries_of(qkv_weight, proj_weight, query_bias, value_bias, pooled)
    own, rest, far = [], [], []
    for c in range(clips):
        across.append(swap_unit(together(near[c][0], wt)[0] if c else near[c][0], 2))
        own.append(forward(*near[c], wt, query[c][0], after=[v[3] for v in own[-1:]]))
    for c in range(clips):
        held, _ = together(across[c], own[c][3])
        far.append((held, swap_unit(held, 1)))
        rest.append(forward(*far[c], wt, query[c][0], after=[v[3] for v in (own + rest)[-1:]]))
    out, hg, attended, factors, keep, send0, across, send1, wpt = middle(
        me,
        [value[3] for value in own],
        [value[3] for value in rest],
        pooled,
        upstream,
        vectors,
        [proj_weight, output_weight, expand_weight, shrink_weight],
    )
    dq, dw = [[None, None] for _ in range(clips)], [[None, None] for _ in range(clips)]
    place = member()
    spread = (2, 4, 6)
    got = [swap_unit(send0, 1), swap_unit(send1, 1)]
    grads = attended_grads(hg, attended, factors, output_weight)
    got, grads = together(got, grads)
    do1, do2, do1t, do2t = grads
    (value,) = between("plain", [across, got[1]], place)
    terms = [keep, got[0]]
    calls = [(c, 1) for c in range(clips)] + [(c, 0) for c in range(clips)]
    parts = [[None] * 3 for _ in range(clips)]
    lent, owed = [], []
    moves = ["unit", "halves", "quarters", "join"]
    bits = []
    bit = 8
    while bit < lax.axis_size("clip"):
        bits.append(bit)
        bit *= 2
    held = [value]
    for at, (c, side) in enumerate(calls):
        keys, kept, grads = (far, rest, (do2, do2t)) if side else (near, own, (do1, do1t))
        move = moves[at] if at < len(moves) else None
        if move == "unit":
            sent = [swap_unit(value, 2)]
        elif move == "halves":
            sent = [swap_clip(value[1], 1)]
        elif move == "quarters":
            sent = [swap_clip(v, d) for v, d in zip(value[1:], spread, strict=True)]
        elif move == "join":
            sent = [swap_clip(value, d) for d in spread]
        else:
            sent = []
        travel = [swap_unit(parts[b][0], 2) for b in lent]
        travel += [swap_unit(gb, 1) for _, gb in owed]
        result = backward(c, *keys[c], wg, *kept[c][:3], *grads, query[c][1], after=held)
        *result, travel, sent = together(*result, travel, sent)
        dq[c][side], dw[c][side], ga, gb = result
        for b in lent:
            parts[b][0] = travel.pop(0)
        lent, loose = [], None
        for ((b, other), _), arrived in zip(owed, travel, strict=True):
            if other:
                loose = [parts[b][0], arrived]
                lent.append(b)
            else:
                parts[b][2] = arrived
        if move == "unit":
            value = list(between("halves", [*terms, *sent], place, loose))
        elif move == "halves":
            value = list(between("quarters", [value[0], *sent], place, loose))
        elif move == "quarters":
            value = list(between("plain", [value[0], *sent], place, loose))
        elif move == "join":
            value = list(between("join", [value, *sent], place, loose))
        if loose and move:
            *value, parts[lent[0]][0] = value
        elif loose:
            parts[lent[0]][0] = add(*loose)
        if move in ("quarters", "join"):
            (value,) = value
        if move == "quarters":
            for bit in bits:
                value = add(value, swap_clip(value, bit))
        owed = [((c, side), gb)]
        parts[c][0 if side else 1] = ga
        held = [dq[c][side], *(value if isinstance(value, list) else [value])]
        held += [parts[b][0] for b in lent]
    other = swap_clip(value, 1)
    travel = [swap_unit(gb, 1) for _, gb in owed]
    result = gather(
        me,
        [v for pair in dq for v in pair],
        [v for pair in dw for v in pair],
        pooled,
        wt,
        wpt,
        first_gain,
        first_shift,
        after=held,
    )
    (keep, send0, across, send1), travel = together(result, travel)
    for ((b, _), _), arrived in zip(owed, travel, strict=True):
        parts[b][2] = arrived
    got = [swap_unit(send0, 1), swap_unit(send1, 1)]
    second = add(across, got[1])
    input_grad, firsts = None, None
    bit = 0
    for c in range(max(clips, 3)):
        sent = swap_clip(second, bit) if bit else swap_unit(second, 2)
        if c < clips:
            input_grad = final(
                c, flat, hg, dq[c], proj_weight, qkv_weight, first_gain, parts[c], input_grad, after=[second]
            )
            sent, input_grad = together(sent, input_grad)
        elif firsts is None:
            firsts = unpack_first(place, value, other, after=[second])
            sent, firsts = together(sent, firsts)
        if c < 3:
            second = add(second, sent) if bit else add(keep, got[0], sent)
            bit = 2 * bit if bit else 1
    if firsts is None:
        firsts = unpack_first(place, value, other)
    for more in bits:
        second = add(second, swap_clip(second, more))
    wp_grad, bp_grad, wo_grad, bo_grad, g2_grad, s2_grad, we_grad, be_grad, ws_grad, bs_grad = firsts
    qkv_grad, bq_grad, bv_grad, g1_grad, s1_grad = unpack_second(second, swap_clip(second, bit))
    return (
        out.reshape(clips, 4, units, D_OUT).transpose(0, 2, 1, 3),
        input_grad.transpose(0, 3, 1, 2),
        g1_grad,
        s1_grad,
        wp_grad,
        bp_grad,
        qkv_grad,
        bq_grad,
        bv_grad,
        wo_grad,
        bo_grad,
        g2_grad,
        s2_grad,
        we_grad,
        be_grad,
        ws_grad,
        bs_grad,
    )


def solution(mesh):
    every = P()
    split = P("clip", "unit", None, None)
    return jax.shard_map(
        shards,
        mesh=mesh,
        in_specs=(split,) + (every,) * 15 + (P("clip"), P("clip", "unit"), split),
        out_specs=(
            split,
            split,
            P("unit"),
            P("unit"),
            P(None, "unit"),
            P("unit"),
            P(None, "unit"),
            P("unit"),
            P("unit"),
            P(None, "unit"),
            P("unit"),
            P("unit"),
            P("unit"),
            P(None, "unit"),
            P("unit"),
            P("unit", None),
            P("unit"),
        ),
        check_vma=False,
    )
```

```python
import functools

import jax
import jax.numpy as jnp
from jax import lax
from jax.experimental import pallas as pl
from jax.experimental.pallas import tpu as pltpu
from jax.sharding import PartitionSpec as P

D_IN = 192
D_OUT = 384
HEADS = 4
HEAD_DIM = 96
FF = 1536
LANES = 128
EXT = 208
SCALE = HEAD_DIM**-0.5
LOG2E = 1.4426950408889634
BF = jnp.bfloat16
F32 = jnp.float32
VMEM_MIB = 46
VMEM_MIB_FIRST = 64
FF_BLOCK = 768


def mm(a, b, ca, cb):
    return lax.dot_general(a, b, (((ca,), (cb,)), ((), ())), preferred_element_type=F32)


def iota(shape, dim):
    return lax.broadcasted_iota(jnp.int32, shape, dim)


def call(body, grid, ins, outs, scratch=(), name=None, cost=None, after=(), aliases=None, stays=None):
    count = len(ins)
    stays = stays or [False] * len(outs)

    def run(*refs):
        body(*refs[:count], *refs[count + len(after) :])

    ins = [*ins, *((pl.BlockSpec(memory_space=pl.ANY), value) for value in after)]
    return pl.pallas_call(
        run,
        grid=grid,
        in_specs=[spec for spec, _ in ins],
        out_specs=[spec for spec, _, _ in outs],
        out_shape=[
            (pltpu.HBM if stay else jax.ShapeDtypeStruct)(shape, dtype)
            for stay, (_, shape, dtype) in zip(stays, outs, strict=True)
        ],
        scratch_shapes=list(scratch),
        compiler_params=pltpu.CompilerParams(
            dimension_semantics=("arbitrary",) * len(grid), vmem_limit_bytes=(VMEM_MIB_FIRST if name in ("normed", "queries") else VMEM_MIB) * 2**20
        ),
        name=name,
        cost_estimate=pl.CostEstimate(
            flops=int(cost * 1.1e9), bytes_accessed=int(cost * 1e6), transcendentals=0
        ),
        input_output_aliases=aliases or {},
    )(*[value for _, value in ins])


def whole(value):
    rank = len(value.shape)
    return (pl.BlockSpec(value.shape, lambda *_: (0,) * rank), value)


def part(value):
    rank = len(value.shape)
    return (pl.BlockSpec((1,) + value.shape[1:], lambda i: (i,) + (0,) * (rank - 1)), value)


def at_clip(value, clip):
    rank = len(value.shape)
    return (pl.BlockSpec((1,) + value.shape[1:], lambda *_: (clip,) + (0,) * (rank - 1)), value)


def at_head(value, clip):
    rank = len(value.shape)
    return (
        pl.BlockSpec((None, 1) + value.shape[2:], lambda i: (clip, i) + (0,) * (rank - 2)),
        value,
    )


def out_part(shape, dtype):
    rank = len(shape)
    return (pl.BlockSpec((1,) + shape[1:], lambda i: (i,) + (0,) * (rank - 1)), shape, dtype)


def out_whole(shape, dtype):
    rank = len(shape)
    return (pl.BlockSpec(shape, lambda *_: (0,) * rank), shape, dtype)


def line(ref):
    return ref[...].astype(F32).reshape(1, -1)


def eye(size):
    return jnp.where(iota((size, size), 0) == iota((size, size), 1), 1.0, 0.0).astype(BF)


def column(ref):
    size = ref.shape[0]
    values = jnp.broadcast_to(line(ref), (16, size)).astype(BF)
    return mm(eye(size), values, 1, 1)[:, 0:1]


def normed_body(clips, tok_ref, frames_ref, counts_ref, gain_ref, shift_ref, *outs):
    slots, _, units = tok_ref.shape[1:]
    clip = pl.program_id(0)
    gain, shift = column(gain_ref), column(shift_ref)
    x = jnp.concatenate([tok_ref[0, s].astype(F32) for s in range(slots)], axis=1)
    center = x - jnp.mean(x, axis=0, keepdims=True)
    var = jnp.mean(center * center, axis=0, keepdims=True)
    normed = (center * lax.rsqrt(var + 1e-06) * gain + shift).astype(BF)
    extra = iota((EXT - D_IN, units), 0)
    invalid = jnp.where(frames_ref[pl.ds(clip, 1), :] >= counts_ref[clip], 1.0, 0.0)
    extra = jnp.where(extra == 0, 1.0, jnp.where(extra == 1, invalid, 0.0))
    extra = jnp.concatenate([extra] * slots, axis=1).astype(BF)
    full = normed.astype(F32)
    pieces = [full[:, units * s : units * (s + 1)] for s in range(slots)]
    means = []
    for p in range(4):
        first = 8 * (p >> 1) + 2 * (p & 1)
        means.append(
            (pieces[first] + pieces[first + 1] + pieces[first + 4] + pieces[first + 5]) * 0.25
        )
    pooled = jnp.concatenate(means, axis=1)
    row = iota((2 * LANES - D_IN, 4 * units), 0)
    pooled = jnp.concatenate([pooled, jnp.where(row == 0, 1.0, 0.0)], axis=0).T.astype(BF)
    for c in range(clips):

        @pl.when(clip == c)
        def _():
            outs[2 * c][:D_IN, :] = normed
            outs[2 * c][D_IN:, :] = extra
            outs[2 * c + 1][...] = pooled


def normed_tokens(tokens, frames, counts, gain, shift):
    clips, slots, _, units = tokens.shape
    outs = call(
        functools.partial(normed_body, clips),
        (clips,),
        [
            part(tokens),
            whole(frames),
            (pl.BlockSpec(memory_space=pltpu.SMEM), counts),
            whole(gain),
            whole(shift),
        ],
        [out_whole((EXT, slots * units), BF), out_whole((4 * units, 2 * LANES), BF)] * clips,
        name="normed",
        cost=5,
    )
    return outs[0::2], outs[1::2]


def query_body(clips, qkv_ref, wp_ref, qbias_ref, vbias_ref, *refs):
    pooled_refs, wt_ref, wg_ref, q_refs = refs[:clips], refs[clips], refs[clips + 1], refs[clips + 2 :]
    bias = jnp.concatenate(
        [line(qbias_ref), jnp.zeros((1, D_OUT), F32), line(vbias_ref)], axis=1
    )
    bias = jnp.where(iota((EXT - D_IN, 3 * D_OUT), 0) == 0, bias, 0.0).astype(BF)
    turned = jnp.concatenate([qkv_ref[...], bias], axis=0).astype(F32).T
    row, lane = iota((LANES - HEAD_DIM, EXT), 0), iota((LANES - HEAD_DIM, EXT), 1)
    ones = lane == D_IN
    extras = (
        jnp.where(ones & (row == 0), 8.0, 0.0),
        jnp.where((lane == D_IN + 1) & (row == 0), -1e30, jnp.where(ones & (row == 1), 1.0, 0.0)),
        jnp.where(ones & (row <= 1), 1.0, 0.0),
    )
    for block in range(3 * HEADS):
        rows = turned[HEAD_DIM * block : HEAD_DIM * (block + 1)]
        rows = jnp.concatenate([rows, extras[block // HEADS]], axis=0)
        wt_ref[block, :, :EXT] = rows.astype(BF)
        wt_ref[block, :, EXT:] = jnp.zeros((LANES, 2 * LANES - EXT), BF)
    wg_ref[...] = jnp.concatenate(
        [
            qkv_ref[:, start : start + HEAD_DIM]
            for h in range(HEADS)
            for start in (D_OUT + HEAD_DIM * h, 2 * D_OUT + HEAD_DIM * h)
        ],
        axis=1,
    )
    for block in range(D_OUT // LANES):
        columns = wp_ref[:, LANES * block : LANES * (block + 1)]
        wt_ref[3 * HEADS + block, :, :D_IN] = mm(eye(LANES), columns, 1, 1).astype(BF)
        wt_ref[3 * HEADS + block, :, D_IN:] = jnp.zeros((LANES, 2 * LANES - D_IN), BF)
    weight = wt_ref[:HEADS].reshape(HEADS * LANES, 2 * LANES)
    for c in range(clips):
        pooled = pooled_refs[c][...]
        q = mm(pooled, weight, 1, 1) * (SCALE * LOG2E)
        turned = mm(weight, pooled, 1, 1) * SCALE
        for h in range(HEADS):
            q_refs[2 * c][h] = q[:, LANES * h : LANES * (h + 1)].astype(BF)
            q_refs[2 * c + 1][h] = turned[LANES * h : LANES * h + HEAD_DIM].astype(BF)


def queries_of(qkv, wp, qbias, vbias, pooled):
    clips, count = len(pooled), pooled[0].shape[0]
    wt, wg, *rest = call(
        functools.partial(query_body, clips),
        (1,),
        [whole(v) for v in (qkv, wp, qbias, vbias, *pooled)],
        [
            out_whole((3 * HEADS + D_OUT // LANES, LANES, 2 * LANES), BF),
            out_whole((D_IN, 2 * D_OUT), BF),
            *[
                out_whole((HEADS, count, LANES), BF),
                out_whole((HEADS, HEAD_DIM, count), BF),
            ]
            * clips,
        ],
        name="queries",
        cost=5,
    )
    return wt, wg, [(rest[2 * c], rest[2 * c + 1]) for c in range(clips)]


def forward_body(na_ref, nb_ref, wt_ref, qs_ref, p_ref, kt_ref, vt_ref, o_ref, n_ref):
    rows = na_ref.shape[1]
    queries = qs_ref.shape[1]

    @pl.when(pl.program_id(0) == 0)
    def _():
        n_ref[:, :rows] = na_ref[...]
        n_ref[:, rows:] = nb_ref[...]

    h = pl.program_id(0)
    lane = iota((queries, LANES), 1)
    bound_lane = lane == HEAD_DIM + 1
    pick = (iota((16, LANES), 0) == 0) & (iota((16, LANES), 1) == HEAD_DIM + 1)
    pick = jnp.where(pick, 1.0, 0.0).astype(BF)
    tall = HEAD_DIM + 16
    kt = mm(wt_ref[HEADS + h][:, :EXT], n_ref[...], 1, 0)
    vt = mm(wt_ref[2 * HEADS + h][:, :EXT], n_ref[...], 1, 0).astype(BF)
    plain = kt[:HEAD_DIM]
    longest = jnp.max(jnp.sum(plain * plain, axis=0, keepdims=True), axis=1, keepdims=True)
    kt = kt.astype(BF)
    kt_ref[0] = kt
    vt_ref[0] = vt
    q = qs_ref[0].astype(F32)
    norm = jnp.sum(jnp.where(lane < HEAD_DIM, q * q, 0.0), axis=1, keepdims=True)
    q = jnp.where(bound_lane, -jnp.sqrt(norm * longest), q).astype(BF)
    p = jnp.exp2(mm(q, kt, 1, 0)).astype(BF)
    p_ref[0] = p
    o = mm(vt[:tall], p, 1, 1)
    o_ref[0, :tall] = o
    o_ref[0, tall:] = mm(pick, q, 1, 1)

    @pl.when(jnp.min(o[HEAD_DIM : HEAD_DIM + 1]) < 1e-27)
    def _():
        s = mm(qs_ref[0], kt_ref[0], 1, 0)
        m = jnp.max(s, axis=1, keepdims=True).astype(BF).astype(F32)
        again = jnp.exp2(s - m).astype(BF)
        p_ref[0] = again
        o_ref[0, :tall] = mm(vt_ref[0, :tall], again, 1, 1)
        o_ref[0, tall:] = mm(
            pick, jnp.where(bound_lane, -m, qs_ref[0].astype(F32)).astype(BF), 1, 1
        )


def forward(na, nb, wt, qs, after=()):
    rows = na.shape[1]
    queries = qs.shape[1]
    return call(
        forward_body,
        (HEADS,),
        [whole(na), whole(nb), whole(wt), part(qs)],
        [
            out_part((HEADS, queries, 2 * rows), BF),
            out_part((HEADS, LANES, 2 * rows), BF),
            out_part((HEADS, LANES, 2 * rows), BF),
            out_part((HEADS, LANES, queries), F32),
        ],
        [pltpu.VMEM((EXT, 2 * rows), BF)],
        name="attend",
        after=after,
        stays=[True] * 4,
        cost=12,
    )


def middle_body(clips, me_ref, *refs):
    o1_refs, o2_refs, pooled_refs = refs[:clips], refs[clips : 2 * clips], refs[2 * clips : 3 * clips]
    up_ref, bproj_ref, bout_ref, gain_ref, shift_ref, bshrink_ref, bexpand_ref = refs[
        3 * clips : 3 * clips + 7
    ]
    wp_ref, wo_ref, we_ref, ws_ref = refs[3 * clips + 7 : 3 * clips + 11]
    out_ref, hg_ref, do1_ref, do2_ref, do1t_ref, do2t_ref = refs[3 * clips + 11 : 3 * clips + 17]
    shard_refs, wpt_ref = refs[3 * clips + 17 : 3 * clips + 21], refs[3 * clips + 21]
    we_acc, ws_acc, wo_acc, wp_acc, misc_acc = refs[3 * clips + 22 :]
    queries = pooled_refs[0].shape[0]
    rows = [slice(queries * c, queries * (c + 1)) for c in range(clips)]
    heads = [[] for _ in range(clips)]
    factors = [[] for _ in range(clips)]
    for c in range(clips):
        for h in range(HEADS):
            o1, o2 = o1_refs[c][h], o2_refs[c][h]
            l1, l2 = o1[HEAD_DIM : HEAD_DIM + 1], o2[HEAD_DIM : HEAD_DIM + 1]
            m1, m2 = -o1[HEAD_DIM + 16 : HEAD_DIM + 17], -o2[HEAD_DIM + 16 : HEAD_DIM + 17]
            m = jnp.maximum(m1, m2)
            a1, a2 = jnp.exp2(m1 - m), jnp.exp2(m2 - m)
            inverse = 1.0 / (a1 * l1 + a2 * l2)
            c1, c2 = a1 * inverse, a2 * inverse
            heads[c].append(o1[:HEAD_DIM] * c1 + o2[:HEAD_DIM] * c2)
            factors[c].append((c1, c2))
    attended = jnp.concatenate([jnp.concatenate(parts, axis=0).T for parts in heads], axis=0)
    attended = attended.astype(BF)
    pooled = jnp.concatenate([ref[...].astype(F32) for ref in pooled_refs], axis=0).astype(BF)
    up = jnp.concatenate([up_ref[c].astype(F32) for c in range(clips)], axis=0)
    up_low = up.astype(BF)
    hidden = mm(pooled[:, :D_IN], wp_ref[...], 1, 0) + line(bproj_ref)
    hidden = hidden + mm(attended, wo_ref[...], 1, 0) + line(bout_ref)
    center = hidden - jnp.mean(hidden, axis=1, keepdims=True)
    inv_std = lax.rsqrt(jnp.mean(center * center, axis=1, keepdims=True) + 1e-06)
    n = center * inv_std
    gain2 = line(gain_ref)
    second = (n * gain2 + line(shift_ref)).astype(BF)
    out = hidden + line(bshrink_ref)
    second_grad = jnp.zeros(out.shape, F32)
    bexpand = line(bexpand_ref)
    for start in range(0, FF, FF_BLOCK):
        block = slice(start, start + FF_BLOCK)
        before = mm(second, we_ref[:, block], 1, 0) + bexpand[:, block]
        cdf = 0.5 + 0.5 * lax.erf(before * (0.5**0.5))
        active = (before * cdf).astype(BF)
        out = out + mm(active, ws_ref[block, :], 1, 0)
        slope = cdf + before * (jnp.exp(before * before * -0.5) * (0.5 / jnp.pi) ** 0.5)
        before_grad = (mm(up_low, ws_ref[block, :], 1, 1) * slope).astype(BF)
        ws_acc[:, block] = mm(up_low, active, 0, 0)
        we_acc[:, block] = mm(second, before_grad, 0, 0)
        second_grad = second_grad + mm(before_grad, we_ref[:, block], 1, 1)
        misc_acc[0:1, block] = jnp.sum(before_grad.astype(F32), axis=0, keepdims=True)
    for c in range(clips):
        out_ref[c] = out[rows[c]]
    e = gain2 * second_grad
    back = (
        e - jnp.mean(e, axis=1, keepdims=True) - n * jnp.mean(e * n, axis=1, keepdims=True)
    ) * inv_std
    hidden_full = (up + back).astype(BF).astype(F32)
    hidden_grad = hidden_full.astype(BF)
    wo_acc[...] = mm(hidden_grad, attended, 0, 0)
    wp_acc[...] = mm(hidden_grad, pooled, 0, 0)
    misc_acc[1:2, :D_OUT] = jnp.sum(second_grad * n, axis=0, keepdims=True)
    misc_acc[2:3, :D_OUT] = jnp.sum(second_grad, axis=0, keepdims=True)
    misc_acc[3:4, :D_OUT] = jnp.sum(up, axis=0, keepdims=True)
    misc_acc[4:5, :D_OUT] = jnp.sum(hidden_full, axis=0, keepdims=True)
    row = iota((LANES - HEAD_DIM, queries), 0)
    for c in range(clips):
        own_grad = hidden_full[rows[c]].astype(BF)
        hg_ref[c] = own_grad
        attended_grad = mm(wo_ref[...], own_grad, 1, 1).astype(BF).astype(F32)
        for h in range(HEADS):
            own = attended_grad[HEAD_DIM * h : HEAD_DIM * (h + 1)]
            for factor, do_ref, dot_ref in zip(
                factors[c][h], (do1_ref, do2_ref), (do1t_ref, do2t_ref), strict=True
            ):
                scaled = (own * factor).astype(BF)
                dot_ref[c, h] = scaled
                scaled = scaled.astype(F32)
                inner = jnp.sum(scaled * heads[c][h], axis=0, keepdims=True)
                high = inner.astype(BF).astype(F32)
                extra = jnp.where(row == 0, -high, jnp.where(row == 1, high - inner, 0.0))
                do_ref[c, h] = jnp.concatenate([scaled, extra], axis=0).T.astype(BF)
    me = me_ref[0]
    wpt_ref[...] = wp_acc[...]
    for u in range(4):
        for k in range(4):
            misc_acc[8 + u : 9 + u, HEAD_DIM * k : HEAD_DIM * (k + 1)] = misc_acc[
                1 + k : 2 + k, HEAD_DIM * u : HEAD_DIM * (u + 1)
            ]
    for r in range(4):
        u = me ^ r
        ref = shard_refs[r]
        wide = pl.ds(pl.multiple_of(u * 384, LANES), 384)
        tall = pl.ds(pl.multiple_of(u * 96, 8), 96)
        ref[0:384, :] = we_acc[:, wide].astype(BF)
        ref[384:768, :] = ws_acc[:, wide].astype(BF)
        ref[768:864, :] = wo_acc[tall, :].astype(BF)
        wp = wp_acc[tall, :]
        ref[864:912, :] = jnp.concatenate([wp[:48, :D_IN], wp[48:, :D_IN]], axis=1).astype(BF)
        bias = misc_acc[0:1, wide]
        others = misc_acc[pl.ds(8 + u, 1), :384]
        row = iota((48, 384), 0)
        ref[912:960, :] = jnp.where(row == 0, bias, jnp.where(row == 1, others, 0.0)).astype(BF)


def middle(me, o1, o2, pooled, up, vectors, weights):
    clips = len(pooled)
    queries = pooled[0].shape[0]
    grad = (clips, HEADS, queries, LANES)
    grad_t = (clips, HEADS, HEAD_DIM, queries)
    return call(
        functools.partial(middle_body, clips),
        (1,),
        [
            (pl.BlockSpec(memory_space=pltpu.SMEM), me),
            *(whole(value) for value in (*o1, *o2, *pooled, up, *vectors, *weights)),
        ],
        [
            out_whole((clips, queries, D_OUT), F32),
            out_whole((clips, queries, D_OUT), BF),
            out_whole(grad, BF),
            out_whole(grad, BF),
            out_whole(grad_t, BF),
            out_whole(grad_t, BF),
            *([out_whole((960, 384), BF)] * 4),
            out_whole((D_OUT, 2 * LANES), F32),
        ],
        [
            pltpu.VMEM((D_OUT, FF), F32),
            pltpu.VMEM((D_OUT, FF), F32),
            pltpu.VMEM((D_OUT, D_OUT), F32),
            pltpu.VMEM((D_OUT, 2 * LANES), F32),
            pltpu.VMEM((16, FF), F32),
        ],
        name="middle",
        stays=[True] * 11,
        cost=16,
    )


def backward_body(
    na_ref,
    nb_ref,
    wg_ref,
    p_ref,
    kt_ref,
    vt_ref,
    do_ref,
    dot_ref,
    qt_ref,
    dq_ref,
    dw_ref,
    ga_ref,
    gb_ref,
    n_ref,
    both_ref,
):
    rows = na_ref.shape[1]
    h = pl.program_id(0)
    p = p_ref[0]
    ds = p * mm(do_ref[0], vt_ref[0], 1, 0).astype(BF)
    dq_ref[0] = mm(kt_ref[0, :HEAD_DIM], ds, 1, 1)
    both_ref[h, :HEAD_DIM] = mm(qt_ref[0], ds, 1, 0).astype(BF)
    both_ref[h, HEAD_DIM:] = mm(dot_ref[0], p, 1, 0).astype(BF)

    @pl.when(h == HEADS - 1)
    def _():
        n_ref[:, :rows] = na_ref[...]
        n_ref[:, rows:] = nb_ref[...]
        both = both_ref[...].reshape(2 * D_OUT, 2 * rows)
        dw_ref[...] = mm(both, n_ref[...], 1, 1)
        g = mm(wg_ref[...], both, 1, 0).astype(BF)
        ga_ref[...] = g[:, :rows]
        gb_ref[...] = g[:, rows:]


def backward(clip, na, nb, wg, p, kt, vt, do, dot, qt, after=()):
    rows = na.shape[1]
    queries = qt.shape[2]
    return call(
        backward_body,
        (HEADS,),
        [
            whole(na),
            whole(nb),
            whole(wg),
            part(p),
            part(kt),
            part(vt),
            at_head(do, clip),
            at_head(dot, clip),
            part(qt),
        ],
        [
            out_part((HEADS, HEAD_DIM, queries), F32),
            out_whole((2 * D_OUT, EXT), F32),
            out_whole((D_IN, rows), BF),
            out_whole((D_IN, rows), BF),
        ],
        [pltpu.VMEM((EXT, 2 * rows), BF), pltpu.VMEM((HEADS, 2 * HEAD_DIM, 2 * rows), BF)],
        name="attend_back",
        after=after,
        cost=17,
    )


def gather_body(clips, me_ref, *refs):
    dq_refs, dw_refs, pooled_refs = (
        refs[: 2 * clips],
        refs[2 * clips : 4 * clips],
        refs[4 * clips : 5 * clips],
    )
    wt_ref, wpt_ref, gain_ref, shift_ref = refs[5 * clips : 5 * clips + 4]
    shard_refs, (dw_acc, line_ref, shard_ref) = refs[5 * clips + 4 : 5 * clips + 8], refs[5 * clips + 8 :]
    total = dw_refs[0][...]
    for ref in dw_refs[1:]:
        total = total + ref[...]
    for h in range(HEADS):
        at = 2 * HEAD_DIM * h
        dw_acc[HEADS + h] = total[at : at + HEAD_DIM]
        dw_acc[2 * HEADS + h] = total[at + HEAD_DIM : at + 2 * HEAD_DIM]
    dw = None
    for c in range(clips):
        dq = (dq_refs[2 * c][...] + dq_refs[2 * c + 1][...]) * SCALE
        dq = dq.reshape(D_OUT, dq.shape[2]).astype(BF)
        term = mm(dq, pooled_refs[c][...], 1, 0)
        dw = term if dw is None else dw + term
    for h in range(HEADS):
        dw_acc[h] = dw[HEAD_DIM * h : HEAD_DIM * (h + 1), :EXT]
    gain_sum = jnp.zeros((1, D_IN), F32)
    shift_sum = jnp.zeros((1, D_IN), F32)
    wp = wt_ref[3 * HEADS :].reshape(D_OUT, 2 * LANES)[:, :D_IN]
    terms = [(wt_ref[b][:HEAD_DIM, :D_IN], dw_acc[b]) for b in range(3 * HEADS)]
    for w, dw in [*terms, (wp, wpt_ref[...])]:
        w = w.astype(F32)
        gain_sum = gain_sum + jnp.sum(w * dw[:, :D_IN], axis=0, keepdims=True)
        shift_sum = shift_sum + jnp.sum(w * dw[:, D_IN : D_IN + 1], axis=0, keepdims=True)
    gain_sum = (gain_sum - line(shift_ref) * shift_sum) / line(gain_ref)
    for at, first in ((0, 0), (1, 2 * HEADS)):
        for h in range(HEADS):
            sums = dw_acc[first + h][:, LANES:]
            sums = jnp.concatenate(
                [sums, jnp.zeros((HEAD_DIM, 2 * LANES - EXT), F32)], axis=1
            )
            sums = jnp.concatenate([sums, jnp.zeros((LANES - HEAD_DIM, LANES), F32)], axis=0).T
            line_ref[at : at + 1, HEAD_DIM * h : HEAD_DIM * (h + 1)] = sums[
                D_IN - LANES : D_IN - LANES + 1, :HEAD_DIM
            ]
    line_ref[2:3, :D_IN] = gain_sum
    line_ref[3:4, :D_IN] = shift_sum
    for u in range(4):
        at = 0
        for source, size in ((0, 96), (1, 96), (2, 48), (3, 48)):
            shard_ref[u : u + 1, at : at + size] = line_ref[
                source : source + 1, size * u : size * (u + 1)
            ]
            at += size
        shard_ref[u : u + 1, at:] = jnp.zeros((1, D_OUT - at), F32)
    for r in range(4):
        u = me_ref[0] ^ r
        ref = shard_refs[r]
        rows = jnp.concatenate([dw_acc[3 * u + i][:, :D_IN] for i in range(3)], axis=0)
        ref[:144, :] = jnp.concatenate([rows[:144], rows[144:]], axis=1).astype(BF)
        ref[144:, :] = jnp.where(
            iota((16, D_OUT), 0) == 0, shard_ref[pl.ds(u, 1), :], 0.0
        ).astype(BF)


def gather(me, dq, dw, pooled, wt, wpt, gain, shift, after=()):
    clips = len(pooled)
    return call(
        functools.partial(gather_body, clips),
        (1,),
        [
            (pl.BlockSpec(memory_space=pltpu.SMEM), me),
            *(whole(v) for v in (*dq, *dw, *pooled, wt, wpt, gain, shift)),
        ],
        [out_whole((160, D_OUT), BF)] * 4,
        [
            pltpu.VMEM((3 * HEADS, HEAD_DIM, EXT), F32),
            pltpu.VMEM((8, D_OUT), F32),
            pltpu.VMEM((8, D_OUT), F32),
        ],
        name="gather",
        after=after,
        cost=6,
    )


def final_body(terms, tok_ref, hg_ref, wp_ref, qkv_ref, gain_ref, dq1_ref, dq2_ref, *refs):
    part_refs, out_ref = refs[:terms], refs[-1]
    slots, _, units = tok_ref.shape[1:]
    gain = column(gain_ref)
    dq = ((dq1_ref[...] + dq2_ref[...]) * SCALE).reshape(D_OUT, 4 * units).astype(BF)
    spread = mm(wp_ref[...], hg_ref[0], 1, 1) + mm(qkv_ref[:, :D_OUT], dq, 1, 0)
    spread = spread * 0.25
    places = [slice(units * s, units * (s + 1)) for s in range(slots)]
    spread = [spread[:, places[2 * (s >> 3) + ((s >> 1) & 1)]] for s in range(slots)]
    grad = total_of(part_refs) + jnp.concatenate(spread, axis=1)
    x = jnp.concatenate([tok_ref[0, s].astype(F32) for s in range(slots)], axis=1)
    center = x - jnp.mean(x, axis=0, keepdims=True)
    inv_std = lax.rsqrt(jnp.mean(center * center, axis=0, keepdims=True) + 1e-06)
    n = center * inv_std
    e = grad * gain
    back = e - jnp.mean(e, axis=0, keepdims=True) - n * jnp.mean(e * n, axis=0, keepdims=True)
    back = back * inv_std
    for s in range(slots):
        out_ref[0, s] = back[:, places[s]]


def final(clip, tokens, hg, dq, wp, qkv, gain, parts, filled, after=()):
    terms = len(parts)
    return call(
        functools.partial(final_body, terms),
        (1,),
        [
            at_clip(tokens, clip),
            at_clip(hg, clip),
            *(whole(v) for v in (wp, qkv, gain, *dq, *parts)),
            *([] if filled is None else [(pl.BlockSpec(memory_space=pl.ANY), filled)]),
        ],
        [(at_clip(tokens, clip)[0], tokens.shape, F32)],
        name="final",
        stays=[True],
        cost=6,
        after=after,
        aliases=None if filled is None else {7 + terms: 0},
    )[0]


def unpack_first_body(
    place_ref,
    value_ref,
    other_ref,
    proj_ref,
    bproj_ref,
    wo_ref,
    bout_ref,
    gain_ref,
    shift_ref,
    we_ref,
    be_ref,
    ws_ref,
    bs_ref,
    rows_ref,
):
    half = value_ref.shape[0]
    at = pl.multiple_of(place_ref[0] * half, 8)
    rows_ref[pl.ds(at, half), :] = value_ref[...].astype(F32)
    rows_ref[pl.ds(pl.multiple_of(half - at, 8), half), :] = other_ref[...].astype(F32)
    we_ref[...] = rows_ref[:384]
    ws_ref[...] = rows_ref[384:768].T
    wo_ref[...] = rows_ref[768:864]
    proj = jnp.concatenate([rows_ref[864:912, :D_IN], rows_ref[864:912, D_IN:]], axis=0)
    proj_ref[...] = proj.T
    lines = rows_ref[912:920]
    be_ref[...] = lines[0:1].reshape(384)
    for ref, k in ((gain_ref, 0), (shift_ref, 1), (bs_ref, 2), (bout_ref, 3), (bproj_ref, 3)):
        ref[...] = lines[1:2, 96 * k : 96 * (k + 1)].reshape(96)


def unpack_first(place, value, other, after=()):
    shapes = [(192, 96), (96,), (96, 384), (96,), (96,), (96,), (384, 384), (384,), (384, 384), (96,)]
    return call(
        unpack_first_body,
        (1,),
        [(pl.BlockSpec(memory_space=pltpu.SMEM), place), whole(value), whole(other)],
        [out_whole(shape, F32) for shape in shapes],
        [pltpu.VMEM((2 * value.shape[0], D_OUT), F32)],
        name="unpack_first",
        stays=[True] * len(shapes),
        after=after,
        cost=2,
    )


def unpack_second_body(a_ref, b_ref, qkv_ref, bq_ref, bv_ref, gain_ref, shift_ref):
    total = a_ref[...].astype(F32) + b_ref[...].astype(F32)
    qkv_ref[...] = jnp.concatenate([total[:144, :D_IN], total[:144, D_IN:]], axis=0).T
    at = 0
    for ref in (bq_ref, bv_ref, gain_ref, shift_ref):
        size = ref.shape[0]
        ref[...] = total[144:145, at : at + size].reshape(size)
        at += size


def unpack_second(a, b):
    shapes = [(192, 288), (96,), (96,), (48,), (48,)]
    return call(
        unpack_second_body,
        (1,),
        [whole(a), whole(b)],
        [out_whole(shape, F32) for shape in shapes],
        name="unpack_second",
        stays=[True] * len(shapes),
        cost=1,
    )


def swap_unit(value, bit):
    return lax.ppermute(value, "unit", [(i, i ^ bit) for i in range(4)])


def swap_clip(value, bit):
    size = lax.axis_size("clip")
    return lax.ppermute(value, "clip", [(i, i ^ bit) for i in range(size)])


def add(*values):
    return functools.reduce(lambda a, b: a + b, [v.astype(F32) for v in values]).astype(BF)


def member():
    at = lax.axis_index("clip").astype(jnp.int32)
    return jnp.stack([at & 1, (at >> 1) & 1])


def total_of(refs):
    return functools.reduce(lambda a, b: a + b, [ref[...].astype(F32) for ref in refs])


def between(sums, place, cut=None, grads=None, join=None):
    rows, width = sums[0].shape
    count, more = len(sums), grads or []
    pieces = 1 if cut is None else 2
    tall = 2 * rows if join is not None else rows // pieces

    def body(place_ref, *refs):
        terms, refs = refs[:count], refs[count:]
        others, refs = refs[: len(more)], refs[len(more) :]
        outs, scratch = refs[:-1], refs[-1]
        if more:
            outs[-1][...] = total_of(others).astype(BF)
        if join is not None:
            for d in range(2):
                at = pl.multiple_of((place_ref[join] ^ d) * rows, 8)
                scratch[pl.ds(at, rows), :] = terms[d][...].astype(F32)
            outs[0][...] = scratch[...].astype(BF)
        elif cut is None:
            outs[0][...] = total_of(terms).astype(BF)
        else:
            scratch[...] = total_of(terms)
            for d in range(2):
                at = pl.multiple_of((place_ref[cut] ^ d) * tall, 8)
                outs[d][...] = scratch[pl.ds(at, tall), :].astype(BF)

    return list(
        call(
            body,
            (1,),
            [(pl.BlockSpec(memory_space=pltpu.SMEM), place), *(whole(v) for v in (*sums, *more))],
            [
                *([out_whole((tall, width), BF)] * pieces),
                *([out_whole(more[0].shape, BF)] if more else []),
            ],
            [pltpu.VMEM((max(rows, tall), width), F32)],
            name="between",
            cost=2,
        )
    )


def in_hbm(*values):
    return [pltpu.with_memory_space_constraint(v, pltpu.HBM) for v in values]


def together(*values):
    return lax.optimization_barrier(values)


def shards(
    tokens,
    first_gain,
    first_shift,
    proj_weight,
    proj_bias,
    qkv_weight,
    query_bias,
    value_bias,
    output_weight,
    output_bias,
    second_gain,
    second_shift,
    expand_weight,
    expand_bias,
    shrink_weight,
    shrink_bias,
    frame_counts,
    unit_frames,
    cotangent,
):
    clips, units = tokens.shape[:2]
    me = lax.axis_index("unit").astype(jnp.int32).reshape(1)
    vectors = [proj_bias, output_bias, second_gain, second_shift, shrink_bias, expand_bias]
    flat = tokens.transpose(0, 2, 3, 1)
    upstream = cotangent.transpose(0, 2, 1, 3).reshape(clips, 4 * units, D_OUT)
    normed, pooled = normed_tokens(flat, unit_frames, frame_counts, first_gain, first_shift)
    near, across = [(n, swap_unit(n, 1)) for n in normed], []
    wt, wg, query = queries_of(qkv_weight, proj_weight, query_bias, value_bias, pooled)
    own, rest, far = [], [], []
    for c in range(clips):
        across.append(swap_unit(together(near[c][0], wt)[0] if c else near[c][0], 2))
        weights = [wt, query[c][0]] if c else in_hbm(wt, query[c][0])
        keys = near[c] if c else in_hbm(*near[c])
        own.append(forward(*keys, *weights, after=in_hbm(*(v[3] for v in own[-1:]))))
    for c in range(clips):
        held, _ = together(across[c], own[c][3])
        far.append((held, swap_unit(held, 1)))
        rest.append(forward(*far[c], wt, query[c][0], after=in_hbm(*(v[3] for v in (own + rest)[-1:]))))
    out, hg, do1, do2, do1t, do2t, keep, send0, across, send1, wpt = middle(
        me,
        in_hbm(*(value[3] for value in own)),
        in_hbm(*(value[3] for value in rest)),
        pooled,
        upstream,
        vectors,
        [proj_weight, output_weight, expand_weight, shrink_weight],
    )
    dq, dw = [[None, None] for _ in range(clips)], [[None, None] for _ in range(clips)]
    place = member()
    got = [swap_unit(send0, 1), swap_unit(send1, 1)]
    out = out.reshape(clips, 4, units, D_OUT).transpose(0, 2, 1, 3)
    got, out = together(got, out)
    (value,) = between([across, got[1]], place)
    terms = [keep, got[0]]
    calls = [(c, 1) for c in range(clips)] + [(c, 0) for c in range(clips)]
    parts = [[None] * 3 for _ in range(clips)]
    lent, owed = [], []
    moves = ["unit", 1, 2, 4]
    bits = []
    bit = 8
    while bit < lax.axis_size("clip"):
        bits.append(bit)
        bit *= 2
    held = [value]
    for at, (c, side) in enumerate(calls):
        keys, kept, grads = (far, rest, (do2, do2t)) if side else (near, own, (do1, do1t))
        move = moves[at]
        sent = [swap_unit(value, 2) if move == "unit" else swap_clip(value, move)]
        travel = [swap_unit(parts[b][0], 2) for b in lent]
        travel += [swap_unit(gb, 1) for _, gb in owed]
        result = backward(c, *keys[c], wg, *kept[c][:3], *grads, query[c][1], after=held)
        *result, travel, sent = together(*result, travel, sent)
        dq[c][side], dw[c][side], ga, gb = result
        for b in lent:
            parts[b][0] = travel.pop(0)
        lent, loose = [], None
        for ((b, other), _), arrived in zip(owed, travel, strict=True):
            if other:
                loose = [parts[b][0], arrived]
                lent.append(b)
            else:
                parts[b][2] = arrived
        cut = {"unit": 0, 1: 1}.get(move)
        result = between([*terms, *sent], place, cut, loose)
        if loose:
            parts[lent[0]][0] = result.pop()
        if cut is None:
            (value,), terms = result, result
        else:
            terms, value = result[:1], result[1]
        if move == 2:
            for bit in bits:
                value = add(value, swap_clip(value, bit))
            terms = [value]
        owed = [((c, side), gb)]
        parts[c][0 if side else 1] = ga
        held = [dq[c][side], value, *terms, *(parts[b][0] for b in lent)]
    half = swap_clip(value, 2)
    travel = [swap_unit(gb, 1) for _, gb in owed]
    result = gather(
        me,
        [v for pair in dq for v in pair],
        [v for pair in dw for v in pair],
        pooled,
        wt,
        wpt,
        first_gain,
        first_shift,
        after=held,
    )
    (keep, send0, across, send1), travel = together(result, travel)
    for ((b, _), _), arrived in zip(owed, travel, strict=True):
        parts[b][2] = arrived
    got = [swap_unit(send0, 1), swap_unit(send1, 1)]
    second = add(across, got[1])
    input_grad, firsts = None, None
    bit = 0
    for c in range(max(clips, 3)):
        sent = swap_clip(second, bit) if bit else swap_unit(second, 2)
        if c < clips:
            input_grad = final(
                c, flat, hg, dq[c], proj_weight, qkv_weight, first_gain, parts[c], input_grad, after=[second]
            )
            if c == 0:
                sent, input_grad, half = together(sent, input_grad, half)
                (value,) = between([value, half], place, join=1)
                other = swap_clip(value, 1)
            else:
                sent, input_grad = together(sent, input_grad)
        if c < 3:
            second = add(second, sent) if bit else add(keep, got[0], sent)
            bit = 2 * bit if bit else 1
    last = swap_clip(second, 4)
    firsts = unpack_first(place, value, other, after=[second])
    last, firsts = together(last, firsts)
    for more in bits:
        second, last = add(second, last), None
        last = swap_clip(second, more)
    wp_grad, bp_grad, wo_grad, bo_grad, g2_grad, s2_grad, we_grad, be_grad, ws_grad, bs_grad = firsts
    qkv_grad, bq_grad, bv_grad, g1_grad, s1_grad = unpack_second(second, last)
    return (
        out,
        input_grad.transpose(0, 3, 1, 2),
        g1_grad,
        s1_grad,
        wp_grad,
        bp_grad,
        qkv_grad,
        bq_grad,
        bv_grad,
        wo_grad.T,
        bo_grad,
        g2_grad,
        s2_grad,
        we_grad,
        be_grad,
        ws_grad,
        bs_grad,
    )


def solution(mesh):
    every = P()
    split = P("clip", "unit", None, None)
    return jax.shard_map(
        shards,
        mesh=mesh,
        in_specs=(split,) + (every,) * 15 + (P("clip"), P("clip", "unit"), split),
        out_specs=(
            split,
            split,
            P("unit"),
            P("unit"),
            P(None, "unit"),
            P("unit"),
            P(None, "unit"),
            P("unit"),
            P("unit"),
            P(None, "unit"),
            P("unit"),
            P("unit"),
            P("unit"),
            P(None, "unit"),
            P("unit"),
            P("unit", None),
            P("unit"),
        ),
        check_vma=False,
    )
```

```python
import functools

import jax
import jax.numpy as jnp
from jax import lax
from jax.experimental import pallas as pl
from jax.experimental.pallas import tpu as pltpu
from jax.sharding import PartitionSpec as P

D_IN = 192
D_OUT = 384
HEADS = 4
HEAD_DIM = 96
FF = 1536
LANES = 128
EXT = 208
SCALE = HEAD_DIM**-0.5
LOG2E = 1.4426950408889634
BF = jnp.bfloat16
F32 = jnp.float32
VMEM_MIB = 46
VMEM_MIB_FIRST = 64
FF_BLOCK = 768


def mm(a, b, ca, cb):
    return lax.dot_general(a, b, (((ca,), (cb,)), ((), ())), preferred_element_type=F32)


def iota(shape, dim):
    return lax.broadcasted_iota(jnp.int32, shape, dim)


def call(body, grid, ins, outs, scratch=(), name=None, cost=None, after=(), aliases=None, stays=None):
    count = len(ins)
    stays = stays or [False] * len(outs)

    def run(*refs):
        body(*refs[:count], *refs[count + len(after) :])

    ins = [*ins, *((pl.BlockSpec(memory_space=pl.ANY), value) for value in after)]
    return pl.pallas_call(
        run,
        grid=grid,
        in_specs=[spec for spec, _ in ins],
        out_specs=[spec for spec, _, _ in outs],
        out_shape=[
            (pltpu.HBM if stay else jax.ShapeDtypeStruct)(shape, dtype)
            for stay, (_, shape, dtype) in zip(stays, outs, strict=True)
        ],
        scratch_shapes=list(scratch),
        compiler_params=pltpu.CompilerParams(
            dimension_semantics=("arbitrary",) * len(grid), vmem_limit_bytes=(VMEM_MIB_FIRST if name in ("normed", "queries") else VMEM_MIB) * 2**20
        ),
        name=name,
        cost_estimate=pl.CostEstimate(
            flops=int(cost * 1.1e9), bytes_accessed=int(cost * 1e6), transcendentals=0
        ),
        input_output_aliases=aliases or {},
    )(*[value for _, value in ins])


def whole(value):
    rank = len(value.shape)
    return (pl.BlockSpec(value.shape, lambda *_: (0,) * rank), value)


def part(value):
    rank = len(value.shape)
    return (pl.BlockSpec((1,) + value.shape[1:], lambda i: (i,) + (0,) * (rank - 1)), value)


def at_clip(value, clip):
    rank = len(value.shape)
    return (pl.BlockSpec((1,) + value.shape[1:], lambda *_: (clip,) + (0,) * (rank - 1)), value)


def at_head(value, clip):
    rank = len(value.shape)
    return (
        pl.BlockSpec((None, 1) + value.shape[2:], lambda i: (clip, i) + (0,) * (rank - 2)),
        value,
    )


def out_part(shape, dtype):
    rank = len(shape)
    return (pl.BlockSpec((1,) + shape[1:], lambda i: (i,) + (0,) * (rank - 1)), shape, dtype)


def out_whole(shape, dtype):
    rank = len(shape)
    return (pl.BlockSpec(shape, lambda *_: (0,) * rank), shape, dtype)


def line(ref):
    return ref[...].astype(F32).reshape(1, -1)


def eye(size):
    return jnp.where(iota((size, size), 0) == iota((size, size), 1), 1.0, 0.0).astype(BF)


def column(ref):
    size = ref.shape[0]
    values = jnp.broadcast_to(line(ref), (16, size)).astype(BF)
    return mm(eye(size), values, 1, 1)[:, 0:1]


def normed_body(clips, tok_ref, frames_ref, counts_ref, gain_ref, shift_ref, *outs):
    slots, _, units = tok_ref.shape[1:]
    clip = pl.program_id(0)
    gain, shift = column(gain_ref), column(shift_ref)
    x = jnp.concatenate([tok_ref[0, s].astype(F32) for s in range(slots)], axis=1)
    center = x - jnp.mean(x, axis=0, keepdims=True)
    var = jnp.mean(center * center, axis=0, keepdims=True)
    normed = (center * lax.rsqrt(var + 1e-06) * gain + shift).astype(BF)
    extra = iota((EXT - D_IN, units), 0)
    invalid = jnp.where(frames_ref[pl.ds(clip, 1), :] >= counts_ref[clip], 1.0, 0.0)
    extra = jnp.where(extra == 0, 1.0, jnp.where(extra == 1, invalid, 0.0))
    extra = jnp.concatenate([extra] * slots, axis=1).astype(BF)
    full = normed.astype(F32)
    pieces = [full[:, units * s : units * (s + 1)] for s in range(slots)]
    means = []
    for p in range(4):
        first = 8 * (p >> 1) + 2 * (p & 1)
        means.append(
            (pieces[first] + pieces[first + 1] + pieces[first + 4] + pieces[first + 5]) * 0.25
        )
    pooled = jnp.concatenate(means, axis=1)
    row = iota((2 * LANES - D_IN, 4 * units), 0)
    pooled = jnp.concatenate([pooled, jnp.where(row == 0, 1.0, 0.0)], axis=0).T.astype(BF)
    for c in range(clips):

        @pl.when(clip == c)
        def _():
            outs[2 * c][:D_IN, :] = normed
            outs[2 * c][D_IN:, :] = extra
            outs[2 * c + 1][...] = pooled


def normed_tokens(tokens, frames, counts, gain, shift):
    clips, slots, _, units = tokens.shape
    outs = call(
        functools.partial(normed_body, clips),
        (clips,),
        [
            part(tokens),
            whole(frames),
            (pl.BlockSpec(memory_space=pltpu.SMEM), counts),
            whole(gain),
            whole(shift),
        ],
        [out_whole((EXT, slots * units), BF), out_whole((4 * units, 2 * LANES), BF)] * clips,
        name="normed",
        cost=5,
    )
    return outs[0::2], outs[1::2]


def query_body(clips, qkv_ref, wp_ref, qbias_ref, vbias_ref, *refs):
    pooled_refs, wt_ref, wg_ref, q_refs = refs[:clips], refs[clips], refs[clips + 1], refs[clips + 2 :]
    bias = jnp.concatenate(
        [line(qbias_ref), jnp.zeros((1, D_OUT), F32), line(vbias_ref)], axis=1
    )
    bias = jnp.where(iota((EXT - D_IN, 3 * D_OUT), 0) == 0, bias, 0.0).astype(BF)
    turned = jnp.concatenate([qkv_ref[...], bias], axis=0).astype(F32).T
    row, lane = iota((LANES - HEAD_DIM, EXT), 0), iota((LANES - HEAD_DIM, EXT), 1)
    ones = lane == D_IN
    extras = (
        jnp.where(ones & (row == 0), 8.0, 0.0),
        jnp.where(
            (lane == D_IN + 1) & (row == 0),
            -1e30,
            jnp.where(ones & (row >= 1) & (row <= 3), 1.0, 0.0),
        ),
        jnp.where(ones & (row <= 1), 1.0, 0.0),
    )
    for block in range(3 * HEADS):
        rows = turned[HEAD_DIM * block : HEAD_DIM * (block + 1)]
        rows = jnp.concatenate([rows, extras[block // HEADS]], axis=0)
        wt_ref[block, :, :EXT] = rows.astype(BF)
        wt_ref[block, :, EXT:] = jnp.zeros((LANES, 2 * LANES - EXT), BF)
    wg_ref[...] = jnp.concatenate(
        [
            qkv_ref[:, start : start + HEAD_DIM]
            for h in range(HEADS)
            for start in (D_OUT + HEAD_DIM * h, 2 * D_OUT + HEAD_DIM * h)
        ],
        axis=1,
    )
    for block in range(D_OUT // LANES):
        columns = wp_ref[:, LANES * block : LANES * (block + 1)]
        wt_ref[3 * HEADS + block, :, :D_IN] = mm(eye(LANES), columns, 1, 1).astype(BF)
        wt_ref[3 * HEADS + block, :, D_IN:] = jnp.zeros((LANES, 2 * LANES - D_IN), BF)
    weight = wt_ref[:HEADS].reshape(HEADS * LANES, 2 * LANES)
    for c in range(clips):
        pooled = pooled_refs[c][...]
        q = mm(pooled, weight, 1, 1) * (SCALE * LOG2E)
        turned = mm(weight, pooled, 1, 1) * SCALE
        for h in range(HEADS):
            q_refs[2 * c][h] = q[:, LANES * h : LANES * (h + 1)].astype(BF)
            q_refs[2 * c + 1][h] = turned[LANES * h : LANES * h + HEAD_DIM].astype(BF)


def queries_of(qkv, wp, qbias, vbias, pooled):
    clips, count = len(pooled), pooled[0].shape[0]
    wt, wg, *rest = call(
        functools.partial(query_body, clips),
        (1,),
        [whole(v) for v in (qkv, wp, qbias, vbias, *pooled)],
        [
            out_whole((3 * HEADS + D_OUT // LANES, LANES, 2 * LANES), BF),
            out_whole((D_IN, 2 * D_OUT), BF),
            *[
                out_whole((HEADS, count, LANES), BF),
                out_whole((HEADS, HEAD_DIM, count), BF),
            ]
            * clips,
        ],
        name="queries",
        cost=5,
    )
    return wt, wg, [(rest[2 * c], rest[2 * c + 1]) for c in range(clips)]


def forward_body(
    na_ref, nb_ref, wt_ref, qs_ref, p_ref, kt_ref, vt_ref, o_ref, n_ref, keys_ref, asks_ref
):
    rows = na_ref.shape[1]
    queries = qs_ref.shape[1]
    h = pl.program_id(0)
    tall = HEAD_DIM + 16
    most, less = 75.0, 60.0

    def asked(head, high, middle=0.0, low=0.0):
        lane = iota((queries, LANES), 1)
        q = qs_ref[head].astype(F32)
        for k, value in enumerate((high, middle, low)):
            q = jnp.where(lane == HEAD_DIM + 1 + k, -value, q)
        asks_ref[head] = q.astype(BF)

    @pl.when(h == 0)
    def _():
        n_ref[:, :rows] = na_ref[...]
        n_ref[:, rows:] = nb_ref[...]
        weight = wt_ref[HEADS : 2 * HEADS].reshape(HEADS * LANES, 2 * LANES)[:, :EXT]
        keys = mm(weight, n_ref[...], 1, 0)
        worst = jnp.zeros((1, 1), F32)
        for head in range(HEADS):
            own = keys[LANES * head : LANES * (head + 1)]
            keys_ref[head] = own.astype(BF)
            plain = own[:HEAD_DIM]
            longest = jnp.max(jnp.sum(plain * plain, axis=0, keepdims=True), axis=1, keepdims=True)
            q = qs_ref[head].astype(F32)
            q = jnp.where(iota(q.shape, 1) < HEAD_DIM, q, 0.0)
            bound = jnp.sqrt(jnp.sum(q * q, axis=1, keepdims=True) * longest)
            asked(head, bound - less)
            worst = jnp.maximum(worst, jnp.max(bound, axis=0, keepdims=True))

        @pl.when(worst[0, 0] > most)
        def _():
            blocks = 2 * rows // LANES
            rest = slice(blocks * LANES, 2 * rows)

            @pl.loop(0, HEADS)
            def _(head):
                def raised(m, place):
                    scores = mm(qs_ref[head], keys_ref[head, :, place], 1, 0)
                    return jnp.maximum(m, jnp.max(scores, axis=1, keepdims=True))

                def step(i, m):
                    return raised(m, pl.ds(pl.multiple_of(i * LANES, LANES), LANES))

                m = lax.fori_loop(0, blocks, step, jnp.full((queries, 1), -jnp.inf, F32))
                if 2 * rows % LANES:
                    m = raised(m, rest)
                high = m.astype(BF).astype(F32)
                middle = (m - high).astype(BF).astype(F32)
                asked(head, high, middle, m - high - middle)

    row, lane = iota((16, LANES), 0), iota((16, LANES), 1)
    pick = (row == 0) & (lane > HEAD_DIM) & (lane <= HEAD_DIM + 3)
    pick = jnp.where(pick, 1.0, 0.0).astype(BF)
    q = asks_ref[h]
    kt = keys_ref[h]
    kt_ref[0] = kt
    vt = mm(wt_ref[2 * HEADS + h][:, :EXT], n_ref[...], 1, 0).astype(BF)
    vt_ref[0] = vt
    p = jnp.exp2(mm(q, kt, 1, 0)).astype(BF)
    p_ref[0] = p
    o_ref[0, :tall] = mm(vt[:tall], p, 1, 1)
    o_ref[0, tall:] = mm(pick, q, 1, 1)


def forward(na, nb, wt, qs, after=()):
    rows = na.shape[1]
    queries = qs.shape[1]
    return call(
        forward_body,
        (HEADS,),
        [whole(na), whole(nb), whole(wt), whole(qs)],
        [
            out_part((HEADS, queries, 2 * rows), BF),
            out_part((HEADS, LANES, 2 * rows), BF),
            out_part((HEADS, LANES, 2 * rows), BF),
            out_part((HEADS, LANES, queries), F32),
        ],
        [
            pltpu.VMEM((EXT, 2 * rows), BF),
            pltpu.VMEM((HEADS, LANES, 2 * rows), BF),
            pltpu.VMEM((HEADS, queries, LANES), BF),
        ],
        name="attend",
        after=after,
        stays=[True] * 4,
        cost=12,
    )


def middle_body(clips, me_ref, *refs):
    o1_refs, o2_refs, pooled_refs = refs[:clips], refs[clips : 2 * clips], refs[2 * clips : 3 * clips]
    up_ref, bproj_ref, bout_ref, gain_ref, shift_ref, bshrink_ref, bexpand_ref = refs[
        3 * clips : 3 * clips + 7
    ]
    wp_ref, wo_ref, we_ref, ws_ref = refs[3 * clips + 7 : 3 * clips + 11]
    out_ref, hg_ref, do1_ref, do2_ref, do1t_ref, do2t_ref = refs[3 * clips + 11 : 3 * clips + 17]
    shard_refs, wpt_ref = refs[3 * clips + 17 : 3 * clips + 21], refs[3 * clips + 21]
    we_acc, ws_acc, wo_acc, wp_acc, misc_acc = refs[3 * clips + 22 :]
    queries = pooled_refs[0].shape[0]
    rows = [slice(queries * c, queries * (c + 1)) for c in range(clips)]
    heads = [[] for _ in range(clips)]
    factors = [[] for _ in range(clips)]
    for c in range(clips):
        for h in range(HEADS):
            o1, o2 = o1_refs[c][h], o2_refs[c][h]
            l1, l2 = o1[HEAD_DIM : HEAD_DIM + 1], o2[HEAD_DIM : HEAD_DIM + 1]
            m1, m2 = -o1[HEAD_DIM + 16 : HEAD_DIM + 17], -o2[HEAD_DIM + 16 : HEAD_DIM + 17]
            m = jnp.maximum(m1, m2)
            a1, a2 = jnp.exp2(m1 - m), jnp.exp2(m2 - m)
            inverse = 1.0 / (a1 * l1 + a2 * l2)
            c1, c2 = a1 * inverse, a2 * inverse
            heads[c].append(o1[:HEAD_DIM] * c1 + o2[:HEAD_DIM] * c2)
            factors[c].append((c1, c2))
    attended = jnp.concatenate([jnp.concatenate(parts, axis=0).T for parts in heads], axis=0)
    attended = attended.astype(BF)
    pooled = jnp.concatenate([ref[...].astype(F32) for ref in pooled_refs], axis=0).astype(BF)
    up = jnp.concatenate([up_ref[c].astype(F32) for c in range(clips)], axis=0)
    up_low = up.astype(BF)
    hidden = mm(pooled[:, :D_IN], wp_ref[...], 1, 0) + line(bproj_ref)
    hidden = hidden + mm(attended, wo_ref[...], 1, 0) + line(bout_ref)
    center = hidden - jnp.mean(hidden, axis=1, keepdims=True)
    inv_std = lax.rsqrt(jnp.mean(center * center, axis=1, keepdims=True) + 1e-06)
    n = center * inv_std
    gain2 = line(gain_ref)
    second = (n * gain2 + line(shift_ref)).astype(BF)
    out = hidden + line(bshrink_ref)
    second_grad = jnp.zeros(out.shape, F32)
    bexpand = line(bexpand_ref)
    for start in range(0, FF, FF_BLOCK):
        block = slice(start, start + FF_BLOCK)
        before = mm(second, we_ref[:, block], 1, 0) + bexpand[:, block]
        cdf = 0.5 + 0.5 * lax.erf(before * (0.5**0.5))
        active = (before * cdf).astype(BF)
        out = out + mm(active, ws_ref[block, :], 1, 0)
        slope = cdf + before * (jnp.exp(before * before * -0.5) * (0.5 / jnp.pi) ** 0.5)
        before_grad = (mm(up_low, ws_ref[block, :], 1, 1) * slope).astype(BF)
        ws_acc[:, block] = mm(up_low, active, 0, 0)
        we_acc[:, block] = mm(second, before_grad, 0, 0)
        second_grad = second_grad + mm(before_grad, we_ref[:, block], 1, 1)
        misc_acc[0:1, block] = jnp.sum(before_grad.astype(F32), axis=0, keepdims=True)
    for c in range(clips):
        out_ref[c] = out[rows[c]]
    e = gain2 * second_grad
    back = (
        e - jnp.mean(e, axis=1, keepdims=True) - n * jnp.mean(e * n, axis=1, keepdims=True)
    ) * inv_std
    hidden_full = (up + back).astype(BF).astype(F32)
    hidden_grad = hidden_full.astype(BF)
    wo_acc[...] = mm(hidden_grad, attended, 0, 0)
    wp_acc[...] = mm(hidden_grad, pooled, 0, 0)
    misc_acc[1:2, :D_OUT] = jnp.sum(second_grad * n, axis=0, keepdims=True)
    misc_acc[2:3, :D_OUT] = jnp.sum(second_grad, axis=0, keepdims=True)
    misc_acc[3:4, :D_OUT] = jnp.sum(up, axis=0, keepdims=True)
    misc_acc[4:5, :D_OUT] = jnp.sum(hidden_full, axis=0, keepdims=True)
    row = iota((LANES - HEAD_DIM, queries), 0)
    for c in range(clips):
        own_grad = hidden_full[rows[c]].astype(BF)
        hg_ref[c] = own_grad
        attended_grad = mm(wo_ref[...], own_grad, 1, 1).astype(BF).astype(F32)
        for h in range(HEADS):
            own = attended_grad[HEAD_DIM * h : HEAD_DIM * (h + 1)]
            for factor, do_ref, dot_ref in zip(
                factors[c][h], (do1_ref, do2_ref), (do1t_ref, do2t_ref), strict=True
            ):
                scaled = (own * factor).astype(BF)
                dot_ref[c, h] = scaled
                scaled = scaled.astype(F32)
                inner = jnp.sum(scaled * heads[c][h], axis=0, keepdims=True)
                high = inner.astype(BF).astype(F32)
                extra = jnp.where(row == 0, -high, jnp.where(row == 1, high - inner, 0.0))
                do_ref[c, h] = jnp.concatenate([scaled, extra], axis=0).T.astype(BF)
    me = me_ref[0]
    wpt_ref[...] = wp_acc[...]
    for u in range(4):
        for k in range(4):
            misc_acc[8 + u : 9 + u, HEAD_DIM * k : HEAD_DIM * (k + 1)] = misc_acc[
                1 + k : 2 + k, HEAD_DIM * u : HEAD_DIM * (u + 1)
            ]
    for r in range(4):
        u = me ^ r
        ref = shard_refs[r]
        wide = pl.ds(pl.multiple_of(u * 384, LANES), 384)
        tall = pl.ds(pl.multiple_of(u * 96, 8), 96)
        ref[0:384, :] = we_acc[:, wide].astype(BF)
        ref[384:768, :] = ws_acc[:, wide].astype(BF)
        ref[768:864, :] = wo_acc[tall, :].astype(BF)
        wp = wp_acc[tall, :]
        ref[864:912, :] = jnp.concatenate([wp[:48, :D_IN], wp[48:, :D_IN]], axis=1).astype(BF)
        bias = misc_acc[0:1, wide]
        others = misc_acc[pl.ds(8 + u, 1), :384]
        row = iota((48, 384), 0)
        ref[912:960, :] = jnp.where(row == 0, bias, jnp.where(row == 1, others, 0.0)).astype(BF)


def middle(me, o1, o2, pooled, up, vectors, weights):
    clips = len(pooled)
    queries = pooled[0].shape[0]
    grad = (clips, HEADS, queries, LANES)
    grad_t = (clips, HEADS, HEAD_DIM, queries)
    return call(
        functools.partial(middle_body, clips),
        (1,),
        [
            (pl.BlockSpec(memory_space=pltpu.SMEM), me),
            *(whole(value) for value in (*o1, *o2, *pooled, up, *vectors, *weights)),
        ],
        [
            out_whole((clips, queries, D_OUT), F32),
            out_whole((clips, queries, D_OUT), BF),
            out_whole(grad, BF),
            out_whole(grad, BF),
            out_whole(grad_t, BF),
            out_whole(grad_t, BF),
            *([out_whole((960, 384), BF)] * 4),
            out_whole((D_OUT, 2 * LANES), F32),
        ],
        [
            pltpu.VMEM((D_OUT, FF), F32),
            pltpu.VMEM((D_OUT, FF), F32),
            pltpu.VMEM((D_OUT, D_OUT), F32),
            pltpu.VMEM((D_OUT, 2 * LANES), F32),
            pltpu.VMEM((16, FF), F32),
        ],
        name="middle",
        stays=[True] * 11,
        cost=16,
    )


def backward_body(
    na_ref,
    nb_ref,
    wg_ref,
    p_ref,
    kt_ref,
    vt_ref,
    do_ref,
    dot_ref,
    qt_ref,
    dq_ref,
    dw_ref,
    ga_ref,
    gb_ref,
    n_ref,
    both_ref,
):
    rows = na_ref.shape[1]
    h = pl.program_id(0)
    p = p_ref[0]
    ds = p * mm(do_ref[0], vt_ref[0], 1, 0).astype(BF)
    dq_ref[0] = mm(kt_ref[0, :HEAD_DIM], ds, 1, 1)
    both_ref[h, :HEAD_DIM] = mm(qt_ref[0], ds, 1, 0).astype(BF)
    both_ref[h, HEAD_DIM:] = mm(dot_ref[0], p, 1, 0).astype(BF)

    @pl.when(h == HEADS - 1)
    def _():
        n_ref[:, :rows] = na_ref[...]
        n_ref[:, rows:] = nb_ref[...]
        both = both_ref[...].reshape(2 * D_OUT, 2 * rows)
        dw_ref[...] = mm(both, n_ref[...], 1, 1)
        g = mm(wg_ref[...], both, 1, 0).astype(BF)
        ga_ref[...] = g[:, :rows]
        gb_ref[...] = g[:, rows:]


def backward(clip, na, nb, wg, p, kt, vt, do, dot, qt, after=()):
    rows = na.shape[1]
    queries = qt.shape[2]
    return call(
        backward_body,
        (HEADS,),
        [
            whole(na),
            whole(nb),
            whole(wg),
            part(p),
            part(kt),
            part(vt),
            at_head(do, clip),
            at_head(dot, clip),
            part(qt),
        ],
        [
            out_part((HEADS, HEAD_DIM, queries), F32),
            out_whole((2 * D_OUT, EXT), F32),
            out_whole((D_IN, rows), BF),
            out_whole((D_IN, rows), BF),
        ],
        [pltpu.VMEM((EXT, 2 * rows), BF), pltpu.VMEM((HEADS, 2 * HEAD_DIM, 2 * rows), BF)],
        name="attend_back",
        after=after,
        cost=17,
    )


def gather_body(clips, me_ref, *refs):
    dq_refs, dw_refs, pooled_refs = (
        refs[: 2 * clips],
        refs[2 * clips : 4 * clips],
        refs[4 * clips : 5 * clips],
    )
    wt_ref, wpt_ref, gain_ref, shift_ref = refs[5 * clips : 5 * clips + 4]
    shard_refs, (dw_acc, line_ref, shard_ref) = refs[5 * clips + 4 : 5 * clips + 8], refs[5 * clips + 8 :]
    total = dw_refs[0][...]
    for ref in dw_refs[1:]:
        total = total + ref[...]
    for h in range(HEADS):
        at = 2 * HEAD_DIM * h
        dw_acc[HEADS + h] = total[at : at + HEAD_DIM]
        dw_acc[2 * HEADS + h] = total[at + HEAD_DIM : at + 2 * HEAD_DIM]
    dw = None
    for c in range(clips):
        dq = (dq_refs[2 * c][...] + dq_refs[2 * c + 1][...]) * SCALE
        dq = dq.reshape(D_OUT, dq.shape[2]).astype(BF)
        term = mm(dq, pooled_refs[c][...], 1, 0)
        dw = term if dw is None else dw + term
    for h in range(HEADS):
        dw_acc[h] = dw[HEAD_DIM * h : HEAD_DIM * (h + 1), :EXT]
    gain_sum = jnp.zeros((1, D_IN), F32)
    shift_sum = jnp.zeros((1, D_IN), F32)
    wp = wt_ref[3 * HEADS :].reshape(D_OUT, 2 * LANES)[:, :D_IN]
    terms = [(wt_ref[b][:HEAD_DIM, :D_IN], dw_acc[b]) for b in range(3 * HEADS)]
    for w, dw in [*terms, (wp, wpt_ref[...])]:
        w = w.astype(F32)
        gain_sum = gain_sum + jnp.sum(w * dw[:, :D_IN], axis=0, keepdims=True)
        shift_sum = shift_sum + jnp.sum(w * dw[:, D_IN : D_IN + 1], axis=0, keepdims=True)
    gain_sum = (gain_sum - line(shift_ref) * shift_sum) / line(gain_ref)
    for at, first in ((0, 0), (1, 2 * HEADS)):
        for h in range(HEADS):
            sums = dw_acc[first + h][:, LANES:]
            sums = jnp.concatenate(
                [sums, jnp.zeros((HEAD_DIM, 2 * LANES - EXT), F32)], axis=1
            )
            sums = jnp.concatenate([sums, jnp.zeros((LANES - HEAD_DIM, LANES), F32)], axis=0).T
            line_ref[at : at + 1, HEAD_DIM * h : HEAD_DIM * (h + 1)] = sums[
                D_IN - LANES : D_IN - LANES + 1, :HEAD_DIM
            ]
    line_ref[2:3, :D_IN] = gain_sum
    line_ref[3:4, :D_IN] = shift_sum
    for u in range(4):
        at = 0
        for source, size in ((0, 96), (1, 96), (2, 48), (3, 48)):
            shard_ref[u : u + 1, at : at + size] = line_ref[
                source : source + 1, size * u : size * (u + 1)
            ]
            at += size
        shard_ref[u : u + 1, at:] = jnp.zeros((1, D_OUT - at), F32)
    for r in range(4):
        u = me_ref[0] ^ r
        ref = shard_refs[r]
        rows = jnp.concatenate([dw_acc[3 * u + i][:, :D_IN] for i in range(3)], axis=0)
        ref[:144, :] = jnp.concatenate([rows[:144], rows[144:]], axis=1).astype(BF)
        ref[144:, :] = jnp.where(
            iota((16, D_OUT), 0) == 0, shard_ref[pl.ds(u, 1), :], 0.0
        ).astype(BF)


def gather(me, dq, dw, pooled, wt, wpt, gain, shift, after=()):
    clips = len(pooled)
    return call(
        functools.partial(gather_body, clips),
        (1,),
        [
            (pl.BlockSpec(memory_space=pltpu.SMEM), me),
            *(whole(v) for v in (*dq, *dw, *pooled, wt, wpt, gain, shift)),
        ],
        [out_whole((160, D_OUT), BF)] * 4,
        [
            pltpu.VMEM((3 * HEADS, HEAD_DIM, EXT), F32),
            pltpu.VMEM((8, D_OUT), F32),
            pltpu.VMEM((8, D_OUT), F32),
        ],
        name="gather",
        after=after,
        cost=6,
    )


def final_body(terms, tok_ref, hg_ref, wp_ref, qkv_ref, gain_ref, dq1_ref, dq2_ref, *refs):
    part_refs, out_ref = refs[:terms], refs[-1]
    slots, _, units = tok_ref.shape[1:]
    gain = column(gain_ref)
    dq = ((dq1_ref[...] + dq2_ref[...]) * SCALE).reshape(D_OUT, 4 * units).astype(BF)
    spread = mm(wp_ref[...], hg_ref[0], 1, 1) + mm(qkv_ref[:, :D_OUT], dq, 1, 0)
    spread = spread * 0.25
    places = [slice(units * s, units * (s + 1)) for s in range(slots)]
    spread = [spread[:, places[2 * (s >> 3) + ((s >> 1) & 1)]] for s in range(slots)]
    grad = total_of(part_refs) + jnp.concatenate(spread, axis=1)
    x = jnp.concatenate([tok_ref[0, s].astype(F32) for s in range(slots)], axis=1)
    center = x - jnp.mean(x, axis=0, keepdims=True)
    inv_std = lax.rsqrt(jnp.mean(center * center, axis=0, keepdims=True) + 1e-06)
    n = center * inv_std
    e = grad * gain
    back = e - jnp.mean(e, axis=0, keepdims=True) - n * jnp.mean(e * n, axis=0, keepdims=True)
    back = back * inv_std
    for s in range(slots):
        out_ref[0, s] = back[:, places[s]]


def final(clip, tokens, hg, dq, wp, qkv, gain, parts, filled, after=()):
    terms = len(parts)
    return call(
        functools.partial(final_body, terms),
        (1,),
        [
            at_clip(tokens, clip),
            at_clip(hg, clip),
            *(whole(v) for v in (wp, qkv, gain, *dq, *parts)),
            *([] if filled is None else [(pl.BlockSpec(memory_space=pl.ANY), filled)]),
        ],
        [(at_clip(tokens, clip)[0], tokens.shape, F32)],
        name="final",
        stays=[True],
        cost=6,
        after=after,
        aliases=None if filled is None else {7 + terms: 0},
    )[0]


def unpack_first_body(
    place_ref,
    value_ref,
    other_ref,
    proj_ref,
    bproj_ref,
    wo_ref,
    bout_ref,
    gain_ref,
    shift_ref,
    we_ref,
    be_ref,
    ws_ref,
    bs_ref,
    rows_ref,
):
    half = value_ref.shape[0]
    at = pl.multiple_of(place_ref[0] * half, 8)
    rows_ref[pl.ds(at, half), :] = value_ref[...].astype(F32)
    rows_ref[pl.ds(pl.multiple_of(half - at, 8), half), :] = other_ref[...].astype(F32)
    we_ref[...] = rows_ref[:384]
    ws_ref[...] = rows_ref[384:768].T
    wo_ref[...] = rows_ref[768:864]
    proj = jnp.concatenate([rows_ref[864:912, :D_IN], rows_ref[864:912, D_IN:]], axis=0)
    proj_ref[...] = proj.T
    lines = rows_ref[912:920]
    be_ref[...] = lines[0:1].reshape(384)
    for ref, k in ((gain_ref, 0), (shift_ref, 1), (bs_ref, 2), (bout_ref, 3), (bproj_ref, 3)):
        ref[...] = lines[1:2, 96 * k : 96 * (k + 1)].reshape(96)


def unpack_first(place, value, other, after=()):
    shapes = [(192, 96), (96,), (96, 384), (96,), (96,), (96,), (384, 384), (384,), (384, 384), (96,)]
    return call(
        unpack_first_body,
        (1,),
        [(pl.BlockSpec(memory_space=pltpu.SMEM), place), whole(value), whole(other)],
        [out_whole(shape, F32) for shape in shapes],
        [pltpu.VMEM((2 * value.shape[0], D_OUT), F32)],
        name="unpack_first",
        stays=[True] * len(shapes),
        after=after,
        cost=2,
    )


def unpack_second_body(a_ref, b_ref, qkv_ref, bq_ref, bv_ref, gain_ref, shift_ref):
    total = a_ref[...].astype(F32) + b_ref[...].astype(F32)
    qkv_ref[...] = jnp.concatenate([total[:144, :D_IN], total[:144, D_IN:]], axis=0).T
    at = 0
    for ref in (bq_ref, bv_ref, gain_ref, shift_ref):
        size = ref.shape[0]
        ref[...] = total[144:145, at : at + size].reshape(size)
        at += size


def unpack_second(a, b):
    shapes = [(192, 288), (96,), (96,), (48,), (48,)]
    return call(
        unpack_second_body,
        (1,),
        [whole(a), whole(b)],
        [out_whole(shape, F32) for shape in shapes],
        name="unpack_second",
        stays=[True] * len(shapes),
        cost=1,
    )


def swap_unit(value, bit):
    return lax.ppermute(value, "unit", [(i, i ^ bit) for i in range(4)])


def swap_clip(value, bit):
    size = lax.axis_size("clip")
    return lax.ppermute(value, "clip", [(i, i ^ bit) for i in range(size)])


def add(*values):
    return functools.reduce(lambda a, b: a + b, [v.astype(F32) for v in values]).astype(BF)


def member():
    at = lax.axis_index("clip").astype(jnp.int32)
    return jnp.stack([at & 1, (at >> 1) & 1])


def total_of(refs):
    return functools.reduce(lambda a, b: a + b, [ref[...].astype(F32) for ref in refs])


def between(sums, place, cut=None, grads=None, join=None):
    rows, width = sums[0].shape
    count, more = len(sums), grads or []
    pieces = 1 if cut is None else 2
    tall = 2 * rows if join is not None else rows // pieces

    def body(place_ref, *refs):
        terms, refs = refs[:count], refs[count:]
        others, refs = refs[: len(more)], refs[len(more) :]
        outs, scratch = refs[:-1], refs[-1]
        if more:
            outs[-1][...] = total_of(others).astype(BF)
        if join is not None:
            for d in range(2):
                at = pl.multiple_of((place_ref[join] ^ d) * rows, 8)
                scratch[pl.ds(at, rows), :] = terms[d][...].astype(F32)
            outs[0][...] = scratch[...].astype(BF)
        elif cut is None:
            outs[0][...] = total_of(terms).astype(BF)
        else:
            scratch[...] = total_of(terms)
            for d in range(2):
                at = pl.multiple_of((place_ref[cut] ^ d) * tall, 8)
                outs[d][...] = scratch[pl.ds(at, tall), :].astype(BF)

    return list(
        call(
            body,
            (1,),
            [(pl.BlockSpec(memory_space=pltpu.SMEM), place), *(whole(v) for v in (*sums, *more))],
            [
                *([out_whole((tall, width), BF)] * pieces),
                *([out_whole(more[0].shape, BF)] if more else []),
            ],
            [pltpu.VMEM((max(rows, tall), width), F32)],
            name="between",
            cost=2,
        )
    )


def in_hbm(*values):
    return [pltpu.with_memory_space_constraint(v, pltpu.HBM) for v in values]


def together(*values):
    return lax.optimization_barrier(values)


def shards(
    tokens,
    first_gain,
    first_shift,
    proj_weight,
    proj_bias,
    qkv_weight,
    query_bias,
    value_bias,
    output_weight,
    output_bias,
    second_gain,
    second_shift,
    expand_weight,
    expand_bias,
    shrink_weight,
    shrink_bias,
    frame_counts,
    unit_frames,
    cotangent,
):
    clips, units = tokens.shape[:2]
    me = lax.axis_index("unit").astype(jnp.int32).reshape(1)
    vectors = [proj_bias, output_bias, second_gain, second_shift, shrink_bias, expand_bias]
    flat = tokens.transpose(0, 2, 3, 1)
    upstream = cotangent.transpose(0, 2, 1, 3).reshape(clips, 4 * units, D_OUT)
    normed, pooled = normed_tokens(flat, unit_frames, frame_counts, first_gain, first_shift)
    near, across = [(n, swap_unit(n, 1)) for n in normed], []
    wt, wg, query = queries_of(qkv_weight, proj_weight, query_bias, value_bias, pooled)
    own, rest, far = [], [], []
    for c in range(clips):
        across.append(swap_unit(together(near[c][0], near[0][1])[0] if c else near[c][0], 2))
        weights = [wt, query[c][0]] if c else in_hbm(wt, query[c][0])
        keys = near[c] if c else in_hbm(*near[c])
        own.append(forward(*keys, *weights, after=in_hbm(*(v[3] for v in own[-1:]))))
    for c in range(clips):
        held, _ = together(across[c], own[c][3])
        far.append((held, swap_unit(held, 1)))
        rest.append(forward(*far[c], wt, query[c][0], after=in_hbm(*(v[3] for v in (own + rest)[-1:]))))
    out, hg, do1, do2, do1t, do2t, keep, send0, across, send1, wpt = middle(
        me,
        in_hbm(*(value[3] for value in own)),
        in_hbm(*(value[3] for value in rest)),
        pooled,
        upstream,
        vectors,
        [proj_weight, output_weight, expand_weight, shrink_weight],
    )
    dq, dw = [[None, None] for _ in range(clips)], [[None, None] for _ in range(clips)]
    place = member()
    got = [swap_unit(send0, 1), swap_unit(send1, 1)]
    out = out.reshape(clips, 4, units, D_OUT).transpose(0, 2, 1, 3)
    got, out = together(got, out)
    (value,) = between([across, got[1]], place)
    terms = [keep, got[0]]
    calls = [(c, 1) for c in range(clips)] + [(c, 0) for c in range(clips)]
    parts = [[None] * 3 for _ in range(clips)]
    lent, owed = [], []
    moves = ["unit", 1, 2, 4]
    bits = []
    bit = 8
    while bit < lax.axis_size("clip"):
        bits.append(bit)
        bit *= 2
    held = [value]
    for at, (c, side) in enumerate(calls):
        keys, kept, grads = (far, rest, (do2, do2t)) if side else (near, own, (do1, do1t))
        move = moves[at]
        sent = [swap_unit(value, 2) if move == "unit" else swap_clip(value, move)]
        travel = [swap_unit(parts[b][0], 2) for b in lent]
        travel += [swap_unit(gb, 1) for _, gb in owed]
        result = backward(c, *keys[c], wg, *kept[c][:3], *grads, query[c][1], after=held)
        *result, travel, sent = together(*result, travel, sent)
        dq[c][side], dw[c][side], ga, gb = result
        for b in lent:
            parts[b][0] = travel.pop(0)
        lent, loose = [], None
        for ((b, other), _), arrived in zip(owed, travel, strict=True):
            if other:
                loose = [parts[b][0], arrived]
                lent.append(b)
            else:
                parts[b][2] = arrived
        cut = {"unit": 0, 1: 1}.get(move)
        result = between([*terms, *sent], place, cut, loose)
        if loose:
            parts[lent[0]][0] = result.pop()
        if cut is None:
            (value,), terms = result, result
        else:
            terms, value = result[:1], result[1]
        if move == 2:
            for bit in bits:
                value = add(value, swap_clip(value, bit))
            terms = [value]
        owed = [((c, side), gb)]
        parts[c][0 if side else 1] = ga
        held = [dq[c][side], value, *terms, *(parts[b][0] for b in lent)]
    half = swap_clip(value, 2)
    travel = [swap_unit(gb, 1) for _, gb in owed]
    result = gather(
        me,
        [v for pair in dq for v in pair],
        [v for pair in dw for v in pair],
        pooled,
        wt,
        wpt,
        first_gain,
        first_shift,
        after=held,
    )
    (keep, send0, across, send1), travel = together(result, travel)
    for ((b, _), _), arrived in zip(owed, travel, strict=True):
        parts[b][2] = arrived
    got = [swap_unit(send0, 1), swap_unit(send1, 1)]
    second = add(across, got[1])
    input_grad, firsts = None, None
    bit = 0
    for c in range(max(clips, 3)):
        sent = swap_clip(second, bit) if bit else swap_unit(second, 2)
        if c < clips:
            input_grad = final(
                c, flat, hg, dq[c], proj_weight, qkv_weight, first_gain, parts[c], input_grad, after=[second]
            )
            if c == 0:
                sent, input_grad, half = together(sent, input_grad, half)
                (value,) = between([value, half], place, join=1)
                other = swap_clip(value, 1)
            else:
                sent, input_grad = together(sent, input_grad)
        if c < 3:
            second = add(second, sent) if bit else add(keep, got[0], sent)
            bit = 2 * bit if bit else 1
    last = swap_clip(second, 4)
    firsts = unpack_first(place, value, other, after=[second])
    last, firsts = together(last, firsts)
    for more in bits:
        second, last = add(second, last), None
        last = swap_clip(second, more)
    wp_grad, bp_grad, wo_grad, bo_grad, g2_grad, s2_grad, we_grad, be_grad, ws_grad, bs_grad = firsts
    qkv_grad, bq_grad, bv_grad, g1_grad, s1_grad = unpack_second(second, last)
    return (
        out,
        input_grad.transpose(0, 3, 1, 2),
        g1_grad,
        s1_grad,
        wp_grad,
        bp_grad,
        qkv_grad,
        bq_grad,
        bv_grad,
        wo_grad.T,
        bo_grad,
        g2_grad,
        s2_grad,
        we_grad,
        be_grad,
        ws_grad,
        bs_grad,
    )


def solution(mesh):
    every = P()
    split = P("clip", "unit", None, None)
    return jax.shard_map(
        shards,
        mesh=mesh,
        in_specs=(split,) + (every,) * 15 + (P("clip"), P("clip", "unit"), split),
        out_specs=(
            split,
            split,
            P("unit"),
            P("unit"),
            P(None, "unit"),
            P("unit"),
            P(None, "unit"),
            P("unit"),
            P("unit"),
            P(None, "unit"),
            P("unit"),
            P("unit"),
            P("unit"),
            P(None, "unit"),
            P("unit"),
            P("unit", None),
            P("unit"),
        ),
        check_vma=False,
    )
```

```python
import functools

import jax
import jax.numpy as jnp
from jax import lax
from jax.experimental import pallas as pl
from jax.experimental.pallas import tpu as pltpu
from jax.sharding import PartitionSpec as P

D_IN = 192
D_OUT = 384
HEADS = 4
HEAD_DIM = 96
FF = 1536
LANES = 128
EXT = 208
SCALE = HEAD_DIM**-0.5
LOG2E = 1.4426950408889634
BF = jnp.bfloat16
F32 = jnp.float32
VMEM_MIB = 46
VMEM_MIB_FIRST = 64
FF_BLOCK = 768


def mm(a, b, ca, cb):
    return lax.dot_general(a, b, (((ca,), (cb,)), ((), ())), preferred_element_type=F32)


def iota(shape, dim):
    return lax.broadcasted_iota(jnp.int32, shape, dim)


def call(body, grid, ins, outs, scratch=(), name=None, cost=None, after=(), aliases=None, stays=None):
    count = len(ins)
    stays = stays or [False] * len(outs)

    def run(*refs):
        body(*refs[:count], *refs[count + len(after) :])

    ins = [*ins, *((pl.BlockSpec(memory_space=pl.ANY), value) for value in after)]
    return pl.pallas_call(
        run,
        grid=grid,
        in_specs=[spec for spec, _ in ins],
        out_specs=[spec for spec, _, _ in outs],
        out_shape=[
            (pltpu.HBM if stay else jax.ShapeDtypeStruct)(shape, dtype)
            for stay, (_, shape, dtype) in zip(stays, outs, strict=True)
        ],
        scratch_shapes=list(scratch),
        compiler_params=pltpu.CompilerParams(
            dimension_semantics=("arbitrary",) * len(grid), vmem_limit_bytes=(VMEM_MIB_FIRST if name in ("normed", "queries") else VMEM_MIB) * 2**20
        ),
        name=name,
        cost_estimate=pl.CostEstimate(
            flops=int(cost * 1.1e9), bytes_accessed=int(cost * 1e6), transcendentals=0
        ),
        input_output_aliases=aliases or {},
    )(*[value for _, value in ins])


def whole(value):
    rank = len(value.shape)
    return (pl.BlockSpec(value.shape, lambda *_: (0,) * rank), value)


def part(value):
    rank = len(value.shape)
    return (pl.BlockSpec((1,) + value.shape[1:], lambda i: (i,) + (0,) * (rank - 1)), value)


def at_clip(value, clip):
    rank = len(value.shape)
    return (pl.BlockSpec((1,) + value.shape[1:], lambda *_: (clip,) + (0,) * (rank - 1)), value)


def at_head(value, clip):
    rank = len(value.shape)
    return (
        pl.BlockSpec((None, 1) + value.shape[2:], lambda i: (clip, i) + (0,) * (rank - 2)),
        value,
    )


def out_part(shape, dtype):
    rank = len(shape)
    return (pl.BlockSpec((1,) + shape[1:], lambda i: (i,) + (0,) * (rank - 1)), shape, dtype)


def out_whole(shape, dtype):
    rank = len(shape)
    return (pl.BlockSpec(shape, lambda *_: (0,) * rank), shape, dtype)


def line(ref):
    return ref[...].astype(F32).reshape(1, -1)


def eye(size):
    return jnp.where(iota((size, size), 0) == iota((size, size), 1), 1.0, 0.0).astype(BF)


def column(ref):
    size = ref.shape[0]
    values = jnp.broadcast_to(line(ref), (16, size)).astype(BF)
    return mm(eye(size), values, 1, 1)[:, 0:1]


def normed_body(clips, tok_ref, frames_ref, counts_ref, gain_ref, shift_ref, *outs):
    slots, _, units = tok_ref.shape[1:]
    clip = pl.program_id(0)
    gain, shift = column(gain_ref), column(shift_ref)
    x = jnp.concatenate([tok_ref[0, s] for s in range(slots)], axis=1).astype(F32)
    center = x - jnp.mean(x, axis=0, keepdims=True)
    var = jnp.mean(center * center, axis=0, keepdims=True)
    normed = (center * lax.rsqrt(var + 1e-06) * gain + shift).astype(BF)
    extra = iota((EXT - D_IN, units), 0)
    invalid = jnp.where(frames_ref[pl.ds(clip, 1), :] >= counts_ref[clip], 1.0, 0.0)
    extra = jnp.where(extra == 0, 1.0, jnp.where(extra == 1, invalid, 0.0))
    extra = jnp.concatenate([extra] * slots, axis=1).astype(BF)
    pieces = [normed[:, units * s : units * (s + 1)].astype(F32) for s in range(slots)]
    means = []
    for p in range(4):
        first = 8 * (p >> 1) + 2 * (p & 1)
        means.append(
            (pieces[first] + pieces[first + 1] + pieces[first + 4] + pieces[first + 5]) * 0.25
        )
    pooled = jnp.concatenate(means, axis=1)
    row = iota((2 * LANES - D_IN, 4 * units), 0)
    pooled = jnp.concatenate([pooled, jnp.where(row == 0, 1.0, 0.0)], axis=0).T.astype(BF)
    for c in range(clips):

        @pl.when(clip == c)
        def _():
            outs[2 * c][:D_IN, :] = normed
            outs[2 * c][D_IN:, :] = extra
            outs[2 * c + 1][...] = pooled


def normed_tokens(tokens, frames, counts, gain, shift):
    clips, slots, _, units = tokens.shape
    outs = call(
        functools.partial(normed_body, clips),
        (clips,),
        [
            part(tokens),
            whole(frames),
            (pl.BlockSpec(memory_space=pltpu.SMEM), counts),
            whole(gain),
            whole(shift),
        ],
        [out_whole((EXT, slots * units), BF), out_whole((4 * units, 2 * LANES), BF)] * clips,
        name="normed",
        cost=5,
    )
    return outs[0::2], outs[1::2]


def query_body(clips, qkv_ref, wp_ref, qbias_ref, vbias_ref, *refs):
    pooled_refs, wt_ref, wg_ref, q_refs = refs[:clips], refs[clips], refs[clips + 1], refs[clips + 2 :]
    bias = jnp.concatenate(
        [line(qbias_ref), jnp.zeros((1, D_OUT), F32), line(vbias_ref)], axis=1
    )
    bias = jnp.where(iota((EXT - D_IN, 3 * D_OUT), 0) == 0, bias, 0.0).astype(BF)
    turned = jnp.concatenate([qkv_ref[...], bias], axis=0).astype(F32).T
    row, lane = iota((LANES - HEAD_DIM, EXT), 0), iota((LANES - HEAD_DIM, EXT), 1)
    ones = lane == D_IN
    extras = (
        jnp.where(ones & (row == 0), 8.0, 0.0),
        jnp.where(
            (lane == D_IN + 1) & (row == 0),
            -1e30,
            jnp.where(ones & (row >= 1) & (row <= 3), 1.0, 0.0),
        ),
        jnp.where(ones & (row <= 1), 1.0, 0.0),
    )
    for block in range(3 * HEADS):
        rows = turned[HEAD_DIM * block : HEAD_DIM * (block + 1)]
        rows = jnp.concatenate([rows, extras[block // HEADS]], axis=0)
        wt_ref[block, :, :EXT] = rows.astype(BF)
        wt_ref[block, :, EXT:] = jnp.zeros((LANES, 2 * LANES - EXT), BF)
    wg_ref[...] = jnp.concatenate(
        [
            qkv_ref[:, start : start + HEAD_DIM]
            for h in range(HEADS)
            for start in (D_OUT + HEAD_DIM * h, 2 * D_OUT + HEAD_DIM * h)
        ],
        axis=1,
    )
    for block in range(D_OUT // LANES):
        columns = wp_ref[:, LANES * block : LANES * (block + 1)]
        wt_ref[3 * HEADS + block, :, :D_IN] = mm(eye(LANES), columns, 1, 1).astype(BF)
        wt_ref[3 * HEADS + block, :, D_IN:] = jnp.zeros((LANES, 2 * LANES - D_IN), BF)
    weight = wt_ref[:HEADS].reshape(HEADS * LANES, 2 * LANES)
    for c in range(clips):
        pooled = pooled_refs[c][...]
        q = mm(pooled, weight, 1, 1) * (SCALE * LOG2E)
        turned = mm(weight, pooled, 1, 1) * SCALE
        for h in range(HEADS):
            q_refs[2 * c][h] = q[:, LANES * h : LANES * (h + 1)].astype(BF)
            q_refs[2 * c + 1][h] = turned[LANES * h : LANES * h + HEAD_DIM].astype(BF)


def queries_of(qkv, wp, qbias, vbias, pooled):
    clips, count = len(pooled), pooled[0].shape[0]
    wt, wg, *rest = call(
        functools.partial(query_body, clips),
        (1,),
        [whole(v) for v in (qkv, wp, qbias, vbias, *pooled)],
        [
            out_whole((3 * HEADS + D_OUT // LANES, LANES, 2 * LANES), BF),
            out_whole((D_IN, 2 * D_OUT), BF),
            *[
                out_whole((HEADS, count, LANES), BF),
                out_whole((HEADS, HEAD_DIM, count), BF),
            ]
            * clips,
        ],
        name="queries",
        cost=5,
    )
    return wt, wg, [(rest[2 * c], rest[2 * c + 1]) for c in range(clips)]


def forward_body(
    na_ref, nb_ref, wt_ref, qs_ref, p_ref, kt_ref, vt_ref, o_ref, n_ref, keys_ref, values_ref, asks_ref, sem
):
    rows = na_ref.shape[1]
    queries = qs_ref.shape[1]
    h = pl.program_id(0)
    tall = HEAD_DIM + 16
    most, less = 75.0, 60.0
    keys_out = pltpu.make_async_copy(keys_ref, kt_ref, sem.at[0])
    values_out = pltpu.make_async_copy(values_ref, vt_ref, sem.at[1])

    def asked(head, high, middle=0.0, low=0.0):
        lane = iota((queries, LANES), 1)
        q = qs_ref[head].astype(F32)
        for k, value in enumerate((high, middle, low)):
            q = jnp.where(lane == HEAD_DIM + 1 + k, -value, q)
        asks_ref[head] = q.astype(BF)

    @pl.when(h == 0)
    def _():
        n_ref[:, :rows] = na_ref[...]
        n_ref[:, rows:] = nb_ref[...]
        weight = wt_ref[HEADS : 2 * HEADS].reshape(HEADS * LANES, 2 * LANES)[:, :EXT]
        keys = mm(weight, n_ref[...], 1, 0)
        worst = jnp.zeros((1, 1), F32)
        for head in range(HEADS):
            own = keys[LANES * head : LANES * (head + 1)]
            keys_ref[head] = own.astype(BF)
            plain = own[:HEAD_DIM]
            longest = jnp.max(jnp.sum(plain * plain, axis=0, keepdims=True), axis=1, keepdims=True)
            q = qs_ref[head].astype(F32)
            q = jnp.where(iota(q.shape, 1) < HEAD_DIM, q, 0.0)
            bound = jnp.sqrt(jnp.sum(q * q, axis=1, keepdims=True) * longest)
            asked(head, bound - less)
            worst = jnp.maximum(worst, jnp.max(bound, axis=0, keepdims=True))
        keys_out.start()
        weight = wt_ref[2 * HEADS : 3 * HEADS].reshape(HEADS * LANES, 2 * LANES)[:, :EXT]
        values = mm(weight, n_ref[...], 1, 0).astype(BF)
        values_ref[...] = values.reshape(HEADS, LANES, 2 * rows)
        values_out.start()

        @pl.when(worst[0, 0] > most)
        def _():
            blocks = 2 * rows // LANES
            rest = slice(blocks * LANES, 2 * rows)

            @pl.loop(0, HEADS)
            def _(head):
                def raised(m, place):
                    scores = mm(qs_ref[head], keys_ref[head, :, place], 1, 0)
                    return jnp.maximum(m, jnp.max(scores, axis=1, keepdims=True))

                def step(i, m):
                    return raised(m, pl.ds(pl.multiple_of(i * LANES, LANES), LANES))

                m = lax.fori_loop(0, blocks, step, jnp.full((queries, 1), -jnp.inf, F32))
                if 2 * rows % LANES:
                    m = raised(m, rest)
                high = m.astype(BF).astype(F32)
                middle = (m - high).astype(BF).astype(F32)
                asked(head, high, middle, m - high - middle)

    @pl.when(h == HEADS - 1)
    def _():
        keys_out.wait()
        values_out.wait()

    row, lane = iota((16, LANES), 0), iota((16, LANES), 1)
    pick = (row == 0) & (lane > HEAD_DIM) & (lane <= HEAD_DIM + 3)
    pick = jnp.where(pick, 1.0, 0.0).astype(BF)
    q = asks_ref[h]
    p = jnp.exp2(mm(q, keys_ref[h], 1, 0)).astype(BF)
    p_ref[0] = p
    o_ref[0, :tall] = mm(values_ref[h, :tall], p, 1, 1)
    o_ref[0, tall:] = mm(pick, q, 1, 1)


def forward(na, nb, wt, qs, after=()):
    rows = na.shape[1]
    queries = qs.shape[1]
    return call(
        forward_body,
        (HEADS,),
        [whole(na), whole(nb), whole(wt), whole(qs)],
        [
            out_part((HEADS, queries, 2 * rows), BF),
            (pl.BlockSpec(memory_space=pl.ANY), (HEADS, LANES, 2 * rows), BF),
            (pl.BlockSpec(memory_space=pl.ANY), (HEADS, LANES, 2 * rows), BF),
            out_part((HEADS, LANES, queries), F32),
        ],
        [
            pltpu.VMEM((EXT, 2 * rows), BF),
            pltpu.VMEM((HEADS, LANES, 2 * rows), BF),
            pltpu.VMEM((HEADS, LANES, 2 * rows), BF),
            pltpu.VMEM((HEADS, queries, LANES), BF),
            pltpu.SemaphoreType.DMA((2,)),
        ],
        name="attend",
        after=after,
        stays=[True] * 4,
        cost=12,
    )


def middle_body(clips, me_ref, *refs):
    o1_refs, o2_refs, pooled_refs = refs[:clips], refs[clips : 2 * clips], refs[2 * clips : 3 * clips]
    up_ref, bproj_ref, bout_ref, gain_ref, shift_ref, bshrink_ref, bexpand_ref = refs[
        3 * clips : 3 * clips + 7
    ]
    wp_ref, wo_ref, we_ref, ws_ref = refs[3 * clips + 7 : 3 * clips + 11]
    out_ref, hg_ref, do1_ref, do2_ref, do1t_ref, do2t_ref = refs[3 * clips + 11 : 3 * clips + 17]
    shard_refs, wpt_ref = refs[3 * clips + 17 : 3 * clips + 21], refs[3 * clips + 21]
    we_acc, ws_acc, wo_acc, wp_acc, misc_acc = refs[3 * clips + 22 :]
    queries = pooled_refs[0].shape[0]
    rows = [slice(queries * c, queries * (c + 1)) for c in range(clips)]
    heads = [[] for _ in range(clips)]
    factors = [[] for _ in range(clips)]
    for c in range(clips):
        for h in range(HEADS):
            o1, o2 = o1_refs[c][h], o2_refs[c][h]
            l1, l2 = o1[HEAD_DIM : HEAD_DIM + 1], o2[HEAD_DIM : HEAD_DIM + 1]
            m1, m2 = -o1[HEAD_DIM + 16 : HEAD_DIM + 17], -o2[HEAD_DIM + 16 : HEAD_DIM + 17]
            m = jnp.maximum(m1, m2)
            a1, a2 = jnp.exp2(m1 - m), jnp.exp2(m2 - m)
            inverse = 1.0 / (a1 * l1 + a2 * l2)
            c1, c2 = a1 * inverse, a2 * inverse
            heads[c].append(o1[:HEAD_DIM] * c1 + o2[:HEAD_DIM] * c2)
            factors[c].append((c1, c2))
    attended = jnp.concatenate([jnp.concatenate(parts, axis=0).T for parts in heads], axis=0)
    attended = attended.astype(BF)
    pooled = jnp.concatenate([ref[...].astype(F32) for ref in pooled_refs], axis=0).astype(BF)
    up = jnp.concatenate([up_ref[c].astype(F32) for c in range(clips)], axis=0)
    up_low = up.astype(BF)
    hidden = mm(pooled[:, :D_IN], wp_ref[...], 1, 0) + line(bproj_ref)
    hidden = hidden + mm(attended, wo_ref[...], 1, 0) + line(bout_ref)
    center = hidden - jnp.mean(hidden, axis=1, keepdims=True)
    inv_std = lax.rsqrt(jnp.mean(center * center, axis=1, keepdims=True) + 1e-06)
    n = center * inv_std
    gain2 = line(gain_ref)
    second = (n * gain2 + line(shift_ref)).astype(BF)
    out = hidden + line(bshrink_ref)
    second_grad = jnp.zeros(out.shape, F32)
    bexpand = line(bexpand_ref)
    for start in range(0, FF, FF_BLOCK):
        block = slice(start, start + FF_BLOCK)
        before = mm(second, we_ref[:, block], 1, 0) + bexpand[:, block]
        cdf = 0.5 + 0.5 * lax.erf(before * (0.5**0.5))
        active = (before * cdf).astype(BF)
        out = out + mm(active, ws_ref[block, :], 1, 0)
        slope = cdf + before * (jnp.exp(before * before * -0.5) * (0.5 / jnp.pi) ** 0.5)
        before_grad = (mm(up_low, ws_ref[block, :], 1, 1) * slope).astype(BF)
        ws_acc[:, block] = mm(up_low, active, 0, 0)
        we_acc[:, block] = mm(second, before_grad, 0, 0)
        second_grad = second_grad + mm(before_grad, we_ref[:, block], 1, 1)
        misc_acc[0:1, block] = jnp.sum(before_grad.astype(F32), axis=0, keepdims=True)
    for c in range(clips):
        out_ref[c] = out[rows[c]]
    e = gain2 * second_grad
    back = (
        e - jnp.mean(e, axis=1, keepdims=True) - n * jnp.mean(e * n, axis=1, keepdims=True)
    ) * inv_std
    hidden_full = (up + back).astype(BF).astype(F32)
    hidden_grad = hidden_full.astype(BF)
    wo_acc[...] = mm(hidden_grad, attended, 0, 0)
    wp_acc[...] = mm(hidden_grad, pooled, 0, 0)
    misc_acc[1:2, :D_OUT] = jnp.sum(second_grad * n, axis=0, keepdims=True)
    misc_acc[2:3, :D_OUT] = jnp.sum(second_grad, axis=0, keepdims=True)
    misc_acc[3:4, :D_OUT] = jnp.sum(up, axis=0, keepdims=True)
    misc_acc[4:5, :D_OUT] = jnp.sum(hidden_full, axis=0, keepdims=True)
    row = iota((LANES - HEAD_DIM, queries), 0)
    for c in range(clips):
        own_grad = hidden_full[rows[c]].astype(BF)
        hg_ref[c] = own_grad
        attended_grad = mm(wo_ref[...], own_grad, 1, 1).astype(BF).astype(F32)
        for h in range(HEADS):
            own = attended_grad[HEAD_DIM * h : HEAD_DIM * (h + 1)]
            for factor, do_ref, dot_ref in zip(
                factors[c][h], (do1_ref, do2_ref), (do1t_ref, do2t_ref), strict=True
            ):
                scaled = (own * factor).astype(BF)
                dot_ref[c, h] = scaled
                scaled = scaled.astype(F32)
                inner = jnp.sum(scaled * heads[c][h], axis=0, keepdims=True)
                high = inner.astype(BF).astype(F32)
                extra = jnp.where(row == 0, -high, jnp.where(row == 1, high - inner, 0.0))
                do_ref[c, h] = jnp.concatenate([scaled, extra], axis=0).T.astype(BF)
    me = me_ref[0]
    wpt_ref[...] = wp_acc[...]
    for u in range(4):
        for k in range(4):
            misc_acc[8 + u : 9 + u, HEAD_DIM * k : HEAD_DIM * (k + 1)] = misc_acc[
                1 + k : 2 + k, HEAD_DIM * u : HEAD_DIM * (u + 1)
            ]
    for r in range(4):
        u = me ^ r
        ref = shard_refs[r]
        wide = pl.ds(pl.multiple_of(u * 384, LANES), 384)
        tall = pl.ds(pl.multiple_of(u * 96, 8), 96)
        ref[0:384, :] = we_acc[:, wide].astype(BF)
        ref[384:768, :] = ws_acc[:, wide].astype(BF)
        ref[768:864, :] = wo_acc[tall, :].astype(BF)
        wp = wp_acc[tall, :]
        ref[864:912, :] = jnp.concatenate([wp[:48, :D_IN], wp[48:, :D_IN]], axis=1).astype(BF)
        bias = misc_acc[0:1, wide]
        others = misc_acc[pl.ds(8 + u, 1), :384]
        row = iota((48, 384), 0)
        ref[912:960, :] = jnp.where(row == 0, bias, jnp.where(row == 1, others, 0.0)).astype(BF)


def middle(me, o1, o2, pooled, up, vectors, weights):
    clips = len(pooled)
    queries = pooled[0].shape[0]
    grad = (clips, HEADS, queries, LANES)
    grad_t = (clips, HEADS, HEAD_DIM, queries)
    return call(
        functools.partial(middle_body, clips),
        (1,),
        [
            (pl.BlockSpec(memory_space=pltpu.SMEM), me),
            *(whole(value) for value in (*o1, *o2, *pooled, up, *vectors, *weights)),
        ],
        [
            out_whole((clips, queries, D_OUT), F32),
            out_whole((clips, queries, D_OUT), BF),
            out_whole(grad, BF),
            out_whole(grad, BF),
            out_whole(grad_t, BF),
            out_whole(grad_t, BF),
            *([out_whole((960, 384), BF)] * 4),
            out_whole((D_OUT, 2 * LANES), F32),
        ],
        [
            pltpu.VMEM((D_OUT, FF), F32),
            pltpu.VMEM((D_OUT, FF), F32),
            pltpu.VMEM((D_OUT, D_OUT), F32),
            pltpu.VMEM((D_OUT, 2 * LANES), F32),
            pltpu.VMEM((16, FF), F32),
        ],
        name="middle",
        stays=[True] * 11,
        cost=16,
    )


def backward_body(
    na_ref,
    nb_ref,
    wg_ref,
    p_ref,
    kt_ref,
    vt_ref,
    do_ref,
    dot_ref,
    qt_ref,
    dq_ref,
    dw_ref,
    ga_ref,
    gb_ref,
    n_ref,
    both_ref,
):
    rows = na_ref.shape[1]
    h = pl.program_id(0)
    p = p_ref[0]
    ds = p * mm(do_ref[0], vt_ref[0], 1, 0).astype(BF)
    dq_ref[0] = mm(kt_ref[0, :HEAD_DIM], ds, 1, 1)
    both_ref[h, :HEAD_DIM] = mm(qt_ref[0], ds, 1, 0).astype(BF)
    both_ref[h, HEAD_DIM:] = mm(dot_ref[0], p, 1, 0).astype(BF)

    @pl.when(h == HEADS - 1)
    def _():
        n_ref[:, :rows] = na_ref[...]
        n_ref[:, rows:] = nb_ref[...]
        both = both_ref[...].reshape(2 * D_OUT, 2 * rows)
        dw_ref[...] = mm(both, n_ref[...], 1, 1)
        g = mm(wg_ref[...], both, 1, 0).astype(BF)
        ga_ref[...] = g[:, :rows]
        gb_ref[...] = g[:, rows:]


def backward(clip, na, nb, wg, p, kt, vt, do, dot, qt, after=()):
    rows = na.shape[1]
    queries = qt.shape[2]
    return call(
        backward_body,
        (HEADS,),
        [
            whole(na),
            whole(nb),
            whole(wg),
            part(p),
            part(kt),
            part(vt),
            at_head(do, clip),
            at_head(dot, clip),
            part(qt),
        ],
        [
            out_part((HEADS, HEAD_DIM, queries), F32),
            out_whole((2 * D_OUT, EXT), F32),
            out_whole((D_IN, rows), BF),
            out_whole((D_IN, rows), BF),
        ],
        [pltpu.VMEM((EXT, 2 * rows), BF), pltpu.VMEM((HEADS, 2 * HEAD_DIM, 2 * rows), BF)],
        name="attend_back",
        after=after,
        cost=17,
    )


def gather_body(clips, me_ref, *refs):
    dq_refs, dw_refs, pooled_refs = (
        refs[: 2 * clips],
        refs[2 * clips : 4 * clips],
        refs[4 * clips : 5 * clips],
    )
    wt_ref, wpt_ref, gain_ref, shift_ref = refs[5 * clips : 5 * clips + 4]
    shard_refs, (dw_acc, line_ref, shard_ref) = refs[5 * clips + 4 : 5 * clips + 8], refs[5 * clips + 8 :]
    total = dw_refs[0][...]
    for ref in dw_refs[1:]:
        total = total + ref[...]
    for h in range(HEADS):
        at = 2 * HEAD_DIM * h
        dw_acc[HEADS + h] = total[at : at + HEAD_DIM]
        dw_acc[2 * HEADS + h] = total[at + HEAD_DIM : at + 2 * HEAD_DIM]
    dw = None
    for c in range(clips):
        dq = (dq_refs[2 * c][...] + dq_refs[2 * c + 1][...]) * SCALE
        dq = dq.reshape(D_OUT, dq.shape[2]).astype(BF)
        term = mm(dq, pooled_refs[c][...], 1, 0)
        dw = term if dw is None else dw + term
    for h in range(HEADS):
        dw_acc[h] = dw[HEAD_DIM * h : HEAD_DIM * (h + 1), :EXT]
    gain_sum = jnp.zeros((1, D_IN), F32)
    shift_sum = jnp.zeros((1, D_IN), F32)
    wp = wt_ref[3 * HEADS :].reshape(D_OUT, 2 * LANES)[:, :D_IN]
    terms = [(wt_ref[b][:HEAD_DIM, :D_IN], dw_acc[b]) for b in range(3 * HEADS)]
    for w, dw in [*terms, (wp, wpt_ref[...])]:
        w = w.astype(F32)
        gain_sum = gain_sum + jnp.sum(w * dw[:, :D_IN], axis=0, keepdims=True)
        shift_sum = shift_sum + jnp.sum(w * dw[:, D_IN : D_IN + 1], axis=0, keepdims=True)
    gain_sum = (gain_sum - line(shift_ref) * shift_sum) / line(gain_ref)
    for at, first in ((0, 0), (1, 2 * HEADS)):
        for h in range(HEADS):
            sums = dw_acc[first + h][:, LANES:]
            sums = jnp.concatenate(
                [sums, jnp.zeros((HEAD_DIM, 2 * LANES - EXT), F32)], axis=1
            )
            sums = jnp.concatenate([sums, jnp.zeros((LANES - HEAD_DIM, LANES), F32)], axis=0).T
            line_ref[at : at + 1, HEAD_DIM * h : HEAD_DIM * (h + 1)] = sums[
                D_IN - LANES : D_IN - LANES + 1, :HEAD_DIM
            ]
    line_ref[2:3, :D_IN] = gain_sum
    line_ref[3:4, :D_IN] = shift_sum
    for u in range(4):
        at = 0
        for source, size in ((0, 96), (1, 96), (2, 48), (3, 48)):
            shard_ref[u : u + 1, at : at + size] = line_ref[
                source : source + 1, size * u : size * (u + 1)
            ]
            at += size
        shard_ref[u : u + 1, at:] = jnp.zeros((1, D_OUT - at), F32)
    for r in range(4):
        u = me_ref[0] ^ r
        ref = shard_refs[r]
        rows = jnp.concatenate([dw_acc[3 * u + i][:, :D_IN] for i in range(3)], axis=0)
        ref[:144, :] = jnp.concatenate([rows[:144], rows[144:]], axis=1).astype(BF)
        ref[144:, :] = jnp.where(
            iota((16, D_OUT), 0) == 0, shard_ref[pl.ds(u, 1), :], 0.0
        ).astype(BF)


def gather(me, dq, dw, pooled, wt, wpt, gain, shift, after=()):
    clips = len(pooled)
    return call(
        functools.partial(gather_body, clips),
        (1,),
        [
            (pl.BlockSpec(memory_space=pltpu.SMEM), me),
            *(whole(v) for v in (*dq, *dw, *pooled, wt, wpt, gain, shift)),
        ],
        [out_whole((160, D_OUT), BF)] * 4,
        [
            pltpu.VMEM((3 * HEADS, HEAD_DIM, EXT), F32),
            pltpu.VMEM((8, D_OUT), F32),
            pltpu.VMEM((8, D_OUT), F32),
        ],
        name="gather",
        after=after,
        cost=6,
    )


def final_body(terms, tok_ref, hg_ref, wp_ref, qkv_ref, gain_ref, dq1_ref, dq2_ref, *refs):
    part_refs, out_ref = refs[:terms], refs[-1]
    slots, _, units = tok_ref.shape[1:]
    gain = column(gain_ref)
    dq = ((dq1_ref[...] + dq2_ref[...]) * SCALE).reshape(D_OUT, 4 * units).astype(BF)
    spread = mm(wp_ref[...], hg_ref[0], 1, 1) + mm(qkv_ref[:, :D_OUT], dq, 1, 0)
    spread = spread * 0.25
    places = [slice(units * s, units * (s + 1)) for s in range(slots)]
    spread = [spread[:, places[2 * (s >> 3) + ((s >> 1) & 1)]] for s in range(slots)]
    grad = total_of(part_refs) + jnp.concatenate(spread, axis=1)
    x = jnp.concatenate([tok_ref[0, s] for s in range(slots)], axis=1).astype(F32)
    center = x - jnp.mean(x, axis=0, keepdims=True)
    inv_std = lax.rsqrt(jnp.mean(center * center, axis=0, keepdims=True) + 1e-06)
    n = center * inv_std
    e = grad * gain
    back = e - jnp.mean(e, axis=0, keepdims=True) - n * jnp.mean(e * n, axis=0, keepdims=True)
    back = back * inv_std
    for s in range(slots):
        out_ref[0, s] = back[:, places[s]]


def final(clip, tokens, hg, dq, wp, qkv, gain, parts, filled, after=()):
    terms = len(parts)
    return call(
        functools.partial(final_body, terms),
        (1,),
        [
            at_clip(tokens, clip),
            at_clip(hg, clip),
            *(whole(v) for v in (wp, qkv, gain, *dq, *parts)),
            *([] if filled is None else [(pl.BlockSpec(memory_space=pl.ANY), filled)]),
        ],
        [(at_clip(tokens, clip)[0], tokens.shape, F32)],
        name="final",
        stays=[True],
        cost=6,
        after=after,
        aliases=None if filled is None else {7 + terms: 0},
    )[0]


def unpack_first_body(
    place_ref,
    value_ref,
    other_ref,
    proj_ref,
    bproj_ref,
    wo_ref,
    bout_ref,
    gain_ref,
    shift_ref,
    we_ref,
    be_ref,
    ws_ref,
    bs_ref,
    rows_ref,
):
    half = value_ref.shape[0]
    at = pl.multiple_of(place_ref[0] * half, 8)
    rows_ref[pl.ds(at, half), :] = value_ref[...].astype(F32)
    rows_ref[pl.ds(pl.multiple_of(half - at, 8), half), :] = other_ref[...].astype(F32)
    we_ref[...] = rows_ref[:384]
    ws_ref[...] = rows_ref[384:768].T
    wo_ref[...] = rows_ref[768:864]
    proj = jnp.concatenate([rows_ref[864:912, :D_IN], rows_ref[864:912, D_IN:]], axis=0)
    proj_ref[...] = proj.T
    lines = rows_ref[912:920]
    be_ref[...] = lines[0:1].reshape(384)
    for ref, k in ((gain_ref, 0), (shift_ref, 1), (bs_ref, 2), (bout_ref, 3), (bproj_ref, 3)):
        ref[...] = lines[1:2, 96 * k : 96 * (k + 1)].reshape(96)


def unpack_first(place, value, other, after=()):
    shapes = [(192, 96), (96,), (96, 384), (96,), (96,), (96,), (384, 384), (384,), (384, 384), (96,)]
    return call(
        unpack_first_body,
        (1,),
        [(pl.BlockSpec(memory_space=pltpu.SMEM), place), whole(value), whole(other)],
        [out_whole(shape, F32) for shape in shapes],
        [pltpu.VMEM((2 * value.shape[0], D_OUT), F32)],
        name="unpack_first",
        stays=[True] * len(shapes),
        after=after,
        cost=2,
    )


def unpack_second_body(a_ref, b_ref, qkv_ref, bq_ref, bv_ref, gain_ref, shift_ref):
    total = a_ref[...].astype(F32) + b_ref[...].astype(F32)
    qkv_ref[...] = jnp.concatenate([total[:144, :D_IN], total[:144, D_IN:]], axis=0).T
    at = 0
    for ref in (bq_ref, bv_ref, gain_ref, shift_ref):
        size = ref.shape[0]
        ref[...] = total[144:145, at : at + size].reshape(size)
        at += size


def unpack_second(a, b):
    shapes = [(192, 288), (96,), (96,), (48,), (48,)]
    return call(
        unpack_second_body,
        (1,),
        [whole(a), whole(b)],
        [out_whole(shape, F32) for shape in shapes],
        name="unpack_second",
        stays=[True] * len(shapes),
        cost=1,
    )


def swap_unit(value, bit):
    return lax.ppermute(value, "unit", [(i, i ^ bit) for i in range(4)])


def swap_clip(value, bit):
    size = lax.axis_size("clip")
    return lax.ppermute(value, "clip", [(i, i ^ bit) for i in range(size)])


def add(*values):
    return functools.reduce(lambda a, b: a + b, [v.astype(F32) for v in values]).astype(BF)


def member():
    at = lax.axis_index("clip").astype(jnp.int32)
    return jnp.stack([at & 1, (at >> 1) & 1])


def total_of(refs):
    return functools.reduce(lambda a, b: a + b, [ref[...].astype(F32) for ref in refs])


def between(sums, place, cut=None, grads=None, join=None):
    rows, width = sums[0].shape
    count, more = len(sums), grads or []
    pieces = 1 if cut is None else 2
    tall = 2 * rows if join is not None else rows // pieces

    def body(place_ref, *refs):
        terms, refs = refs[:count], refs[count:]
        others, refs = refs[: len(more)], refs[len(more) :]
        outs, scratch = refs[:-1], refs[-1]
        if more:
            outs[-1][...] = total_of(others).astype(BF)
        if join is not None:
            for d in range(2):
                at = pl.multiple_of((place_ref[join] ^ d) * rows, 8)
                scratch[pl.ds(at, rows), :] = terms[d][...].astype(F32)
            outs[0][...] = scratch[...].astype(BF)
        elif cut is None:
            outs[0][...] = total_of(terms).astype(BF)
        else:
            scratch[...] = total_of(terms)
            for d in range(2):
                at = pl.multiple_of((place_ref[cut] ^ d) * tall, 8)
                outs[d][...] = scratch[pl.ds(at, tall), :].astype(BF)

    return list(
        call(
            body,
            (1,),
            [(pl.BlockSpec(memory_space=pltpu.SMEM), place), *(whole(v) for v in (*sums, *more))],
            [
                *([out_whole((tall, width), BF)] * pieces),
                *([out_whole(more[0].shape, BF)] if more else []),
            ],
            [pltpu.VMEM((max(rows, tall), width), F32)],
            name="between",
            cost=2,
        )
    )


def in_hbm(*values):
    return [pltpu.with_memory_space_constraint(v, pltpu.HBM) for v in values]


def together(*values):
    return lax.optimization_barrier(values)


def shards(
    tokens,
    first_gain,
    first_shift,
    proj_weight,
    proj_bias,
    qkv_weight,
    query_bias,
    value_bias,
    output_weight,
    output_bias,
    second_gain,
    second_shift,
    expand_weight,
    expand_bias,
    shrink_weight,
    shrink_bias,
    frame_counts,
    unit_frames,
    cotangent,
):
    clips, units = tokens.shape[:2]
    me = lax.axis_index("unit").astype(jnp.int32).reshape(1)
    vectors = [proj_bias, output_bias, second_gain, second_shift, shrink_bias, expand_bias]
    flat = tokens.transpose(0, 2, 3, 1)
    upstream = cotangent.transpose(0, 2, 1, 3).reshape(clips, 4 * units, D_OUT)
    normed, pooled = normed_tokens(flat, unit_frames, frame_counts, first_gain, first_shift)
    near, across = [(n, swap_unit(n, 1)) for n in normed], []
    wt, wg, query = queries_of(qkv_weight, proj_weight, query_bias, value_bias, pooled)
    own, rest, far = [], [], []
    for c in range(clips):
        across.append(swap_unit(together(near[c][0], near[0][1])[0] if c else near[c][0], 2))
        weights = [wt, query[c][0]] if c else in_hbm(wt, query[c][0])
        keys = near[c] if c else in_hbm(*near[c])
        own.append(forward(*keys, *weights, after=in_hbm(*(v[3] for v in own[-1:]))))
    for c in range(clips):
        held, _ = together(across[c], own[c][3])
        far.append((held, swap_unit(held, 1)))
        rest.append(forward(*far[c], wt, query[c][0], after=in_hbm(*(v[3] for v in (own + rest)[-1:]))))
    out, hg, do1, do2, do1t, do2t, keep, send0, across, send1, wpt = middle(
        me,
        in_hbm(*(value[3] for value in own)),
        in_hbm(*(value[3] for value in rest)),
        pooled,
        upstream,
        vectors,
        [proj_weight, output_weight, expand_weight, shrink_weight],
    )
    dq, dw = [[None, None] for _ in range(clips)], [[None, None] for _ in range(clips)]
    place = member()
    got = [swap_unit(send0, 1), swap_unit(send1, 1)]
    out = out.reshape(clips, 4, units, D_OUT).transpose(0, 2, 1, 3)
    got, out = together(got, out)
    (value,) = between([*in_hbm(across), got[1]], place)
    terms = [keep, got[0]]
    calls = [(c, 1) for c in range(clips)] + [(c, 0) for c in range(clips)]
    parts = [[None] * 3 for _ in range(clips)]
    lent, owed = [], []
    moves = ["unit", 1, 2, 4]
    bits = []
    bit = 8
    while bit < lax.axis_size("clip"):
        bits.append(bit)
        bit *= 2
    held = [value]
    for at, (c, side) in enumerate(calls):
        keys, kept, grads = (far, rest, (do2, do2t)) if side else (near, own, (do1, do1t))
        move = moves[at]
        sent = [swap_unit(value, 2) if move == "unit" else swap_clip(value, move)]
        travel = [swap_unit(parts[b][0], 2) for b in lent]
        travel += [swap_unit(gb, 1) for _, gb in owed]
        result = backward(c, *keys[c], wg, *kept[c][:3], *grads, query[c][1], after=held)
        *result, travel, sent = together(*result, travel, sent)
        dq[c][side], dw[c][side], ga, gb = result
        for b in lent:
            parts[b][0] = travel.pop(0)
        lent, loose = [], None
        for ((b, other), _), arrived in zip(owed, travel, strict=True):
            if other:
                loose = [parts[b][0], arrived]
                lent.append(b)
            else:
                parts[b][2] = arrived
        cut = {"unit": 0, 1: 1}.get(move)
        result = between([*terms, *sent], place, cut, loose)
        if loose:
            parts[lent[0]][0] = result.pop()
        if cut is None:
            (value,), terms = result, result
        else:
            terms, value = result[:1], result[1]
        if move == 2:
            for bit in bits:
                value = add(value, swap_clip(value, bit))
            terms = [value]
        owed = [((c, side), gb)]
        parts[c][0 if side else 1] = ga
        held = [dq[c][side], value, *terms, *(parts[b][0] for b in lent)]
    half = swap_clip(value, 2)
    travel = [swap_unit(gb, 1) for _, gb in owed]
    result = gather(
        me,
        [v for pair in dq for v in pair],
        [v for pair in dw for v in pair],
        pooled,
        wt,
        wpt,
        first_gain,
        first_shift,
        after=held,
    )
    (keep, send0, across, send1), travel = together(result, travel)
    for ((b, _), _), arrived in zip(owed, travel, strict=True):
        parts[b][2] = arrived
    got = [swap_unit(send0, 1), swap_unit(send1, 1)]
    second = add(across, got[1])
    input_grad, firsts = None, None
    bit = 0
    for c in range(max(clips, 3)):
        sent = swap_clip(second, bit) if bit else swap_unit(second, 2)
        if c < clips:
            input_grad = final(
                c, flat, hg, dq[c], proj_weight, qkv_weight, first_gain, parts[c], input_grad, after=[second]
            )
            if c == 0:
                sent, input_grad, half = together(sent, input_grad, half)
                (value,) = between([value, half], place, join=1)
                other = swap_clip(value, 1)
            else:
                sent, input_grad = together(sent, input_grad)
        if c < 3:
            second = add(second, sent) if bit else add(keep, got[0], sent)
            bit = 2 * bit if bit else 1
    last = swap_clip(second, 4)
    firsts = unpack_first(place, value, other, after=[second])
    last, firsts = together(last, firsts)
    for more in bits:
        second, last = add(second, last), None
        last = swap_clip(second, more)
    wp_grad, bp_grad, wo_grad, bo_grad, g2_grad, s2_grad, we_grad, be_grad, ws_grad, bs_grad = firsts
    qkv_grad, bq_grad, bv_grad, g1_grad, s1_grad = unpack_second(second, last)
    return (
        out,
        input_grad.transpose(0, 3, 1, 2),
        g1_grad,
        s1_grad,
        wp_grad,
        bp_grad,
        qkv_grad,
        bq_grad,
        bv_grad,
        wo_grad.T,
        bo_grad,
        g2_grad,
        s2_grad,
        we_grad,
        be_grad,
        ws_grad,
        bs_grad,
    )


def solution(mesh):
    every = P()
    split = P("clip", "unit", None, None)
    return jax.shard_map(
        shards,
        mesh=mesh,
        in_specs=(split,) + (every,) * 15 + (P("clip"), P("clip", "unit"), split),
        out_specs=(
            split,
            split,
            P("unit"),
            P("unit"),
            P(None, "unit"),
            P("unit"),
            P(None, "unit"),
            P("unit"),
            P("unit"),
            P(None, "unit"),
            P("unit"),
            P("unit"),
            P("unit"),
            P(None, "unit"),
            P("unit"),
            P("unit", None),
            P("unit"),
        ),
        check_vma=False,
    )
```

```python
import functools

import jax
import jax.numpy as jnp
from jax import lax
from jax.experimental import pallas as pl
from jax.experimental.pallas import tpu as pltpu
from jax.sharding import PartitionSpec as P

D_IN = 192
D_OUT = 384
HEADS = 4
HEAD_DIM = 96
FF = 1536
LANES = 128
EXT = 208
SCALE = HEAD_DIM**-0.5
LOG2E = 1.4426950408889634
BF = jnp.bfloat16
F32 = jnp.float32
VMEM_MIB = 46
VMEM_MIB_FIRST = 64
FF_BLOCK = 768


def mm(a, b, ca, cb):
    return lax.dot_general(a, b, (((ca,), (cb,)), ((), ())), preferred_element_type=F32)


def iota(shape, dim):
    return lax.broadcasted_iota(jnp.int32, shape, dim)


def call(body, grid, ins, outs, scratch=(), name=None, cost=None, after=(), aliases=None, stays=None):
    count = len(ins)
    stays = stays or [False] * len(outs)

    def run(*refs):
        body(*refs[:count], *refs[count + len(after) :])

    ins = [*ins, *((pl.BlockSpec(memory_space=pl.ANY), value) for value in after)]
    return pl.pallas_call(
        run,
        grid=grid,
        in_specs=[spec for spec, _ in ins],
        out_specs=[spec for spec, _, _ in outs],
        out_shape=[
            (pltpu.HBM if stay else jax.ShapeDtypeStruct)(shape, dtype)
            for stay, (_, shape, dtype) in zip(stays, outs, strict=True)
        ],
        scratch_shapes=list(scratch),
        compiler_params=pltpu.CompilerParams(
            dimension_semantics=("arbitrary",) * len(grid), vmem_limit_bytes=(VMEM_MIB_FIRST if name in ("normed", "queries") else VMEM_MIB) * 2**20
        ),
        name=name,
        cost_estimate=pl.CostEstimate(
            flops=int(cost * 1.1e9), bytes_accessed=int(cost * 1e6), transcendentals=0
        ),
        input_output_aliases=aliases or {},
    )(*[value for _, value in ins])


def whole(value):
    rank = len(value.shape)
    return (pl.BlockSpec(value.shape, lambda *_: (0,) * rank), value)


def part(value):
    rank = len(value.shape)
    return (pl.BlockSpec((1,) + value.shape[1:], lambda i: (i,) + (0,) * (rank - 1)), value)


def at_clip(value, clip):
    rank = len(value.shape)
    return (pl.BlockSpec((1,) + value.shape[1:], lambda *_: (clip,) + (0,) * (rank - 1)), value)


def at_head(value, clip):
    rank = len(value.shape)
    return (
        pl.BlockSpec((None, 1) + value.shape[2:], lambda i: (clip, i) + (0,) * (rank - 2)),
        value,
    )


def out_part(shape, dtype):
    rank = len(shape)
    return (pl.BlockSpec((1,) + shape[1:], lambda i: (i,) + (0,) * (rank - 1)), shape, dtype)


def out_whole(shape, dtype):
    rank = len(shape)
    return (pl.BlockSpec(shape, lambda *_: (0,) * rank), shape, dtype)


def line(ref):
    return ref[...].astype(F32).reshape(1, -1)


def eye(size):
    return jnp.where(iota((size, size), 0) == iota((size, size), 1), 1.0, 0.0).astype(BF)


def column(ref):
    size = ref.shape[0]
    values = jnp.broadcast_to(line(ref), (16, size)).astype(BF)
    return mm(eye(size), values, 1, 1)[:, 0:1]


def normed_body(clips, tok_ref, frames_ref, counts_ref, gain_ref, shift_ref, *outs):
    slots, _, units = tok_ref.shape[1:]
    clip = pl.program_id(0)
    gain, shift = column(gain_ref), column(shift_ref)
    x = jnp.concatenate([tok_ref[0, s] for s in range(slots)], axis=1).astype(F32)
    center = x - jnp.mean(x, axis=0, keepdims=True)
    var = jnp.mean(center * center, axis=0, keepdims=True)
    normed = (center * lax.rsqrt(var + 1e-06) * gain + shift).astype(BF)
    extra = iota((EXT - D_IN, units), 0)
    invalid = jnp.where(frames_ref[pl.ds(clip, 1), :] >= counts_ref[clip], 1.0, 0.0)
    extra = jnp.where(extra == 0, 1.0, jnp.where(extra == 1, invalid, 0.0))
    extra = jnp.concatenate([extra] * slots, axis=1).astype(BF)
    pieces = [normed[:, units * s : units * (s + 1)].astype(F32) for s in range(slots)]
    means = []
    for p in range(4):
        first = 8 * (p >> 1) + 2 * (p & 1)
        means.append(
            (pieces[first] + pieces[first + 1] + pieces[first + 4] + pieces[first + 5]) * 0.25
        )
    pooled = jnp.concatenate(means, axis=1)
    row = iota((2 * LANES - D_IN, 4 * units), 0)
    pooled = jnp.concatenate([pooled, jnp.where(row == 0, 1.0, 0.0)], axis=0).T.astype(BF)
    for c in range(clips):

        @pl.when(clip == c)
        def _():
            outs[2 * c][:D_IN, :] = normed
            outs[2 * c][D_IN:, :] = extra
            outs[2 * c + 1][...] = pooled


def normed_tokens(tokens, frames, counts, gain, shift):
    clips, slots, _, units = tokens.shape
    outs = call(
        functools.partial(normed_body, clips),
        (clips,),
        [
            part(tokens),
            whole(frames),
            (pl.BlockSpec(memory_space=pltpu.SMEM), counts),
            whole(gain),
            whole(shift),
        ],
        [out_whole((EXT, slots * units), BF), out_whole((4 * units, 2 * LANES), BF)] * clips,
        name="normed",
        cost=5,
    )
    return outs[0::2], outs[1::2]


def query_body(clips, qkv_ref, wp_ref, qbias_ref, vbias_ref, *refs):
    pooled_refs, wt_ref, wg_ref, q_refs = refs[:clips], refs[clips], refs[clips + 1], refs[clips + 2 :]
    bias = jnp.concatenate(
        [line(qbias_ref), jnp.zeros((1, D_OUT), F32), line(vbias_ref)], axis=1
    )
    bias = jnp.where(iota((EXT - D_IN, 3 * D_OUT), 0) == 0, bias, 0.0).astype(BF)
    turned = jnp.concatenate([qkv_ref[...], bias], axis=0).astype(F32).T
    row, lane = iota((LANES - HEAD_DIM, EXT), 0), iota((LANES - HEAD_DIM, EXT), 1)
    ones = lane == D_IN
    extras = (
        jnp.where(ones & (row == 0), 8.0, 0.0),
        jnp.where(
            (lane == D_IN + 1) & (row == 0),
            -1e30,
            jnp.where(ones & (row >= 1) & (row <= 3), 1.0, 0.0),
        ),
        jnp.where(ones & (row <= 1), 1.0, 0.0),
    )
    for block in range(3 * HEADS):
        rows = turned[HEAD_DIM * block : HEAD_DIM * (block + 1)]
        rows = jnp.concatenate([rows, extras[block // HEADS]], axis=0)
        wt_ref[block, :, :EXT] = rows.astype(BF)
        wt_ref[block, :, EXT:] = jnp.zeros((LANES, 2 * LANES - EXT), BF)
    wg_ref[...] = jnp.concatenate(
        [
            qkv_ref[:, start : start + HEAD_DIM]
            for h in range(HEADS)
            for start in (D_OUT + HEAD_DIM * h, 2 * D_OUT + HEAD_DIM * h)
        ],
        axis=1,
    )
    for block in range(D_OUT // LANES):
        columns = wp_ref[:, LANES * block : LANES * (block + 1)]
        wt_ref[3 * HEADS + block, :, :D_IN] = mm(eye(LANES), columns, 1, 1).astype(BF)
        wt_ref[3 * HEADS + block, :, D_IN:] = jnp.zeros((LANES, 2 * LANES - D_IN), BF)
    weight = wt_ref[:HEADS].reshape(HEADS * LANES, 2 * LANES)
    for c in range(clips):
        pooled = pooled_refs[c][...]
        q = mm(pooled, weight, 1, 1) * (SCALE * LOG2E)
        turned = mm(weight, pooled, 1, 1) * SCALE
        for h in range(HEADS):
            q_refs[2 * c][h] = q[:, LANES * h : LANES * (h + 1)].astype(BF)
            q_refs[2 * c + 1][h] = turned[LANES * h : LANES * h + HEAD_DIM].astype(BF)


def queries_of(qkv, wp, qbias, vbias, pooled):
    clips, count = len(pooled), pooled[0].shape[0]
    wt, wg, *rest = call(
        functools.partial(query_body, clips),
        (1,),
        [whole(v) for v in (qkv, wp, qbias, vbias, *pooled)],
        [
            out_whole((3 * HEADS + D_OUT // LANES, LANES, 2 * LANES), BF),
            out_whole((D_IN, 2 * D_OUT), BF),
            *[
                out_whole((HEADS, count, LANES), BF),
                out_whole((HEADS, HEAD_DIM, count), BF),
            ]
            * clips,
        ],
        name="queries",
        cost=5,
    )
    return wt, wg, [(rest[2 * c], rest[2 * c + 1]) for c in range(clips)]


def forward_body(
    na_ref, nb_ref, wk_ref, wv_ref, qs_ref, p_ref, kt_ref, vt_ref, o_ref, n_ref, keys_ref, values_ref, asks_ref, sem
):
    rows = na_ref.shape[1]
    queries = qs_ref.shape[1]
    h = pl.program_id(0)
    tall = HEAD_DIM + 16
    most, less = 75.0, 60.0
    keys_out = pltpu.make_async_copy(keys_ref, kt_ref, sem.at[0])
    values_out = pltpu.make_async_copy(values_ref, vt_ref, sem.at[1])

    def asked(head, high, middle=0.0, low=0.0):
        lane = iota((queries, LANES), 1)
        q = qs_ref[head].astype(F32)
        for k, value in enumerate((high, middle, low)):
            q = jnp.where(lane == HEAD_DIM + 1 + k, -value, q)
        asks_ref[head] = q.astype(BF)

    @pl.when(h == 0)
    def _():
        n_ref[:, :rows] = na_ref[...]
        n_ref[:, rows:] = nb_ref[...]
        weight = wk_ref[...].reshape(HEADS * LANES, 2 * LANES)[:, :EXT]
        keys = mm(weight, n_ref[...], 1, 0)
        worst = jnp.zeros((1, 1), F32)
        for head in range(HEADS):
            own = keys[LANES * head : LANES * (head + 1)]
            keys_ref[head] = own.astype(BF)
            plain = own[:HEAD_DIM]
            longest = jnp.max(jnp.sum(plain * plain, axis=0, keepdims=True), axis=1, keepdims=True)
            q = qs_ref[head].astype(F32)
            q = jnp.where(iota(q.shape, 1) < HEAD_DIM, q, 0.0)
            bound = jnp.sqrt(jnp.sum(q * q, axis=1, keepdims=True) * longest)
            asked(head, bound - less)
            worst = jnp.maximum(worst, jnp.max(bound, axis=0, keepdims=True))
        keys_out.start()
        weight = wv_ref[...].reshape(HEADS * LANES, 2 * LANES)[:, :EXT]
        values = mm(weight, n_ref[...], 1, 0).astype(BF)
        values_ref[...] = values.reshape(HEADS, LANES, 2 * rows)
        values_out.start()

        @pl.when(worst[0, 0] > most)
        def _():
            blocks = 2 * rows // LANES
            rest = slice(blocks * LANES, 2 * rows)

            @pl.loop(0, HEADS)
            def _(head):
                def raised(m, place):
                    scores = mm(qs_ref[head], keys_ref[head, :, place], 1, 0)
                    return jnp.maximum(m, jnp.max(scores, axis=1, keepdims=True))

                def step(i, m):
                    return raised(m, pl.ds(pl.multiple_of(i * LANES, LANES), LANES))

                m = lax.fori_loop(0, blocks, step, jnp.full((queries, 1), -jnp.inf, F32))
                if 2 * rows % LANES:
                    m = raised(m, rest)
                high = m.astype(BF).astype(F32)
                middle = (m - high).astype(BF).astype(F32)
                asked(head, high, middle, m - high - middle)

    @pl.when(h == HEADS - 1)
    def _():
        keys_out.wait()
        values_out.wait()

    row, lane = iota((16, LANES), 0), iota((16, LANES), 1)
    pick = (row == 0) & (lane > HEAD_DIM) & (lane <= HEAD_DIM + 3)
    pick = jnp.where(pick, 1.0, 0.0).astype(BF)
    q = asks_ref[h]
    p = jnp.exp2(mm(q, keys_ref[h], 1, 0)).astype(BF)
    p_ref[0] = p
    o_ref[0, :tall] = mm(values_ref[h, :tall], p, 1, 1)
    o_ref[0, tall:] = mm(pick, q, 1, 1)


def forward(na, nb, wt, qs, after=()):
    rows = na.shape[1]
    queries = qs.shape[1]
    return call(
        forward_body,
        (HEADS,),
        [
            whole(na),
            whole(nb),
            *((pl.BlockSpec((HEADS,) + wt.shape[1:], lambda *_, at=at: (at, 0, 0)), wt) for at in (1, 2)),
            whole(qs),
        ],
        [
            out_part((HEADS, queries, 2 * rows), BF),
            (pl.BlockSpec(memory_space=pl.ANY), (HEADS, LANES, 2 * rows), BF),
            (pl.BlockSpec(memory_space=pl.ANY), (HEADS, LANES, 2 * rows), BF),
            out_part((HEADS, LANES, queries), F32),
        ],
        [
            pltpu.VMEM((EXT, 2 * rows), BF),
            pltpu.VMEM((HEADS, LANES, 2 * rows), BF),
            pltpu.VMEM((HEADS, LANES, 2 * rows), BF),
            pltpu.VMEM((HEADS, queries, LANES), BF),
            pltpu.SemaphoreType.DMA((2,)),
        ],
        name="attend",
        after=after,
        stays=[True] * 4,
        cost=12,
    )


def middle_body(clips, me_ref, *refs):
    o1_refs, o2_refs, pooled_refs = refs[:clips], refs[clips : 2 * clips], refs[2 * clips : 3 * clips]
    up_ref, bproj_ref, bout_ref, gain_ref, shift_ref, bshrink_ref, bexpand_ref = refs[
        3 * clips : 3 * clips + 7
    ]
    wp_ref, wo_ref, we_ref, ws_ref = refs[3 * clips + 7 : 3 * clips + 11]
    out_ref, hg_ref, do1_ref, do2_ref, do1t_ref, do2t_ref = refs[3 * clips + 11 : 3 * clips + 17]
    shard_refs, wpt_ref = refs[3 * clips + 17 : 3 * clips + 21], refs[3 * clips + 21]
    we_acc, ws_acc, wo_acc, wp_acc, misc_acc = refs[3 * clips + 22 :]
    queries = pooled_refs[0].shape[0]
    rows = [slice(queries * c, queries * (c + 1)) for c in range(clips)]
    heads = [[] for _ in range(clips)]
    factors = [[] for _ in range(clips)]
    for c in range(clips):
        for h in range(HEADS):
            o1, o2 = o1_refs[c][h], o2_refs[c][h]
            l1, l2 = o1[HEAD_DIM : HEAD_DIM + 1], o2[HEAD_DIM : HEAD_DIM + 1]
            m1, m2 = -o1[HEAD_DIM + 16 : HEAD_DIM + 17], -o2[HEAD_DIM + 16 : HEAD_DIM + 17]
            m = jnp.maximum(m1, m2)
            a1, a2 = jnp.exp2(m1 - m), jnp.exp2(m2 - m)
            inverse = 1.0 / (a1 * l1 + a2 * l2)
            c1, c2 = a1 * inverse, a2 * inverse
            heads[c].append(o1[:HEAD_DIM] * c1 + o2[:HEAD_DIM] * c2)
            factors[c].append((c1, c2))
    attended = jnp.concatenate([jnp.concatenate(parts, axis=0).T for parts in heads], axis=0)
    attended = attended.astype(BF)
    pooled = jnp.concatenate([ref[...].astype(F32) for ref in pooled_refs], axis=0).astype(BF)
    up = jnp.concatenate([up_ref[c].astype(F32) for c in range(clips)], axis=0)
    up_low = up.astype(BF)
    hidden = mm(pooled[:, :D_IN], wp_ref[...], 1, 0) + line(bproj_ref)
    hidden = hidden + mm(attended, wo_ref[...], 1, 0) + line(bout_ref)
    center = hidden - jnp.mean(hidden, axis=1, keepdims=True)
    inv_std = lax.rsqrt(jnp.mean(center * center, axis=1, keepdims=True) + 1e-06)
    n = center * inv_std
    gain2 = line(gain_ref)
    second = (n * gain2 + line(shift_ref)).astype(BF)
    out = hidden + line(bshrink_ref)
    second_grad = jnp.zeros(out.shape, F32)
    bexpand = line(bexpand_ref)
    for start in range(0, FF, FF_BLOCK):
        block = slice(start, start + FF_BLOCK)
        before = mm(second, we_ref[:, block], 1, 0) + bexpand[:, block]
        cdf = 0.5 + 0.5 * lax.erf(before * (0.5**0.5))
        active = (before * cdf).astype(BF)
        out = out + mm(active, ws_ref[block, :], 1, 0)
        slope = cdf + before * (jnp.exp(before * before * -0.5) * (0.5 / jnp.pi) ** 0.5)
        before_grad = (mm(up_low, ws_ref[block, :], 1, 1) * slope).astype(BF)
        ws_acc[:, block] = mm(up_low, active, 0, 0)
        we_acc[:, block] = mm(second, before_grad, 0, 0)
        second_grad = second_grad + mm(before_grad, we_ref[:, block], 1, 1)
        misc_acc[0:1, block] = jnp.sum(before_grad.astype(F32), axis=0, keepdims=True)
    for c in range(clips):
        out_ref[c] = out[rows[c]]
    e = gain2 * second_grad
    back = (
        e - jnp.mean(e, axis=1, keepdims=True) - n * jnp.mean(e * n, axis=1, keepdims=True)
    ) * inv_std
    hidden_full = (up + back).astype(BF).astype(F32)
    hidden_grad = hidden_full.astype(BF)
    wo_acc[...] = mm(hidden_grad, attended, 0, 0)
    wp_acc[...] = mm(hidden_grad, pooled, 0, 0)
    misc_acc[1:2, :D_OUT] = jnp.sum(second_grad * n, axis=0, keepdims=True)
    misc_acc[2:3, :D_OUT] = jnp.sum(second_grad, axis=0, keepdims=True)
    misc_acc[3:4, :D_OUT] = jnp.sum(up, axis=0, keepdims=True)
    misc_acc[4:5, :D_OUT] = jnp.sum(hidden_full, axis=0, keepdims=True)
    row = iota((LANES - HEAD_DIM, queries), 0)
    for c in range(clips):
        own_grad = hidden_full[rows[c]].astype(BF)
        hg_ref[c] = own_grad
        attended_grad = mm(wo_ref[...], own_grad, 1, 1).astype(BF).astype(F32)
        for h in range(HEADS):
            own = attended_grad[HEAD_DIM * h : HEAD_DIM * (h + 1)]
            for factor, do_ref, dot_ref in zip(
                factors[c][h], (do1_ref, do2_ref), (do1t_ref, do2t_ref), strict=True
            ):
                scaled = (own * factor).astype(BF)
                dot_ref[c, h] = scaled
                scaled = scaled.astype(F32)
                inner = jnp.sum(scaled * heads[c][h], axis=0, keepdims=True)
                high = inner.astype(BF).astype(F32)
                extra = jnp.where(row == 0, -high, jnp.where(row == 1, high - inner, 0.0))
                do_ref[c, h] = jnp.concatenate([scaled, extra], axis=0).T.astype(BF)
    me = me_ref[0]
    wpt_ref[...] = wp_acc[...]
    for u in range(4):
        for k in range(4):
            misc_acc[8 + u : 9 + u, HEAD_DIM * k : HEAD_DIM * (k + 1)] = misc_acc[
                1 + k : 2 + k, HEAD_DIM * u : HEAD_DIM * (u + 1)
            ]
    for r in range(4):
        u = me ^ r
        ref = shard_refs[r]
        wide = pl.ds(pl.multiple_of(u * 384, LANES), 384)
        tall = pl.ds(pl.multiple_of(u * 96, 8), 96)
        ref[0:384, :] = we_acc[:, wide].astype(BF)
        ref[384:768, :] = ws_acc[:, wide].astype(BF)
        ref[768:864, :] = wo_acc[tall, :].astype(BF)
        wp = wp_acc[tall, :]
        ref[864:912, :] = jnp.concatenate([wp[:48, :D_IN], wp[48:, :D_IN]], axis=1).astype(BF)
        bias = misc_acc[0:1, wide]
        others = misc_acc[pl.ds(8 + u, 1), :384]
        row = iota((48, 384), 0)
        ref[912:960, :] = jnp.where(row == 0, bias, jnp.where(row == 1, others, 0.0)).astype(BF)


def middle(me, o1, o2, pooled, up, vectors, weights):
    clips = len(pooled)
    queries = pooled[0].shape[0]
    grad = (clips, HEADS, queries, LANES)
    grad_t = (clips, HEADS, HEAD_DIM, queries)
    return call(
        functools.partial(middle_body, clips),
        (1,),
        [
            (pl.BlockSpec(memory_space=pltpu.SMEM), me),
            *(whole(value) for value in (*o1, *o2, *pooled, up, *vectors, *weights)),
        ],
        [
            out_whole((clips, queries, D_OUT), F32),
            out_whole((clips, queries, D_OUT), BF),
            out_whole(grad, BF),
            out_whole(grad, BF),
            out_whole(grad_t, BF),
            out_whole(grad_t, BF),
            *([out_whole((960, 384), BF)] * 4),
            out_whole((D_OUT, 2 * LANES), F32),
        ],
        [
            pltpu.VMEM((D_OUT, FF), F32),
            pltpu.VMEM((D_OUT, FF), F32),
            pltpu.VMEM((D_OUT, D_OUT), F32),
            pltpu.VMEM((D_OUT, 2 * LANES), F32),
            pltpu.VMEM((16, FF), F32),
        ],
        name="middle",
        stays=[True] * 11,
        cost=16,
    )


def backward_body(
    na_ref,
    nb_ref,
    wg_ref,
    p_ref,
    kt_ref,
    vt_ref,
    do_ref,
    dot_ref,
    qt_ref,
    dq_ref,
    dw_ref,
    ga_ref,
    gb_ref,
    n_ref,
    both_ref,
):
    rows = na_ref.shape[1]
    h = pl.program_id(0)
    p = p_ref[0]
    ds = p * mm(do_ref[0], vt_ref[0], 1, 0).astype(BF)
    dq_ref[0] = mm(kt_ref[0, :HEAD_DIM], ds, 1, 1)
    both_ref[h, :HEAD_DIM] = mm(qt_ref[0], ds, 1, 0).astype(BF)
    both_ref[h, HEAD_DIM:] = mm(dot_ref[0], p, 1, 0).astype(BF)

    @pl.when(h == HEADS - 1)
    def _():
        n_ref[:, :rows] = na_ref[...]
        n_ref[:, rows:] = nb_ref[...]
        both = both_ref[...].reshape(2 * D_OUT, 2 * rows)
        dw_ref[...] = mm(both, n_ref[...], 1, 1)
        g = mm(wg_ref[...], both, 1, 0).astype(BF)
        ga_ref[...] = g[:, :rows]
        gb_ref[...] = g[:, rows:]


def backward(clip, na, nb, wg, p, kt, vt, do, dot, qt, after=()):
    rows = na.shape[1]
    queries = qt.shape[2]
    return call(
        backward_body,
        (HEADS,),
        [
            whole(na),
            whole(nb),
            whole(wg),
            part(p),
            part(kt),
            part(vt),
            at_head(do, clip),
            at_head(dot, clip),
            part(qt),
        ],
        [
            out_part((HEADS, HEAD_DIM, queries), F32),
            out_whole((2 * D_OUT, EXT), F32),
            out_whole((D_IN, rows), BF),
            out_whole((D_IN, rows), BF),
        ],
        [pltpu.VMEM((EXT, 2 * rows), BF), pltpu.VMEM((HEADS, 2 * HEAD_DIM, 2 * rows), BF)],
        name="attend_back",
        after=after,
        cost=17,
    )


def gather_body(clips, me_ref, *refs):
    dq_refs, dw_refs, pooled_refs = (
        refs[: 2 * clips],
        refs[2 * clips : 4 * clips],
        refs[4 * clips : 5 * clips],
    )
    wt_ref, wpt_ref, gain_ref, shift_ref = refs[5 * clips : 5 * clips + 4]
    shard_refs, (dw_acc, line_ref, shard_ref) = refs[5 * clips + 4 : 5 * clips + 8], refs[5 * clips + 8 :]
    total = dw_refs[0][...]
    for ref in dw_refs[1:]:
        total = total + ref[...]
    for h in range(HEADS):
        at = 2 * HEAD_DIM * h
        dw_acc[HEADS + h] = total[at : at + HEAD_DIM]
        dw_acc[2 * HEADS + h] = total[at + HEAD_DIM : at + 2 * HEAD_DIM]
    dw = None
    for c in range(clips):
        dq = (dq_refs[2 * c][...] + dq_refs[2 * c + 1][...]) * SCALE
        dq = dq.reshape(D_OUT, dq.shape[2]).astype(BF)
        term = mm(dq, pooled_refs[c][...], 1, 0)
        dw = term if dw is None else dw + term
    for h in range(HEADS):
        dw_acc[h] = dw[HEAD_DIM * h : HEAD_DIM * (h + 1), :EXT]
    gain_sum = jnp.zeros((1, D_IN), F32)
    shift_sum = jnp.zeros((1, D_IN), F32)
    wp = wt_ref[3 * HEADS :].reshape(D_OUT, 2 * LANES)[:, :D_IN]
    terms = [(wt_ref[b][:HEAD_DIM, :D_IN], dw_acc[b]) for b in range(3 * HEADS)]
    for w, dw in [*terms, (wp, wpt_ref[...])]:
        w = w.astype(F32)
        gain_sum = gain_sum + jnp.sum(w * dw[:, :D_IN], axis=0, keepdims=True)
        shift_sum = shift_sum + jnp.sum(w * dw[:, D_IN : D_IN + 1], axis=0, keepdims=True)
    gain_sum = (gain_sum - line(shift_ref) * shift_sum) / line(gain_ref)
    for at, first in ((0, 0), (1, 2 * HEADS)):
        for h in range(HEADS):
            sums = dw_acc[first + h][:, LANES:]
            sums = jnp.concatenate(
                [sums, jnp.zeros((HEAD_DIM, 2 * LANES - EXT), F32)], axis=1
            )
            sums = jnp.concatenate([sums, jnp.zeros((LANES - HEAD_DIM, LANES), F32)], axis=0).T
            line_ref[at : at + 1, HEAD_DIM * h : HEAD_DIM * (h + 1)] = sums[
                D_IN - LANES : D_IN - LANES + 1, :HEAD_DIM
            ]
    line_ref[2:3, :D_IN] = gain_sum
    line_ref[3:4, :D_IN] = shift_sum
    for u in range(4):
        at = 0
        for source, size in ((0, 96), (1, 96), (2, 48), (3, 48)):
            shard_ref[u : u + 1, at : at + size] = line_ref[
                source : source + 1, size * u : size * (u + 1)
            ]
            at += size
        shard_ref[u : u + 1, at:] = jnp.zeros((1, D_OUT - at), F32)
    for r in range(4):
        u = me_ref[0] ^ r
        ref = shard_refs[r]
        rows = jnp.concatenate([dw_acc[3 * u + i][:, :D_IN] for i in range(3)], axis=0)
        ref[:144, :] = jnp.concatenate([rows[:144], rows[144:]], axis=1).astype(BF)
        ref[144:, :] = jnp.where(
            iota((16, D_OUT), 0) == 0, shard_ref[pl.ds(u, 1), :], 0.0
        ).astype(BF)


def gather(me, dq, dw, pooled, wt, wpt, gain, shift, after=()):
    clips = len(pooled)
    return call(
        functools.partial(gather_body, clips),
        (1,),
        [
            (pl.BlockSpec(memory_space=pltpu.SMEM), me),
            *(whole(v) for v in (*dq, *dw, *pooled, wt, wpt, gain, shift)),
        ],
        [out_whole((160, D_OUT), BF)] * 4,
        [
            pltpu.VMEM((3 * HEADS, HEAD_DIM, EXT), F32),
            pltpu.VMEM((8, D_OUT), F32),
            pltpu.VMEM((8, D_OUT), F32),
        ],
        name="gather",
        after=after,
        cost=6,
    )


def final_body(terms, tok_ref, hg_ref, wp_ref, qkv_ref, gain_ref, dq1_ref, dq2_ref, *refs):
    part_refs, out_ref = refs[:terms], refs[-1]
    slots, _, units = tok_ref.shape[1:]
    gain = column(gain_ref)
    dq = ((dq1_ref[...] + dq2_ref[...]) * SCALE).reshape(D_OUT, 4 * units).astype(BF)
    spread = mm(wp_ref[...], hg_ref[0], 1, 1) + mm(qkv_ref[:, :D_OUT], dq, 1, 0)
    spread = spread * 0.25
    places = [slice(units * s, units * (s + 1)) for s in range(slots)]
    spread = [spread[:, places[2 * (s >> 3) + ((s >> 1) & 1)]] for s in range(slots)]
    grad = total_of(part_refs) + jnp.concatenate(spread, axis=1)
    x = jnp.concatenate([tok_ref[0, s] for s in range(slots)], axis=1).astype(F32)
    center = x - jnp.mean(x, axis=0, keepdims=True)
    inv_std = lax.rsqrt(jnp.mean(center * center, axis=0, keepdims=True) + 1e-06)
    n = center * inv_std
    e = grad * gain
    back = e - jnp.mean(e, axis=0, keepdims=True) - n * jnp.mean(e * n, axis=0, keepdims=True)
    back = back * inv_std
    for s in range(slots):
        out_ref[0, s] = back[:, places[s]]


def final(clip, tokens, hg, dq, wp, qkv, gain, parts, filled, after=()):
    terms = len(parts)
    return call(
        functools.partial(final_body, terms),
        (1,),
        [
            at_clip(tokens, clip),
            at_clip(hg, clip),
            *(whole(v) for v in (wp, qkv, gain, *dq, *parts)),
            *([] if filled is None else [(pl.BlockSpec(memory_space=pl.ANY), filled)]),
        ],
        [(at_clip(tokens, clip)[0], tokens.shape, F32)],
        name="final",
        stays=[True],
        cost=6,
        after=after,
        aliases=None if filled is None else {7 + terms: 0},
    )[0]


def unpack_first_body(
    place_ref,
    value_ref,
    other_ref,
    proj_ref,
    bproj_ref,
    wo_ref,
    bout_ref,
    gain_ref,
    shift_ref,
    we_ref,
    be_ref,
    ws_ref,
    bs_ref,
    rows_ref,
):
    half = value_ref.shape[0]
    at = pl.multiple_of(place_ref[0] * half, 8)
    rows_ref[pl.ds(at, half), :] = value_ref[...].astype(F32)
    rows_ref[pl.ds(pl.multiple_of(half - at, 8), half), :] = other_ref[...].astype(F32)
    we_ref[...] = rows_ref[:384]
    ws_ref[...] = rows_ref[384:768].T
    wo_ref[...] = rows_ref[768:864]
    proj = jnp.concatenate([rows_ref[864:912, :D_IN], rows_ref[864:912, D_IN:]], axis=0)
    proj_ref[...] = proj.T
    lines = rows_ref[912:920]
    be_ref[...] = lines[0:1].reshape(384)
    for ref, k in ((gain_ref, 0), (shift_ref, 1), (bs_ref, 2), (bout_ref, 3), (bproj_ref, 3)):
        ref[...] = lines[1:2, 96 * k : 96 * (k + 1)].reshape(96)


def unpack_first(place, value, other, after=()):
    shapes = [(192, 96), (96,), (96, 384), (96,), (96,), (96,), (384, 384), (384,), (384, 384), (96,)]
    return call(
        unpack_first_body,
        (1,),
        [(pl.BlockSpec(memory_space=pltpu.SMEM), place), whole(value), whole(other)],
        [out_whole(shape, F32) for shape in shapes],
        [pltpu.VMEM((2 * value.shape[0], D_OUT), F32)],
        name="unpack_first",
        stays=[True] * len(shapes),
        after=after,
        cost=2,
    )


def unpack_second_body(a_ref, b_ref, qkv_ref, bq_ref, bv_ref, gain_ref, shift_ref):
    total = a_ref[...].astype(F32) + b_ref[...].astype(F32)
    qkv_ref[...] = jnp.concatenate([total[:144, :D_IN], total[:144, D_IN:]], axis=0).T
    at = 0
    for ref in (bq_ref, bv_ref, gain_ref, shift_ref):
        size = ref.shape[0]
        ref[...] = total[144:145, at : at + size].reshape(size)
        at += size


def unpack_second(a, b):
    shapes = [(192, 288), (96,), (96,), (48,), (48,)]
    return call(
        unpack_second_body,
        (1,),
        [whole(a), whole(b)],
        [out_whole(shape, F32) for shape in shapes],
        name="unpack_second",
        stays=[True] * len(shapes),
        cost=1,
    )


def swap_unit(value, bit):
    return lax.ppermute(value, "unit", [(i, i ^ bit) for i in range(4)])


def swap_clip(value, bit):
    size = lax.axis_size("clip")
    return lax.ppermute(value, "clip", [(i, i ^ bit) for i in range(size)])


def add(*values):
    return functools.reduce(lambda a, b: a + b, [v.astype(F32) for v in values]).astype(BF)


def member():
    at = lax.axis_index("clip").astype(jnp.int32)
    return jnp.stack([at & 1, (at >> 1) & 1])


def total_of(refs):
    return functools.reduce(lambda a, b: a + b, [ref[...].astype(F32) for ref in refs])


def between(sums, place, cut=None, grads=None, join=None):
    rows, width = sums[0].shape
    count, more = len(sums), grads or []
    pieces = 1 if cut is None else 2
    tall = 2 * rows if join is not None else rows // pieces

    def body(place_ref, *refs):
        terms, refs = refs[:count], refs[count:]
        others, refs = refs[: len(more)], refs[len(more) :]
        outs, scratch = refs[:-1], refs[-1]
        if more:
            outs[-1][...] = total_of(others).astype(BF)
        if join is not None:
            for d in range(2):
                at = pl.multiple_of((place_ref[join] ^ d) * rows, 8)
                scratch[pl.ds(at, rows), :] = terms[d][...].astype(F32)
            outs[0][...] = scratch[...].astype(BF)
        elif cut is None:
            outs[0][...] = total_of(terms).astype(BF)
        else:
            scratch[...] = total_of(terms)
            for d in range(2):
                at = pl.multiple_of((place_ref[cut] ^ d) * tall, 8)
                outs[d][...] = scratch[pl.ds(at, tall), :].astype(BF)

    return list(
        call(
            body,
            (1,),
            [(pl.BlockSpec(memory_space=pltpu.SMEM), place), *(whole(v) for v in (*sums, *more))],
            [
                *([out_whole((tall, width), BF)] * pieces),
                *([out_whole(more[0].shape, BF)] if more else []),
            ],
            [pltpu.VMEM((max(rows, tall), width), F32)],
            name="between",
            cost=2,
        )
    )


def in_hbm(*values):
    return [pltpu.with_memory_space_constraint(v, pltpu.HBM) for v in values]


def together(*values):
    return lax.optimization_barrier(values)


def shards(
    tokens,
    first_gain,
    first_shift,
    proj_weight,
    proj_bias,
    qkv_weight,
    query_bias,
    value_bias,
    output_weight,
    output_bias,
    second_gain,
    second_shift,
    expand_weight,
    expand_bias,
    shrink_weight,
    shrink_bias,
    frame_counts,
    unit_frames,
    cotangent,
):
    clips, units = tokens.shape[:2]
    me = lax.axis_index("unit").astype(jnp.int32).reshape(1)
    vectors = [proj_bias, output_bias, second_gain, second_shift, shrink_bias, expand_bias]
    flat = tokens.transpose(0, 2, 3, 1)
    upstream = cotangent.transpose(0, 2, 1, 3).reshape(clips, 4 * units, D_OUT)
    normed, pooled = normed_tokens(flat, unit_frames, frame_counts, first_gain, first_shift)
    near, across = [(n, swap_unit(n, 1)) for n in normed], []
    wt, wg, query = queries_of(qkv_weight, proj_weight, query_bias, value_bias, pooled)
    own, rest, far = [], [], []
    for c in range(clips):
        across.append(swap_unit(together(near[c][0], near[0][1])[0] if c else near[c][0], 2))
        weights = [wt, query[c][0]] if c else in_hbm(wt, query[c][0])
        keys = near[c] if c else in_hbm(*near[c])
        own.append(forward(*keys, *weights, after=in_hbm(*(v[3] for v in own[-1:]))))
    for c in range(clips):
        held, _ = together(across[c], own[c][3])
        far.append((held, swap_unit(held, 1)))
        rest.append(forward(*far[c], wt, query[c][0], after=in_hbm(*(v[3] for v in (own + rest)[-1:]))))
    out, hg, do1, do2, do1t, do2t, keep, send0, across, send1, wpt = middle(
        me,
        in_hbm(*(value[3] for value in own)),
        in_hbm(*(value[3] for value in rest)),
        pooled,
        upstream,
        vectors,
        [proj_weight, output_weight, expand_weight, shrink_weight],
    )
    dq, dw = [[None, None] for _ in range(clips)], [[None, None] for _ in range(clips)]
    place = member()
    got = [swap_unit(send0, 1), swap_unit(send1, 1)]
    out = out.reshape(clips, 4, units, D_OUT).transpose(0, 2, 1, 3)
    got, out = together(got, out)
    (value,) = between([*in_hbm(across), got[1]], place)
    terms = [keep, got[0]]
    calls = [(c, 1) for c in range(clips)] + [(c, 0) for c in range(clips)]
    parts = [[None] * 3 for _ in range(clips)]
    lent, owed = [], []
    moves = ["unit", 1, 2, 4]
    bits = []
    bit = 8
    while bit < lax.axis_size("clip"):
        bits.append(bit)
        bit *= 2
    held = [value]
    for at, (c, side) in enumerate(calls):
        keys, kept, grads = (far, rest, (do2, do2t)) if side else (near, own, (do1, do1t))
        move = moves[at]
        sent = [swap_unit(value, 2) if move == "unit" else swap_clip(value, move)]
        travel = [swap_unit(parts[b][0], 2) for b in lent]
        travel += [swap_unit(gb, 1) for _, gb in owed]
        result = backward(c, *keys[c], wg, *kept[c][:3], *grads, query[c][1], after=held)
        *result, travel, sent = together(*result, travel, sent)
        dq[c][side], dw[c][side], ga, gb = result
        for b in lent:
            parts[b][0] = travel.pop(0)
        lent, loose = [], None
        for ((b, other), _), arrived in zip(owed, travel, strict=True):
            if other:
                loose = [parts[b][0], arrived]
                lent.append(b)
            else:
                parts[b][2] = arrived
        cut = {"unit": 0, 1: 1}.get(move)
        result = between([*terms, *sent], place, cut, loose)
        if loose:
            parts[lent[0]][0] = result.pop()
        if cut is None:
            (value,), terms = result, result
        else:
            terms, value = result[:1], result[1]
        if move == 2:
            for bit in bits:
                value = add(value, swap_clip(value, bit))
            terms = [value]
        owed = [((c, side), gb)]
        parts[c][0 if side else 1] = ga
        held = [dq[c][side], value, *terms, *(parts[b][0] for b in lent)]
    half = swap_clip(value, 2)
    travel = [swap_unit(gb, 1) for _, gb in owed]
    result = gather(
        me,
        [v for pair in dq for v in pair],
        [v for pair in dw for v in pair],
        pooled,
        wt,
        wpt,
        first_gain,
        first_shift,
        after=held,
    )
    (keep, send0, across, send1), travel = together(result, travel)
    for ((b, _), _), arrived in zip(owed, travel, strict=True):
        parts[b][2] = arrived
    got = [swap_unit(send0, 1), swap_unit(send1, 1)]
    second = add(across, got[1])
    input_grad, firsts = None, None
    bit = 0
    for c in range(max(clips, 3)):
        sent = swap_clip(second, bit) if bit else swap_unit(second, 2)
        if c < clips:
            input_grad = final(
                c, flat, hg, dq[c], proj_weight, qkv_weight, first_gain, parts[c], input_grad, after=[second]
            )
            if c == 0:
                sent, input_grad, half = together(sent, input_grad, half)
                (value,) = between([value, half], place, join=1)
                other = swap_clip(value, 1)
            else:
                sent, input_grad = together(sent, input_grad)
        if c < 3:
            second = add(second, sent) if bit else add(keep, got[0], sent)
            bit = 2 * bit if bit else 1
    last = swap_clip(second, 4)
    firsts = unpack_first(place, value, other, after=[second])
    last, firsts = together(last, firsts)
    for more in bits:
        second, last = add(second, last), None
        last = swap_clip(second, more)
    wp_grad, bp_grad, wo_grad, bo_grad, g2_grad, s2_grad, we_grad, be_grad, ws_grad, bs_grad = firsts
    qkv_grad, bq_grad, bv_grad, g1_grad, s1_grad = unpack_second(second, last)
    return (
        out,
        input_grad.transpose(0, 3, 1, 2),
        g1_grad,
        s1_grad,
        wp_grad,
        bp_grad,
        qkv_grad,
        bq_grad,
        bv_grad,
        wo_grad.T,
        bo_grad,
        g2_grad,
        s2_grad,
        we_grad,
        be_grad,
        ws_grad,
        bs_grad,
    )


def solution(mesh):
    every = P()
    split = P("clip", "unit", None, None)
    return jax.shard_map(
        shards,
        mesh=mesh,
        in_specs=(split,) + (every,) * 15 + (P("clip"), P("clip", "unit"), split),
        out_specs=(
            split,
            split,
            P("unit"),
            P("unit"),
            P(None, "unit"),
            P("unit"),
            P(None, "unit"),
            P("unit"),
            P("unit"),
            P(None, "unit"),
            P("unit"),
            P("unit"),
            P("unit"),
            P(None, "unit"),
            P("unit"),
            P("unit", None),
            P("unit"),
        ),
        check_vma=False,
    )
```
